32 devices in a mesh: dp: 8 (over z, y), blk: 4 (over x, core).
Axes of the slice: x: 2, y: 2, z: 4, core: 2. Of those that a mesh axis runs over, the one named last changes fastest.
Arguments:
- inputs: bfloat16 [4096, 512], P('dp'), may hold values from -6 to 6
- out_grads: bfloat16 [4096, 512], P('dp'), may hold values from -6 to 6
- pre_act: bfloat16 [4096, 36864], P('dp', 'blk'), may hold values from -6 to 6
- w_in: bfloat16 [36864, 512], P('blk'), may hold values from -0.03125 to 0.03125
- w_out: bfloat16 [36864, 512], P('blk'), may hold values from -0.25 to 0.25
Outputs:
- grad_inputs: bfloat16 [4096, 512], P(('dp', 'blk'))
- grad_w_in: float32 [36864, 512], P(('blk', 'dp'))
- grad_w_out: float32 [36864, 512], P(('blk', 'dp'))
The draws below stay inside these ranges and needn't reach their ends.
All inputs are finite; a program needn't handle non-finite values.
Results may differ from the reference program's by a relative error of at most 0.0049.
Values sent between devices are 32-bit elements; how exact they have to be, the bound alone decides.
No kernel may reach another device: no remote copies, remote signals or barrier semaphores. Data moves between devices by JAX's collectives and lax.ppermute only.
A program may use at most 128 MiB of HBM per device.

```python
import jax
import jax.numpy as jnp
from jax import lax

D = 512
FF = 36864
TOKENS = 4096
N_BLK = 4


def levels(stream_key, extent, split, smallest, top_value):
    factor_of, own = 1.0, jax.random.fold_in(stream_key, 6)
    for position, shards_of in split:
        heights = jnp.exp(jax.random.uniform(jax.random.fold_in(own, position), (shards_of,), jnp.float32, smallest / len(split), top_value / len(split)))
        factor_of = factor_of * jnp.repeat(heights, extent[position] // shards_of).reshape([-1 if axis == position else 1 for axis in range(len(extent))])
    return factor_of


def normal_values(key, extent, spread, most, pieces=(), kind=jnp.bfloat16):
    result = jax.random.normal(key, extent, jnp.float32) * spread
    if len(pieces) > 0:
        result = levels(key, extent, pieces, -0.22, 0.18) * result
    return jnp.clip(result, min=-most, max=most).astype(kind)


def setup_inputs(seed: int = 0) -> dict:
    streams_of = jax.random.split(jax.random.key(seed), 6)
    return {
        "inputs": normal_values(streams_of[0], (TOKENS, D), 1.0, 6.0, ((0, 8),)),
        "out_grads": normal_values(streams_of[1], (TOKENS, D), 1.0, 6.0, ((0, 8),)),
        "pre_act": normal_values(streams_of[2], (TOKENS, FF), 1.0, 6.0, ((0, 8), (1, 4))),
        "w_in": normal_values(streams_of[3], (FF, D), FF ** -0.5, 0.03125, ((0, 4),)),
        "w_out": normal_values(streams_of[4], (FF, D), D ** -0.5, 0.25, ((0, 4),)),
    }


def reference(inputs, out_grads, pre_act, w_in, w_out):
    width = FF // N_BLK
    high = lax.Precision.HIGHEST
    inputs_wide = inputs.astype(jnp.float32)
    grads_wide = out_grads.astype(jnp.float32)
    factor = lax.rsqrt(jnp.asarray(TOKENS, jnp.float32))

    def one_block(index):
        start = index * width
        pre = lax.dynamic_slice_in_dim(pre_act, start, width, 1)
        out_rows = lax.dynamic_slice_in_dim(w_out, start, width, 0).astype(jnp.float32)
        in_rows = lax.dynamic_slice_in_dim(w_in, start, width, 0).astype(jnp.float32)
        back = jnp.dot(grads_wide, out_rows.T, precision=high)
        grad_hidden = jnp.where(pre > 0, back, jnp.zeros_like(back)).astype(jnp.bfloat16)
        hidden_wide = grad_hidden.astype(jnp.float32)
        act = jnp.maximum(pre, jnp.zeros_like(pre)).astype(jnp.float32)
        grad_out = jnp.dot(act.T, grads_wide, precision=high) * factor
        grad_in = jnp.dot(hidden_wide.T, inputs_wide, precision=high) * factor
        partial_sum = jnp.dot(hidden_wide, in_rows, precision=high)
        return (grad_in, grad_out, partial_sum)
    grad_in, grad_out, partials = lax.map(one_block, jnp.arange(N_BLK, dtype=jnp.int32))
    grad_inputs = lax.optimization_barrier(jnp.sum(partials, axis=0)).astype(jnp.bfloat16)
    return (grad_inputs, grad_in.reshape(FF, D), grad_out.reshape(FF, D))
```

```python
import functools

import jax
import jax.numpy as jnp
from jax import lax
from jax.experimental import pallas as pl
from jax.experimental.pallas import tpu as pltpu
from jax.sharding import PartitionSpec as P

PIECES = 3
LAG = 2
VMEM_LIMIT = 48 * 1024 * 1024


def contract_rows(left, right):
    return lax.dot_general(
        left, right, (((0,), (0,)), ((), ())), preferred_element_type=jnp.float32
    )


def hidden_grads(out_grads, pre_act, w_out):
    back = lax.dot_general(
        out_grads, w_out, (((1,), (1,)), ((), ())), preferred_element_type=jnp.float32
    )
    return jnp.where(pre_act > 0, back, jnp.zeros_like(back)).astype(jnp.bfloat16)


def input_grads(grad_hidden, w_in):
    return lax.psum_scatter(
        jnp.dot(grad_hidden, w_in, preferred_element_type=jnp.float32),
        "blk",
        scatter_dimension=0,
        tiled=True,
    ).astype(jnp.bfloat16)


def plain_body(inputs, out_grads, pre_act, w_in, w_out):
    token_total = inputs.shape[0] * lax.axis_size("dp")
    factor = lax.rsqrt(jnp.asarray(token_total, jnp.float32))
    act = jnp.maximum(pre_act, jnp.zeros_like(pre_act))
    grad_hidden = hidden_grads(out_grads, pre_act, w_out)
    grad_out = contract_rows(act, out_grads) * factor
    grad_in = contract_rows(grad_hidden, inputs) * factor
    return (
        input_grads(grad_hidden, w_in),
        lax.psum_scatter(grad_in, "dp", scatter_dimension=0, tiled=True),
        lax.psum_scatter(grad_out, "dp", scatter_dimension=0, tiled=True),
    )


def join_kernel(core_ref, grads_ref, inputs_ref, mine_ref, other_ref, g_ref, x_ref):
    rows = grads_ref.shape[0]
    half = rows // 2
    core = core_ref[0]
    g_ref[:rows, :] = grads_ref[...]
    x_ref[:rows, :] = inputs_ref[...]
    mine = pl.ds(pl.multiple_of(rows + core * half, half), half)
    other = pl.ds(pl.multiple_of(rows + (1 - core) * half, half), half)
    g_ref[mine, :] = mine_ref[:half, :].astype(jnp.bfloat16)
    x_ref[mine, :] = mine_ref[half:, :].astype(jnp.bfloat16)
    g_ref[other, :] = other_ref[:half, :].astype(jnp.bfloat16)
    x_ref[other, :] = other_ref[half:, :].astype(jnp.bfloat16)


def join(core, out_grads, inputs, mine, other):
    rows, width = out_grads.shape
    shape = jax.ShapeDtypeStruct((2 * rows, width), jnp.bfloat16)
    vmem = pl.BlockSpec(memory_space=pltpu.VMEM)
    return pl.pallas_call(
        join_kernel,
        out_shape=(shape, shape),
        in_specs=[pl.BlockSpec(memory_space=pltpu.SMEM)] + [vmem] * 4,
        out_specs=(vmem, vmem),
        compiler_params=pltpu.CompilerParams(vmem_limit_bytes=VMEM_LIMIT),
        name="join_tokens",
    )(core.reshape(1), out_grads, inputs, mine, other)


def piece_math(scale, own, partner, g, x, w, sums):
    partner = partner.astype(jnp.bfloat16)
    pre = jnp.concatenate([own, partner], axis=0)
    back = lax.dot_general(g, w, (((1,), (1,)), ((), ())), preferred_element_type=jnp.float32)
    hidden = jnp.where(pre > 0, back, 0.0).astype(jnp.bfloat16)
    act = jnp.maximum(pre, jnp.zeros_like(pre))
    grad_in = contract_rows(hidden, x) * scale
    grad_out = contract_rows(act, g) * scale
    for ref in sums:
        grad_in = grad_in + ref[0]
        grad_out = grad_out + ref[1]
    return grad_in, grad_out


def piece_kernel(scale, n_sums, idx_ref, own_ref, partner_ref, g_ref, x_ref, w_ref, *refs):
    sums, out_ref = refs[:n_sums], refs[n_sums]
    out_ref[0], out_ref[1] = piece_math(
        scale, own_ref[...], partner_ref[...], g_ref[...], x_ref[...], w_ref[...], sums
    )


def final_kernel(scale, n_sums, idx_ref, own_ref, inner_ref, outer_ref, g_ref, x_ref, w_ref, *refs):
    sums, (in_ref, out_ref) = refs[:n_sums], refs[-2:]
    partner = jnp.where(idx_ref[1] > 0, inner_ref[...], outer_ref[...])
    in_ref[...], out_ref[...] = piece_math(
        scale, own_ref[...], partner, g_ref[...], x_ref[...], w_ref[...], sums
    )


def piece_specs(rows, size, width, n_partners, n_sums):
    whole = lambda shape: pl.BlockSpec(shape, lambda i, idx: (0,) * len(shape))
    return (
        [pl.BlockSpec((rows, size), lambda i, idx: (0, idx[0]))]
        + [whole((rows, size))] * n_partners
        + [whole((2 * rows, width))] * 2
        + [pl.BlockSpec((size, width), lambda i, idx: (idx[0], 0))]
        + [whole((2, size, width))] * n_sums
    )


def piece_cost(rows, size, width, n_sums):
    return pl.CostEstimate(
        flops=3 * 2 * 2 * rows * size * width,
        bytes_accessed=rows * size * 6 + rows * width * 8 + size * width * (10 + 8 * n_sums),
        transcendentals=0,
    )


def piece(scale, index, pre_act, partner, g, x, w_out, sums):
    rows, size = partner.shape
    width = g.shape[1]
    return pl.pallas_call(
        functools.partial(piece_kernel, scale, len(sums)),
        grid_spec=pltpu.PrefetchScalarGridSpec(
            num_scalar_prefetch=1,
            grid=(1,),
            in_specs=piece_specs(rows, size, width, 1, len(sums)),
            out_specs=pl.BlockSpec((2, size, width), lambda i, idx: (0, 0, 0)),
        ),
        out_shape=jax.ShapeDtypeStruct((2, size, width), jnp.float32),
        compiler_params=pltpu.CompilerParams(vmem_limit_bytes=VMEM_LIMIT),
        cost_estimate=piece_cost(rows, size, width, len(sums)),
        name="piece",
    )(index.reshape(1), pre_act, partner, g, x, w_out, *sums)


def final(scale, place, count, index, is_inner, pre_act, partners, g, x, w_out, sums, held):
    rows, size = partners[0].shape
    width = g.shape[1]
    shape = jax.ShapeDtypeStruct((count * size, width), jnp.float32)
    first = 6 + 1 + len(sums)
    return pl.pallas_call(
        functools.partial(final_kernel, scale, len(sums)),
        grid_spec=pltpu.PrefetchScalarGridSpec(
            num_scalar_prefetch=1,
            grid=(1,),
            in_specs=piece_specs(rows, size, width, 2, len(sums))
            + [pl.BlockSpec(memory_space=pl.ANY)] * len(held),
            out_specs=[pl.BlockSpec((size, width), lambda i, idx: (place, 0))] * 2,
        ),
        out_shape=(shape, shape),
        input_output_aliases={first + i: i for i in range(len(held))},
        compiler_params=pltpu.CompilerParams(vmem_limit_bytes=VMEM_LIMIT),
        cost_estimate=piece_cost(rows, size, width, len(sums)),
        name="final_piece",
    )(jnp.stack([index, is_inner]), pre_act, *partners, g, x, w_out, *sums, *held)


def line_body(inputs, out_grads, pre_act, w_in, w_out):
    count = PIECES
    rows, hidden = pre_act.shape
    size = hidden // (8 * count)
    scale = 1.0 / (rows * lax.axis_size("dp")) ** 0.5
    me = lax.axis_index("dp")
    plane, half = me // 2, me % 2
    core = lax.axis_index("blk") % 2
    side = plane // 2
    is_inner = jnp.where((plane == 1) | (plane == 2), 1, 0).astype(jnp.int32)

    def links(pairs):
        return [(2 * a + h, 2 * b + h) for a, b in pairs for h in range(2)]

    def swaps(planes):
        return [(2 * a + h, 2 * a + 1 - h) for a in planes for h in range(2)]

    outer_to_inner = links([(0, 1), (3, 2)])
    inner_to_inner = links([(1, 2), (2, 1)])
    inner_to_outer = links([(1, 0), (2, 3)])

    def block(q, which):
        place = q // count
        chunk = jnp.where(side == 0, 3 - place, place)
        return (chunk * 2 + which) * count + q % count

    quarter = rows // 2
    part = jnp.concatenate(
        [
            lax.dynamic_slice_in_dim(out_grads, core * quarter, quarter, 0),
            lax.dynamic_slice_in_dim(inputs, core * quarter, quarter, 0),
        ],
        axis=0,
    ).astype(jnp.float32)
    mine = lax.ppermute(part, "dp", swaps(range(4)))
    blks = lax.axis_size("blk")
    other = lax.ppermute(mine, "blk", [(i, i ^ 1) for i in range(blks)])
    g, x = join(core, out_grads, inputs, mine, other)

    started = []

    def exchange(q, planes):
        if len(started) >= 2:
            q, started[-2][0] = lax.optimization_barrier((q, started[-2][0]))
        start = block(q, 1 - half) * size
        send = lax.dynamic_slice_in_dim(pre_act, start, size, 1).astype(jnp.float32)
        box = [lax.ppermute(send, "dp", swaps(planes))]
        started.append(box)
        return box

    main_steps = 3 * count
    every, outer, inner = (0, 1, 2, 3), (0, 3), (1, 2)
    main_q = [
        jnp.clip(s - LAG * is_inner, 0, (2 * count - 1) * is_inner + (main_steps - 1) * (1 - is_inner))
        for s in range(main_steps)
    ]
    near_outer = [jnp.int32(main_steps + j) for j in range(count)]
    near_inner = [jnp.int32(2 * count + j) for j in range(count)]

    y_main, y_no, y_ni = [], [], []
    for s in range(main_steps):
        relevant = outer if s < LAG or s >= 2 * count + LAG else every
        y_main.append(exchange(main_q[s], relevant))
        j = s - (LAG + 2)
        if 0 <= j < count:
            y_no.append(exchange(near_outer[j], every))
        if s >= main_steps - count:
            y_ni.append(exchange(near_inner[s - (main_steps - count)], inner))

    def run(q, partner, sums):
        return piece(scale, block(q, half), pre_act, partner, g, x, w_out, sums)

    from_outer, from_inner, to_outer = [], [], []
    for s in range(main_steps):
        out = run(main_q[s], y_main[s][0], [from_outer[s - LAG]] if s >= LAG else [])
        from_outer.append(lax.ppermute(out, "dp", outer_to_inner))
        if LAG <= s < 2 * count + LAG:
            from_inner.append(lax.ppermute(out, "dp", inner_to_inner))
        j = s - (LAG + 2)
        if 0 <= j < count:
            out = run(near_outer[j], y_no[j][0], [from_inner[j]])
            to_outer.append(lax.ppermute(out, "dp", inner_to_outer))

    held = ()
    for i in range(count):
        q = jnp.where(is_inner > 0, near_inner[i], near_outer[i])
        held = final(
            scale,
            i,
            count,
            block(q, half),
            is_inner,
            pre_act,
            (y_ni[i][0], y_no[i][0]),
            g,
            x,
            w_out,
            [from_outer[2 * count + i], from_inner[count + i], to_outer[i]],
            held,
        )

    grad_inputs = input_grads(hidden_grads(out_grads, pre_act, w_out), w_in)
    return (grad_inputs, held[0], held[1])


def solution(mesh):
    def body(inputs, out_grads, pre_act, w_in, w_out):
        fits = pre_act.shape[1] % (8 * PIECES * 128) == 0 and inputs.shape[0] % 32 == 0
        paired = mesh.shape["blk"] % 2 == 0
        run = line_body if mesh.shape["dp"] == 8 and paired and fits else plain_body
        return run(inputs, out_grads, pre_act, w_in, w_out)

    return jax.shard_map(
        body,
        mesh=mesh,
        in_specs=(P("dp", None), P("dp", None), P("dp", "blk"), P("blk", None), P("blk", None)),
        out_specs=(P(("dp", "blk"), None), P(("blk", "dp"), None), P(("blk", "dp"), None)),
        check_vma=False,
    )
```

```python
import functools

import jax
import jax.numpy as jnp
from jax import lax
from jax.experimental import pallas as pl
from jax.experimental.pallas import tpu as pltpu
from jax.sharding import PartitionSpec as P

PIECES = 3
FLOPS = 100_000_000_000
VMEM_LIMIT = 56 * 1024 * 1024


def contract_rows(left, right):
    return lax.dot_general(
        left, right, (((0,), (0,)), ((), ())), preferred_element_type=jnp.float32
    )


def hidden_grads(out_grads, pre_act, w_out):
    back = lax.dot_general(
        out_grads, w_out, (((1,), (1,)), ((), ())), preferred_element_type=jnp.float32
    )
    return jnp.where(pre_act > 0, back, jnp.zeros_like(back)).astype(jnp.bfloat16)


def input_grads(grad_hidden, w_in):
    return lax.psum_scatter(
        jnp.dot(grad_hidden, w_in, preferred_element_type=jnp.float32),
        "blk",
        scatter_dimension=0,
        tiled=True,
    ).astype(jnp.bfloat16)


def plain_body(inputs, out_grads, pre_act, w_in, w_out):
    token_total = inputs.shape[0] * lax.axis_size("dp")
    factor = lax.rsqrt(jnp.asarray(token_total, jnp.float32))
    act = jnp.maximum(pre_act, jnp.zeros_like(pre_act))
    grad_hidden = hidden_grads(out_grads, pre_act, w_out)
    grad_out = contract_rows(act, out_grads) * factor
    grad_in = contract_rows(grad_hidden, inputs) * factor
    return (
        input_grads(grad_hidden, w_in),
        lax.psum_scatter(grad_in, "dp", scatter_dimension=0, tiled=True),
        lax.psum_scatter(grad_out, "dp", scatter_dimension=0, tiled=True),
    )


def params():
    return pltpu.CompilerParams(vmem_limit_bytes=VMEM_LIMIT)


def anywhere(arrays):
    return [pl.BlockSpec(memory_space=pl.ANY)] * len(arrays)


def start_kernel(idx_ref, grads_ref, inputs_ref, *refs):
    columns, (quarter_ref, *outs) = refs[:4], refs[4:]
    quarter, rows = grads_ref.shape[0], columns[0].shape[0]
    quarter_ref[:quarter, :] = grads_ref[...].astype(jnp.float32)
    quarter_ref[quarter:, :] = inputs_ref[...].astype(jnp.float32)
    for k, ref in enumerate(columns):
        place = k % 2
        outs[k // 2][place * rows : (place + 1) * rows, :] = ref[...].astype(jnp.float32)


def start_sends(blk, out_grads, inputs, columns, pre_act, size):
    rows, width = out_grads.shape
    quarter = rows // 4
    tokens = pl.BlockSpec((quarter, width), lambda i, idx: (idx[0], 0))
    shapes = [(2 * quarter, width), (2 * rows, size), (2 * rows, size)]
    return pl.pallas_call(
        start_kernel,
        grid_spec=pltpu.PrefetchScalarGridSpec(
            num_scalar_prefetch=1,
            grid=(1,),
            in_specs=[tokens, tokens]
            + [pl.BlockSpec((rows, size), lambda i, idx, k=k: (0, idx[k])) for k in (1, 2, 3, 4)],
            out_specs=[pl.BlockSpec(shape, lambda i, idx: (0, 0)) for shape in shapes],
        ),
        out_shape=[jax.ShapeDtypeStruct(shape, jnp.float32) for shape in shapes],
        compiler_params=params(),
        cost_estimate=piece_cost(),
        name="start_sends",
    )(jnp.stack([blk, *columns]), out_grads, inputs, *([pre_act] * 4))


def join_kernel(blk_ref, grads_ref, inputs_ref, *refs):
    quarters, (g_ref, x_ref) = refs[:4], refs[-2:]
    rows = grads_ref.shape[0]
    quarter = rows // 4
    g_ref[:rows, :] = grads_ref[...]
    x_ref[:rows, :] = inputs_ref[...]
    for flip, ref in enumerate(quarters):
        where = jnp.bitwise_xor(blk_ref[0], flip)
        place = pl.ds(pl.multiple_of(rows + where * quarter, quarter), quarter)
        g_ref[place, :] = ref[:quarter, :].astype(jnp.bfloat16)
        x_ref[place, :] = ref[quarter:, :].astype(jnp.bfloat16)


def join(blk, out_grads, inputs, quarters, after):
    rows, width = out_grads.shape
    shape = jax.ShapeDtypeStruct((2 * rows, width), jnp.bfloat16)
    vmem = pl.BlockSpec(memory_space=pltpu.VMEM)
    return pl.pallas_call(
        join_kernel,
        out_shape=(shape, shape),
        in_specs=[pl.BlockSpec(memory_space=pltpu.SMEM)] + [vmem] * 6 + anywhere(after),
        out_specs=(vmem, vmem),
        compiler_params=params(),
        name="join_tokens",
    )(blk.reshape(1), out_grads, inputs, *quarters, *after)


def input_kernel(grads_ref, pre_ref, out_rows_ref, in_rows_ref, *refs):
    total_ref = refs[-1]

    @pl.when(pl.program_id(0) == 0)
    def _():
        total_ref[...] = jnp.zeros_like(total_ref)

    hidden = hidden_grads(grads_ref[...], pre_ref[...], out_rows_ref[...])
    total_ref[...] += jnp.dot(hidden, in_rows_ref[...], preferred_element_type=jnp.float32)


def input_partial(out_grads, pre_act, w_in, w_out, size, after):
    rows, hidden = pre_act.shape
    width = out_grads.shape[1]
    tokens = pl.BlockSpec((rows, width), lambda i: (0, 0))
    weights = pl.BlockSpec((size, width), lambda i: (i, 0))
    return pl.pallas_call(
        input_kernel,
        grid=(hidden // size,),
        in_specs=[tokens, pl.BlockSpec((rows, size), lambda i: (0, i)), weights, weights] + anywhere(after),
        out_specs=tokens,
        out_shape=jax.ShapeDtypeStruct((rows, width), jnp.float32),
        compiler_params=params(),
        cost_estimate=piece_cost(),
        name="input_partial",
    )(out_grads, pre_act, w_out, w_in, *after)


def piece_math(scale, own, partner, g, x, w):
    pre = jnp.concatenate([own, partner.astype(jnp.bfloat16)], axis=0)
    hidden = hidden_grads(g, pre, w)
    act = jnp.maximum(pre, jnp.zeros_like(pre))
    return contract_rows(hidden, x) * scale, contract_rows(act, g) * scale


def piece_kernel(scale, counts, idx_ref, own_ref, g_ref, x_ref, w_ref, *refs):
    groups = []
    for n in counts:
        groups.append(refs[:n])
        refs = refs[n:]
    partners, others, columns, sums, _, (out_ref, *sends) = groups + [refs]
    partner = jnp.concatenate([ref[...] for ref in partners], axis=1)
    for ref in others:
        partner = jnp.where(idx_ref[2] > 0, ref[...], partner)
    grad_in, grad_out = piece_math(scale, own_ref[...], partner, g_ref[...], x_ref[...], w_ref[...])
    for ref in sums:
        grad_in = grad_in + ref[0]
        grad_out = grad_out + ref[1]
    out_ref[0], out_ref[1] = grad_in, grad_out
    rows = own_ref.shape[0]
    for ref in sends:
        n = ref.shape[0] // rows
        for k in range(n):
            ref[k * rows : (k + 1) * rows, :] = columns[k][...].astype(jnp.float32)
        columns = columns[n:]


def piece_specs(rows, size, width):
    tokens = pl.BlockSpec((2 * rows, width), lambda i, idx: (0, 0))
    return [
        pl.BlockSpec((rows, size), lambda i, idx: (0, idx[0])),
        tokens,
        tokens,
        pl.BlockSpec((size, width), lambda i, idx: (idx[0], 0)),
    ]


def partner_spec(rows, size, place):
    return pl.BlockSpec((rows, size), lambda i, idx: (place, 0))


def piece_cost(flops=1):
    return pl.CostEstimate(flops=flops, bytes_accessed=1, transcendentals=0)


def piece(
    scale, index, pre_act, partners, place, g, x, w_out, sums=(), other=None, is_inner=None, sends=(), after=(), flops=1
):
    rows, width = pre_act.shape[0], g.shape[1]
    size = sum(p.shape[1] for p in partners)
    whole = pl.BlockSpec((2, size, width), lambda i, idx: (0, 0, 0))
    others, other_specs = [], []
    if other is not None:
        others = [other[0]]
        other_specs = [partner_spec(rows, size, other[1])]
    columns = [column for send in sends for column in send]
    zero = jnp.int32(0)
    counts = (len(partners), len(others), len(columns), len(sums), len(after))
    out, *blocks = pl.pallas_call(
        functools.partial(piece_kernel, scale, counts),
        grid_spec=pltpu.PrefetchScalarGridSpec(
            num_scalar_prefetch=1,
            grid=(1,),
            in_specs=piece_specs(rows, size, width)
            + [partner_spec(rows, p.shape[1], place) for p in partners]
            + other_specs
            + [pl.BlockSpec((rows, size), lambda i, idx, k=k: (0, idx[3 + k])) for k in range(len(columns))]
            + [whole] * len(sums)
            + anywhere(after),
            out_specs=[whole] + [pl.BlockSpec((len(send) * rows, size), lambda i, idx: (0, 0)) for send in sends],
        ),
        out_shape=[jax.ShapeDtypeStruct((2, size, width), jnp.float32)]
        + [jax.ShapeDtypeStruct((len(send) * rows, size), jnp.float32) for send in sends],
        compiler_params=params(),
        cost_estimate=piece_cost(flops),
        name="piece",
    )(
        jnp.stack([index, zero, zero if is_inner is None else is_inner, *columns]),
        pre_act,
        g,
        x,
        w_out,
        *partners,
        *others,
        *([pre_act] * len(columns)),
        *sums,
        *after,
    )
    return out, *blocks


def final_kernel(scale, idx_ref, own_ref, g_ref, x_ref, w_ref, partner_ref, inner_ref, outer_ref, *refs):
    sum_ref, (in_ref, out_ref) = refs[0], refs[-2:]
    grad_in, grad_out = piece_math(
        scale, own_ref[...], partner_ref[...], g_ref[...], x_ref[...], w_ref[...]
    )
    is_inner = idx_ref[1] > 0
    in_ref[...] = jnp.where(is_inner, inner_ref[0], grad_in + outer_ref[0]) + sum_ref[0]
    out_ref[...] = jnp.where(is_inner, inner_ref[1], grad_out + outer_ref[1]) + sum_ref[1]


def final_first(scale, count, index, is_inner, pre_act, partner, place, g, x, w_out, held, received, added, after):
    rows, size, width = pre_act.shape[0], partner.shape[1], g.shape[1]
    whole = pl.BlockSpec((2, size, width), lambda i, idx: (0, 0, 0))
    shape = jax.ShapeDtypeStruct((count * size, width), jnp.float32)
    return pl.pallas_call(
        functools.partial(final_kernel, scale),
        grid_spec=pltpu.PrefetchScalarGridSpec(
            num_scalar_prefetch=1,
            grid=(1,),
            in_specs=piece_specs(rows, size, width)
            + [partner_spec(rows, size, place)]
            + [whole] * 3
            + anywhere(after),
            out_specs=[pl.BlockSpec((size, width), lambda i, idx: (0, 0))] * 2,
        ),
        out_shape=(shape, shape),
        compiler_params=params(),
        cost_estimate=piece_cost(),
        name="final_first",
    )(jnp.stack([index, is_inner]), pre_act, g, x, w_out, partner, held, received, added, *after)


def add_kernel(a_ref, b_ref, *refs):
    in_ref, out_ref = refs[-2:]
    in_ref[...] = a_ref[0] + b_ref[0]
    out_ref[...] = a_ref[1] + b_ref[1]


def final_add(place, a, b, held, after):
    _, size, width = a.shape
    steps = 3
    block = pl.BlockSpec((2, size // steps, width), lambda i: (0, i, 0))
    return pl.pallas_call(
        add_kernel,
        grid=(steps,),
        in_specs=[block, block] + anywhere(held) + anywhere(after),
        out_specs=[pl.BlockSpec((size // steps, width), lambda i: (place * steps + i, 0))] * 2,
        out_shape=[jax.ShapeDtypeStruct(h.shape, h.dtype) for h in held],
        input_output_aliases={2: 0, 3: 1},
        compiler_params=params(),
        name="final_add",
    )(a, b, *held, *after)


def line_body(inputs, out_grads, pre_act, w_in, w_out):
    count = PIECES
    rows, hidden = pre_act.shape
    size = hidden // (8 * count)
    scale = 1.0 / (rows * lax.axis_size("dp")) ** 0.5
    me, blk = lax.axis_index("dp"), lax.axis_index("blk")
    plane, half = me // 2, me % 2
    side = plane // 2
    inner = jnp.where((plane == 1) | (plane == 2), 1, 0).astype(jnp.int32)

    def by_role(on_inner, on_outer):
        return jnp.where(inner > 0, jnp.int32(on_inner), jnp.int32(on_outer))

    def links(pairs):
        return [(2 * a + h, 2 * b + h) for a, b in pairs for h in range(2)]

    def swap(array, planes):
        return lax.ppermute(array, "dp", [(2 * a + h, 2 * a + 1 - h) for a in planes for h in range(2)])

    def flip(array, bit):
        return lax.ppermute(array, "blk", [(i, i ^ bit) for i in range(4)])

    outer_to_inner = links([(0, 1), (3, 2)])
    inner_to_inner = links([(1, 2), (2, 1)])
    inner_to_outer = links([(1, 0), (2, 3)])
    every, outer_planes, inner_planes = (0, 1, 2, 3), (0, 3), (1, 2)

    def block(q, which):
        place = q // count
        chunk = jnp.where(side == 0, 3 - place, place)
        return (chunk * 2 + which) * count + q % count

    def mine(q):
        return block(q, half)

    def theirs(q):
        return block(q, 1 - half)

    near_inner = [2 * count + j for j in range(count)]
    near_outer = [3 * count + j for j in range(count)]
    steps = 3 * count - 1
    ahead = [s if s < 2 * count else s + 1 for s in range(steps)]
    main = [by_role(min(max(s - 2, 0), 2 * count - 1), ahead[s]) for s in range(steps)]
    own_chunk = [by_role(near_inner[j], near_outer[j]) for j in range(count)]
    double = steps - count
    first = jnp.int32(near_inner[0])

    quarter, send, raw = start_sends(
        blk,
        out_grads,
        inputs,
        [theirs(main[0]), theirs(main[1]), theirs(first), mine(first)],
        pre_act,
        size,
    )
    pair_0 = swap(quarter, every)
    received = swap(send, outer_planes)
    y = {0: (received, 0), 1: (received, 1)}
    quarter_in = lax.ppermute(quarter, "dp", outer_to_inner)
    raw_in = lax.ppermute(raw, "dp", outer_to_inner)
    pair_1, pair_2 = flip(pair_0, 1), flip(pair_0, 2)
    pair_3 = flip(pair_2, 1)
    g, x = join(blk, out_grads, inputs, [pair_0, pair_1, pair_2, pair_3], [])
    last = g

    def run(q, partner, **more):
        return piece(scale, mine(q), pre_act, [partner[0]], partner[1], g, x, w_out, **more)

    no, own = {}, {}
    toward, across = [], {}
    for s in range(steps):
        block_names, sends = [], []
        if s % 2 == 0:
            for store, key, q in (
                (y, s + 2, main[s + 2] if s + 2 < steps else None),
                (y, s + 3, main[s + 3] if s + 3 < steps else None),
                (no, s // 2, jnp.int32(near_outer[s // 2]) if s // 2 < count else None),
            ):
                if q is not None:
                    block_names.append((store, key))
                    sends.append(theirs(q))
            if s + 2 >= steps:
                for i in range(1, count):
                    block_names.append((own, i))
                    sends.append(theirs(own_chunk[i]))
        sums = [toward[s - 2]] if s >= 2 else []
        held_back = ([across[s - 4]] if s >= 4 else []) + ([raw_in, quarter_in] if s == 0 else []) + ([first_in] if s == 3 else [])
        j = s - double
        if j < 0:
            after = [last] + held_back
        else:
            (last,) = run(
                by_role(near_outer[j], ahead[s]),
                y[s],
                sums=[across[j]],
                other=no[j],
                is_inner=inner,
                after=[last] + sums + held_back,
            )
            toward.append(lax.ppermute(last, "dp", outer_to_inner + inner_to_outer))
            after = [last] + ([grad_inputs] if j == 0 else [])
        out, *blocks = run(main[s], y[s], sums=sums, sends=[sends] if sends else [], after=after, flops=FLOPS if s == 3 else 1)
        last = out
        if j < 0:
            toward.append(lax.ppermute(out, "dp", outer_to_inner))
        if blocks:
            received = swap(blocks[0], every)
            for place, (store, key) in enumerate(block_names):
                store[key] = (received, place)
        if s >= 2:
            across[s - 2] = lax.ppermute(out, "dp", inner_to_inner)
        if s == 1:
            in_1, in_2 = flip(quarter_in, 1), flip(quarter_in, 2)
            in_3 = flip(in_2, 1)
            line_g, line_x = join(blk, out_grads, inputs, [quarter_in, in_1, in_2, in_3], [last])
            (last,) = piece(scale, theirs(first), pre_act, [raw_in], 0, line_g, line_x, w_out, after=[last])
            first_in = swap(last, inner_planes)
            last = input_partial(out_grads, pre_act, w_in, w_out, 4 * size, [last])
            grad_inputs = lax.psum_scatter(last, "blk", scatter_dimension=0, tiled=True)
            grad_inputs = grad_inputs.astype(jnp.bfloat16)
        if s == 4:
            (held_in,) = piece(
                scale, mine(first), pre_act, [raw_in], 1, line_g, line_x, w_out, sums=[first_in], after=[last]
            )
            last = held_in

    held = final_first(
        scale,
        count,
        mine(jnp.int32(near_outer[0])),
        inner,
        pre_act,
        no[0][0],
        no[0][1],
        g,
        x,
        w_out,
        held_in,
        toward[double],
        across[count],
        [last],
    )
    for i in range(1, count):
        (out,) = run(own_chunk[i], own[i], sums=[across[count + i]], after=[held[0]])
        held = final_add(i, out, toward[double + i], held, [])
    return (grad_inputs, held[0], held[1])


def solution(mesh):
    def body(inputs, out_grads, pre_act, w_in, w_out):
        fits = pre_act.shape[1] % (8 * PIECES * 128) == 0 and inputs.shape[0] % 64 == 0
        run = line_body if (mesh.shape["dp"], mesh.shape["blk"]) == (8, 4) and fits else plain_body
        return run(inputs, out_grads, pre_act, w_in, w_out)

    return jax.shard_map(
        body,
        mesh=mesh,
        in_specs=(P("dp", None), P("dp", None), P("dp", "blk"), P("blk", None), P("blk", None)),
        out_specs=(P(("dp", "blk"), None), P(("blk", "dp"), None), P(("blk", "dp"), None)),
        check_vma=False,
    )
```

```python
import functools

import jax
import jax.numpy as jnp
from jax import lax
from jax.experimental import pallas as pl
from jax.experimental.pallas import tpu as pltpu
from jax.sharding import PartitionSpec as P

PIECES = 3
FLOPS = 100_000_000_000
VMEM_LIMIT = 56 * 1024 * 1024


def contract_rows(left, right):
    return lax.dot_general(
        left, right, (((0,), (0,)), ((), ())), preferred_element_type=jnp.float32
    )


def hidden_grads(out_grads, pre_act, w_out):
    back = lax.dot_general(
        out_grads, w_out, (((1,), (1,)), ((), ())), preferred_element_type=jnp.float32
    )
    return jnp.where(pre_act > 0, back, jnp.zeros_like(back)).astype(jnp.bfloat16)


def input_grads(grad_hidden, w_in):
    return lax.psum_scatter(
        jnp.dot(grad_hidden, w_in, preferred_element_type=jnp.float32),
        "blk",
        scatter_dimension=0,
        tiled=True,
    ).astype(jnp.bfloat16)


def plain_body(inputs, out_grads, pre_act, w_in, w_out):
    token_total = inputs.shape[0] * lax.axis_size("dp")
    factor = lax.rsqrt(jnp.asarray(token_total, jnp.float32))
    act = jnp.maximum(pre_act, jnp.zeros_like(pre_act))
    grad_hidden = hidden_grads(out_grads, pre_act, w_out)
    grad_out = contract_rows(act, out_grads) * factor
    grad_in = contract_rows(grad_hidden, inputs) * factor
    return (
        input_grads(grad_hidden, w_in),
        lax.psum_scatter(grad_in, "dp", scatter_dimension=0, tiled=True),
        lax.psum_scatter(grad_out, "dp", scatter_dimension=0, tiled=True),
    )


def params():
    return pltpu.CompilerParams(vmem_limit_bytes=VMEM_LIMIT)


def anywhere(arrays):
    return [pl.BlockSpec(memory_space=pl.ANY)] * len(arrays)


def cast_kernel(idx_ref, pre_ref, *refs):
    refs[-1][...] = pre_ref[...].astype(jnp.float32)


def cast_block(index, pre_act, size, after):
    rows = pre_act.shape[0]
    return pl.pallas_call(
        cast_kernel,
        grid_spec=pltpu.PrefetchScalarGridSpec(
            num_scalar_prefetch=1,
            grid=(1,),
            in_specs=[pl.BlockSpec((rows, size), lambda i, idx: (0, idx[0]))] + anywhere(after),
            out_specs=pl.BlockSpec((rows, size), lambda i, idx: (0, 0)),
        ),
        out_shape=jax.ShapeDtypeStruct((rows, size), jnp.float32),
        compiler_params=params(),
        cost_estimate=piece_cost(),
        name="cast_block",
    )(index.reshape(1), pre_act, *after)


def start_kernel(idx_ref, grads_ref, inputs_ref, *refs):
    columns, (quarter_ref, *outs) = refs[:2], refs[-3:]
    quarter, rows = grads_ref.shape[0], columns[0].shape[0]
    quarter_ref[:quarter, :] = grads_ref[...].astype(jnp.float32)
    quarter_ref[quarter:, :] = inputs_ref[...].astype(jnp.float32)
    for ref, out_ref in zip(columns, outs):
        out_ref[...] = ref[...].astype(jnp.float32)


def start_sends(blk, out_grads, inputs, columns, pre_act, size, after):
    rows, width = out_grads.shape
    quarter = rows // 4
    tokens = pl.BlockSpec((quarter, width), lambda i, idx: (idx[0], 0))
    shapes = [(2 * quarter, width)] + [(rows, size)] * 2
    return pl.pallas_call(
        start_kernel,
        grid_spec=pltpu.PrefetchScalarGridSpec(
            num_scalar_prefetch=1,
            grid=(1,),
            in_specs=[tokens, tokens]
            + [pl.BlockSpec((rows, size), lambda i, idx, k=k: (0, idx[k])) for k in (1, 2)]
            + anywhere(after),
            out_specs=[pl.BlockSpec(shape, lambda i, idx: (0, 0)) for shape in shapes],
        ),
        out_shape=[jax.ShapeDtypeStruct(shape, jnp.float32) for shape in shapes],
        compiler_params=params(),
        cost_estimate=piece_cost(),
        name="start_sends",
    )(jnp.stack([blk, *columns]), out_grads, inputs, *([pre_act] * 2), *after)


def join_kernel(n_quarters, blk_ref, grads_ref, inputs_ref, *refs):
    quarters, (g_ref, x_ref) = refs[:n_quarters], refs[-2:]
    rows = grads_ref.shape[0]
    quarter = rows // 4
    g_ref[:rows, :] = grads_ref[...]
    x_ref[:rows, :] = inputs_ref[...]
    for k in range(4):
        if n_quarters == 1:
            place = pl.ds(rows + k * quarter, quarter)
            ref, start = quarters[0], 2 * k * quarter
        else:
            where = jnp.bitwise_xor(blk_ref[0], k)
            place = pl.ds(pl.multiple_of(rows + where * quarter, quarter), quarter)
            ref, start = quarters[k], 0
        g_ref[place, :] = ref[start : start + quarter, :].astype(jnp.bfloat16)
        x_ref[place, :] = ref[start + quarter : start + 2 * quarter, :].astype(jnp.bfloat16)


def join(blk, out_grads, inputs, quarters, after):
    rows, width = out_grads.shape
    shape = jax.ShapeDtypeStruct((2 * rows, width), jnp.bfloat16)
    vmem = pl.BlockSpec(memory_space=pltpu.VMEM)
    return pl.pallas_call(
        functools.partial(join_kernel, len(quarters)),
        out_shape=(shape, shape),
        in_specs=[pl.BlockSpec(memory_space=pltpu.SMEM)] + [vmem] * (2 + len(quarters)) + anywhere(after),
        out_specs=(vmem, vmem),
        compiler_params=params(),
        cost_estimate=piece_cost(),
        name="join_tokens",
    )(blk.reshape(1), out_grads, inputs, *quarters, *after)


def input_kernel(grads_ref, pre_ref, out_rows_ref, in_rows_ref, *refs):
    total_ref = refs[-1]

    @pl.when(pl.program_id(0) == 0)
    def _():
        total_ref[...] = jnp.zeros_like(total_ref)

    hidden = hidden_grads(grads_ref[...], pre_ref[...], out_rows_ref[...])
    total_ref[...] += jnp.dot(hidden, in_rows_ref[...], preferred_element_type=jnp.float32)


def input_partial(out_grads, pre_act, w_in, w_out, size, after):
    rows, hidden = pre_act.shape
    width = out_grads.shape[1]
    tokens = pl.BlockSpec((rows, width), lambda i: (0, 0))
    weights = pl.BlockSpec((size, width), lambda i: (i, 0))
    return pl.pallas_call(
        input_kernel,
        grid=(hidden // size,),
        in_specs=[tokens, pl.BlockSpec((rows, size), lambda i: (0, i)), weights, weights] + anywhere(after),
        out_specs=tokens,
        out_shape=jax.ShapeDtypeStruct((rows, width), jnp.float32),
        compiler_params=params(),
        cost_estimate=piece_cost(),
        name="input_partial",
    )(out_grads, pre_act, w_out, w_in, *after)


def piece_math(scale, own, partner, g, x, w):
    pre = jnp.concatenate([own, partner.astype(jnp.bfloat16)], axis=0)
    hidden = hidden_grads(g, pre, w)
    act = jnp.maximum(pre, jnp.zeros_like(pre))
    return contract_rows(hidden, x) * scale, contract_rows(act, g) * scale


def piece_kernel(scale, counts, idx_ref, own_ref, g_ref, x_ref, w_ref, *refs):
    groups = []
    for n in counts:
        groups.append(refs[:n])
        refs = refs[n:]
    partners, others, columns, sums, _, (out_ref, *sends) = groups + [refs]
    partner = jnp.concatenate([ref[...] for ref in partners], axis=1)
    for ref in others:
        partner = jnp.where(idx_ref[2] > 0, ref[...], partner)
    grad_in, grad_out = piece_math(scale, own_ref[...], partner, g_ref[...], x_ref[...], w_ref[...])
    for ref in sums:
        grad_in = grad_in + ref[0]
        grad_out = grad_out + ref[1]
    out_ref[0], out_ref[1] = grad_in, grad_out
    rows = own_ref.shape[0]
    for ref in sends:
        n = ref.shape[0] // rows
        for k in range(n):
            ref[k * rows : (k + 1) * rows, :] = columns[k][...].astype(jnp.float32)
        columns = columns[n:]


def piece_specs(rows, size, width):
    tokens = pl.BlockSpec((2 * rows, width), lambda i, idx: (0, 0))
    return [
        pl.BlockSpec((rows, size), lambda i, idx: (0, idx[0])),
        tokens,
        tokens,
        pl.BlockSpec((size, width), lambda i, idx: (idx[0], 0)),
    ]


def partner_spec(rows, size, place):
    return pl.BlockSpec((rows, size), lambda i, idx: (place, 0))


def piece_cost(flops=1):
    return pl.CostEstimate(flops=flops, bytes_accessed=1, transcendentals=0)


def piece(
    scale, index, pre_act, partners, place, g, x, w_out, sums=(), other=None, is_inner=None, sends=(), after=(), flops=1
):
    rows, width = pre_act.shape[0], g.shape[1]
    size = sum(p.shape[1] for p in partners)
    whole = pl.BlockSpec((2, size, width), lambda i, idx: (0, 0, 0))
    others, other_specs = [], []
    if other is not None:
        others = [other[0]]
        other_specs = [partner_spec(rows, size, other[1])]
    columns = [column for send in sends for column in send]
    zero = jnp.int32(0)
    counts = (len(partners), len(others), len(columns), len(sums), len(after))
    out, *blocks = pl.pallas_call(
        functools.partial(piece_kernel, scale, counts),
        grid_spec=pltpu.PrefetchScalarGridSpec(
            num_scalar_prefetch=1,
            grid=(1,),
            in_specs=piece_specs(rows, size, width)
            + [partner_spec(rows, p.shape[1], place) for p in partners]
            + other_specs
            + [pl.BlockSpec((rows, size), lambda i, idx, k=k: (0, idx[3 + k])) for k in range(len(columns))]
            + [whole] * len(sums)
            + anywhere(after),
            out_specs=[whole] + [pl.BlockSpec((len(send) * rows, size), lambda i, idx: (0, 0)) for send in sends],
        ),
        out_shape=[jax.ShapeDtypeStruct((2, size, width), jnp.float32)]
        + [jax.ShapeDtypeStruct((len(send) * rows, size), jnp.float32) for send in sends],
        compiler_params=params(),
        cost_estimate=piece_cost(flops),
        name="piece",
    )(
        jnp.stack([index, zero, zero if is_inner is None else is_inner, *columns]),
        pre_act,
        g,
        x,
        w_out,
        *partners,
        *others,
        *([pre_act] * len(columns)),
        *sums,
        *after,
    )
    return out, *blocks


def final_kernel(scale, idx_ref, own_ref, g_ref, x_ref, w_ref, partner_ref, inner_ref, outer_ref, *refs):
    sum_ref, (in_ref, out_ref) = refs[0], refs[-2:]
    grad_in, grad_out = piece_math(
        scale, own_ref[...], partner_ref[...], g_ref[...], x_ref[...], w_ref[...]
    )
    is_inner = idx_ref[1] > 0
    in_ref[...] = jnp.where(is_inner, inner_ref[0], grad_in + outer_ref[0]) + sum_ref[0]
    out_ref[...] = jnp.where(is_inner, inner_ref[1], grad_out + outer_ref[1]) + sum_ref[1]


def final_first(scale, count, index, is_inner, pre_act, partner, place, g, x, w_out, held, received, added, after):
    rows, size, width = pre_act.shape[0], partner.shape[1], g.shape[1]
    whole = pl.BlockSpec((2, size, width), lambda i, idx: (0, 0, 0))
    shape = jax.ShapeDtypeStruct((count * size, width), jnp.float32)
    return pl.pallas_call(
        functools.partial(final_kernel, scale),
        grid_spec=pltpu.PrefetchScalarGridSpec(
            num_scalar_prefetch=1,
            grid=(1,),
            in_specs=piece_specs(rows, size, width)
            + [partner_spec(rows, size, place)]
            + [whole] * 3
            + anywhere(after),
            out_specs=[pl.BlockSpec((size, width), lambda i, idx: (0, 0))] * 2,
        ),
        out_shape=(shape, shape),
        compiler_params=params(),
        cost_estimate=piece_cost(),
        name="final_first",
    )(jnp.stack([index, is_inner]), pre_act, g, x, w_out, partner, held, received, added, *after)


def add_kernel(a_ref, b_ref, *refs):
    in_ref, out_ref = refs[-2:]
    in_ref[...] = a_ref[0] + b_ref[0]
    out_ref[...] = a_ref[1] + b_ref[1]


def final_add(place, a, b, held, after):
    _, size, width = a.shape
    steps = 3
    block = pl.BlockSpec((2, size // steps, width), lambda i: (0, i, 0))
    return pl.pallas_call(
        add_kernel,
        grid=(steps,),
        in_specs=[block, block] + anywhere(held) + anywhere(after),
        out_specs=[pl.BlockSpec((size // steps, width), lambda i: (place * steps + i, 0))] * 2,
        out_shape=[jax.ShapeDtypeStruct(h.shape, h.dtype) for h in held],
        input_output_aliases={2: 0, 3: 1},
        compiler_params=params(),
        name="final_add",
    )(a, b, *held, *after)


def line_body(inputs, out_grads, pre_act, w_in, w_out):
    count = PIECES
    rows, hidden = pre_act.shape
    size = hidden // (8 * count)
    scale = 1.0 / (rows * lax.axis_size("dp")) ** 0.5
    me, blk = lax.axis_index("dp"), lax.axis_index("blk")
    plane, half = me // 2, me % 2
    side = plane // 2
    inner = jnp.where((plane == 1) | (plane == 2), 1, 0).astype(jnp.int32)

    def by_role(on_inner, on_outer):
        return jnp.where(inner > 0, jnp.int32(on_inner), jnp.int32(on_outer))

    def links(pairs):
        return [(2 * a + h, 2 * b + h) for a, b in pairs for h in range(2)]

    def swap(array, planes):
        return lax.ppermute(array, "dp", [(2 * a + h, 2 * a + 1 - h) for a in planes for h in range(2)])

    def flip(array, bit):
        return lax.ppermute(array, "blk", [(i, i ^ bit) for i in range(4)])

    outer_to_inner = links([(0, 1), (3, 2)])
    inner_to_inner = links([(1, 2), (2, 1)])
    inner_to_outer = links([(1, 0), (2, 3)])
    every, inner_planes = (0, 1, 2, 3), (1, 2)

    def block(q, which):
        place = q // count
        chunk = jnp.where(side == 0, 3 - place, place)
        return (chunk * 2 + which) * count + q % count

    def mine(q):
        return block(q, half)

    def theirs(q):
        return block(q, 1 - half)

    near_inner = [2 * count + j for j in range(count)]
    near_outer = [3 * count + j for j in range(count)]
    steps = 3 * count - 1
    ahead = [s if s < 2 * count else s + 1 for s in range(steps)]
    main = [by_role(min(max(s - 2, 0), 2 * count - 1), ahead[s]) for s in range(steps)]
    own_chunk = [by_role(near_inner[j], near_outer[j]) for j in range(count)]
    double = steps - count
    first = jnp.int32(near_inner[0])

    inner_main, outer_main = [max(s - 2, 0) for s in range(steps)], ahead
    exchanges = [
        [(near_outer[0], outer_main[0])],
        [(near_outer[1], outer_main[1])],
        [(inner_main[2], outer_main[2]), (inner_main[3], outer_main[3])],
        [(inner_main[4], outer_main[4]), (inner_main[5], outer_main[5])],
        [
            (inner_main[6], outer_main[6]),
            (inner_main[7], outer_main[7]),
            (near_outer[2], near_outer[0]),
        ],
        [(near_inner[1], near_outer[1]), (near_inner[2], near_outer[2])],
    ]

    def columns_of(e):
        return [theirs(by_role(*pair)) for pair in exchanges[e]]

    raw = [cast_block(theirs(first), pre_act, size, [])]
    quarter, send, last = start_sends(
        blk, out_grads, inputs, columns_of(0) + [mine(first)], pre_act, size, raw
    )
    raw.append(last)
    pair_0 = swap(quarter, every)
    got = [swap(send, every)]
    quarter_in = lax.ppermute(quarter, "dp", outer_to_inner)
    raw_in = [lax.ppermute(array, "dp", outer_to_inner) for array in raw]
    last = cast_block(columns_of(1)[0], pre_act, size, [pair_0])
    got.append(swap(last, every))
    pair_1, pair_2 = flip(pair_0, 1), flip(pair_0, 2)
    pair_2, got[0], raw_in[0] = lax.optimization_barrier((pair_2, got[0], raw_in[0]))
    pair_3 = flip(pair_2, 1)
    pair_3, quarter_in = lax.optimization_barrier((pair_3, quarter_in))
    line_rows = lax.all_gather(quarter_in, "blk", tiled=True)
    g, x = join(blk, out_grads, inputs, [pair_0, pair_1, pair_2, pair_3], [last, got[0], raw_in[0]])
    last = g

    def run(q, partner, **more):
        return piece(scale, mine(q), pre_act, [partner[0]], partner[1], g, x, w_out, **more)

    toward, across = [], {}
    for s in range(steps):
        partner = (got[s], 0) if s < 2 else (got[1 + s // 2], s % 2)
        sends = columns_of(2 + s // 2) if s % 2 == 0 else []
        sums = [toward[s - 2]] if s >= 2 else []
        held_back = ([across[s - 4]] if s >= 4 else []) + ([raw_in[1]] if s == 1 else []) + ([first_in] if s == 3 else [])
        j = s - double
        if j < 0:
            after = [last] + held_back
        else:
            (last,) = run(
                by_role(near_outer[j], ahead[s]),
                partner,
                sums=[across[j]],
                other=(got[j], 0) if j < 2 else (got[4], 2),
                is_inner=inner,
                after=[last] + sums + held_back,
            )
            toward.append(lax.ppermute(last, "dp", outer_to_inner + inner_to_outer))
            after = [last] + ([grad_inputs] if j == 0 else [])
        out, *blocks = run(main[s], partner, sums=sums, sends=[sends] if sends else [], after=after, flops=FLOPS if s == 3 else 1)
        last = out
        if j < 0:
            toward.append(lax.ppermute(out, "dp", outer_to_inner))
        if blocks:
            got.append(swap(blocks[0], every))
        if s >= 2:
            across[s - 2] = lax.ppermute(out, "dp", inner_to_inner)
        if s == 1:
            line_g, line_x = join(blk, out_grads, inputs, [line_rows], [last])
            (last,) = piece(scale, theirs(first), pre_act, [raw_in[0]], 0, line_g, line_x, w_out, after=[last])
            first_in = swap(last, inner_planes)
            last = input_partial(out_grads, pre_act, w_in, w_out, 4 * size, [last])
            grad_inputs = lax.psum_scatter(last, "blk", scatter_dimension=0, tiled=True)
            grad_inputs = grad_inputs.astype(jnp.bfloat16)
        if s == 4:
            (held_in,) = piece(
                scale, mine(first), pre_act, [raw_in[1]], 0, line_g, line_x, w_out, sums=[first_in], after=[last]
            )
            last = held_in

    held = final_first(
        scale,
        count,
        mine(jnp.int32(near_outer[0])),
        inner,
        pre_act,
        got[4],
        2,
        g,
        x,
        w_out,
        held_in,
        toward[double],
        across[count],
        [last],
    )
    for i in range(1, count):
        (out,) = run(own_chunk[i], (got[5], i - 1), sums=[across[count + i]], after=[held[0]])
        held = final_add(i, out, toward[double + i], held, [])
    return (grad_inputs, held[0], held[1])


def solution(mesh):
    def body(inputs, out_grads, pre_act, w_in, w_out):
        fits = pre_act.shape[1] % (8 * PIECES * 128) == 0 and inputs.shape[0] % 64 == 0
        run = line_body if (mesh.shape["dp"], mesh.shape["blk"]) == (8, 4) and fits else plain_body
        return run(inputs, out_grads, pre_act, w_in, w_out)

    return jax.shard_map(
        body,
        mesh=mesh,
        in_specs=(P("dp", None), P("dp", None), P("dp", "blk"), P("blk", None), P("blk", None)),
        out_specs=(P(("dp", "blk"), None), P(("blk", "dp"), None), P(("blk", "dp"), None)),
        check_vma=False,
    )
```

```python
import functools

import jax
import jax.numpy as jnp
from jax import lax
from jax.experimental import pallas as pl
from jax.experimental.pallas import tpu as pltpu
from jax.sharding import PartitionSpec as P

PIECES = 3
FLOPS = 100_000_000_000
VMEM_LIMIT = 63 * 1024 * 1024


def contract_rows(left, right):
    return lax.dot_general(
        left, right, (((0,), (0,)), ((), ())), preferred_element_type=jnp.float32
    )


def hidden_grads(out_grads, pre_act, w_out):
    back = lax.dot_general(
        out_grads, w_out, (((1,), (1,)), ((), ())), preferred_element_type=jnp.float32
    )
    return jnp.where(pre_act > 0, back, jnp.zeros_like(back)).astype(jnp.bfloat16)


def input_grads(grad_hidden, w_in):
    return lax.psum_scatter(
        jnp.dot(grad_hidden, w_in, preferred_element_type=jnp.float32),
        "blk",
        scatter_dimension=0,
        tiled=True,
    ).astype(jnp.bfloat16)


def plain_body(inputs, out_grads, pre_act, w_in, w_out):
    token_total = inputs.shape[0] * lax.axis_size("dp")
    factor = lax.rsqrt(jnp.asarray(token_total, jnp.float32))
    act = jnp.maximum(pre_act, jnp.zeros_like(pre_act))
    grad_hidden = hidden_grads(out_grads, pre_act, w_out)
    grad_out = contract_rows(act, out_grads) * factor
    grad_in = contract_rows(grad_hidden, inputs) * factor
    return (
        input_grads(grad_hidden, w_in),
        lax.psum_scatter(grad_in, "dp", scatter_dimension=0, tiled=True),
        lax.psum_scatter(grad_out, "dp", scatter_dimension=0, tiled=True),
    )


def params():
    return pltpu.CompilerParams(vmem_limit_bytes=VMEM_LIMIT)


def anywhere(arrays):
    return [pl.BlockSpec(memory_space=pl.ANY)] * len(arrays)


def cast_kernel(shapes, idx_ref, *refs):
    outs = refs[-len(shapes) :]
    for (_, count), out_ref in zip(shapes, outs):
        width = out_ref.shape[1] // count
        for k in range(count):
            out_ref[:, k * width : (k + 1) * width] = refs[k][...].astype(jnp.float32)
        refs = refs[count:]


def cast_blocks(table, groups, pre_act, after):
    rows = pre_act.shape[0]
    in_specs = [columns_spec(rows, width, at) for width, places in groups for at in places]
    shapes = [(width * len(places), len(places)) for width, places in groups]
    return pl.pallas_call(
        functools.partial(cast_kernel, shapes),
        grid_spec=pltpu.PrefetchScalarGridSpec(
            num_scalar_prefetch=1,
            grid=(1,),
            in_specs=in_specs + anywhere(after),
            out_specs=[pl.BlockSpec((rows, width), lambda i, idx: (0, 0)) for width, _ in shapes],
        ),
        out_shape=[jax.ShapeDtypeStruct((rows, width), jnp.float32) for width, _ in shapes],
        compiler_params=params(),
        cost_estimate=piece_cost(),
        name="cast_blocks",
    )(table, *([pre_act] * len(in_specs)), *after)


def first_kernel(idx_ref, grads_ref, inputs_ref, pre_ref, quarter_ref, raw_ref):
    quarter = grads_ref.shape[0]
    quarter_ref[:quarter, :] = grads_ref[...].astype(jnp.float32)
    quarter_ref[quarter:, :] = inputs_ref[...].astype(jnp.float32)
    raw_ref[...] = pre_ref[...].astype(jnp.float32)


def first_sends(indices, out_grads, inputs, pre_act, size):
    rows, width = out_grads.shape
    quarter = rows // 4
    tokens = pl.BlockSpec((quarter, width), lambda i, idx: (idx[0], 0))
    return pl.pallas_call(
        first_kernel,
        grid_spec=pltpu.PrefetchScalarGridSpec(
            num_scalar_prefetch=1,
            grid=(1,),
            in_specs=[tokens, tokens, columns_spec(rows, size, 1)],
            out_specs=[
                pl.BlockSpec((2 * quarter, width), lambda i, idx: (0, 0)),
                pl.BlockSpec((rows, size), lambda i, idx: (0, 0)),
            ],
        ),
        out_shape=[
            jax.ShapeDtypeStruct((2 * quarter, width), jnp.float32),
            jax.ShapeDtypeStruct((rows, size), jnp.float32),
        ],
        compiler_params=params(),
        cost_estimate=piece_cost(),
        name="first_sends",
    )(indices, out_grads, inputs, pre_act)


def join_kernel(n_quarters, blk_ref, grads_ref, inputs_ref, *refs):
    quarters, (g_ref, x_ref) = refs[:n_quarters], refs[-2:]
    rows = grads_ref.shape[0]
    quarter = rows // 4
    g_ref[:rows, :] = grads_ref[...]
    x_ref[:rows, :] = inputs_ref[...]
    for k in range(4):
        if n_quarters == 1:
            place = pl.ds(rows + k * quarter, quarter)
            ref, start = quarters[0], 2 * k * quarter
        else:
            where = jnp.bitwise_xor(blk_ref[0], k)
            place = pl.ds(pl.multiple_of(rows + where * quarter, quarter), quarter)
            ref, start = quarters[k], 0
        g_ref[place, :] = ref[start : start + quarter, :].astype(jnp.bfloat16)
        x_ref[place, :] = ref[start + quarter : start + 2 * quarter, :].astype(jnp.bfloat16)


def join(blk, out_grads, inputs, quarters, after):
    rows, width = out_grads.shape
    shape = jax.ShapeDtypeStruct((2 * rows, width), jnp.bfloat16)
    vmem = pl.BlockSpec(memory_space=pltpu.VMEM)
    return pl.pallas_call(
        functools.partial(join_kernel, len(quarters)),
        out_shape=(shape, shape),
        in_specs=[pl.BlockSpec(memory_space=pltpu.SMEM)] + [vmem] * (2 + len(quarters)) + anywhere(after),
        out_specs=(vmem, vmem),
        compiler_params=params(),
        cost_estimate=piece_cost(),
        name="join_tokens",
    )(blk.reshape(1), out_grads, inputs, *quarters, *after)


def input_kernel(grads_ref, pre_ref, out_rows_ref, in_rows_ref, *refs):
    total_ref = refs[-1]

    @pl.when(pl.program_id(0) == 0)
    def _():
        total_ref[...] = jnp.zeros_like(total_ref)

    hidden = hidden_grads(grads_ref[...], pre_ref[...], out_rows_ref[...])
    total_ref[...] += jnp.dot(hidden, in_rows_ref[...], preferred_element_type=jnp.float32)


def input_partial(out_grads, pre_act, w_in, w_out, size, after):
    rows, hidden = pre_act.shape
    width = out_grads.shape[1]
    tokens = pl.BlockSpec((rows, width), lambda i: (0, 0))
    weights = pl.BlockSpec((size, width), lambda i: (i, 0))
    return pl.pallas_call(
        input_kernel,
        grid=(hidden // size,),
        in_specs=[tokens, pl.BlockSpec((rows, size), lambda i: (0, i)), weights, weights] + anywhere(after),
        out_specs=tokens,
        out_shape=jax.ShapeDtypeStruct((rows, width), jnp.float32),
        compiler_params=params(),
        cost_estimate=piece_cost(FLOPS),
        name="input_partial",
    )(out_grads, pre_act, w_out, w_in, *after)


def piece_math(scale, own, partner, g, x, w):
    pre = jnp.concatenate([own, partner.astype(jnp.bfloat16)], axis=0)
    hidden = hidden_grads(g, pre, w)
    act = jnp.maximum(pre, jnp.zeros_like(pre))
    return contract_rows(hidden, x) * scale, contract_rows(act, g) * scale


def piece_kernel(scale, counts, inner_at, table_ref, own_ref, g_ref, x_ref, w_ref, *refs):
    groups = []
    for n in counts:
        groups.append(refs[:n])
        refs = refs[n:]
    partners, others, columns, sums, _, (out_ref, *sends) = groups + [refs]
    partner = jnp.concatenate([ref[...] for ref in partners], axis=1)
    for ref in others:
        partner = jnp.where(table_ref[inner_at] > 0, ref[...], partner)
    grad_in, grad_out = piece_math(scale, own_ref[...], partner, g_ref[...], x_ref[...], w_ref[...])
    for ref in sums:
        grad_in = grad_in + ref[0]
        grad_out = grad_out + ref[1]
    out_ref[0], out_ref[1] = grad_in, grad_out
    rows = own_ref.shape[0]
    for ref in sends:
        for k, column_ref in enumerate(columns):
            ref[k * rows : (k + 1) * rows, :] = column_ref[...].astype(jnp.float32)


def columns_spec(rows, size, at):
    return pl.BlockSpec((rows, size), lambda i, table: (0, table[at]))


def piece_specs(rows, size, width, at):
    tokens = pl.BlockSpec((2 * rows, width), lambda i, table: (0, 0))
    return [
        columns_spec(rows, size, at),
        tokens,
        tokens,
        pl.BlockSpec((size, width), lambda i, table: (table[at], 0)),
    ]


def partner_spec(rows, size, place):
    return pl.BlockSpec((rows, size), lambda i, table: (place, 0))


def piece_cost(flops=1):
    return pl.CostEstimate(flops=flops, bytes_accessed=1, transcendentals=0)


def piece(
    scale, table, at, pre_act, partners, place, g, x, w_out, sums=(), other=None, inner_at=0, sends=(), after=(), flops=1
):
    rows, width = pre_act.shape[0], g.shape[1]
    size = sum(p.shape[1] for p in partners)
    whole = pl.BlockSpec((2, size, width), lambda i, table: (0, 0, 0))
    others, other_specs = [], []
    if other is not None:
        others = [other[0]]
        other_specs = [partner_spec(rows, size, other[1])]
    counts = (len(partners), len(others), len(sends), len(sums), len(after))
    sent = [(len(sends) * rows, size)] if sends else []
    return pl.pallas_call(
        functools.partial(piece_kernel, scale, counts, inner_at),
        grid_spec=pltpu.PrefetchScalarGridSpec(
            num_scalar_prefetch=1,
            grid=(1,),
            in_specs=piece_specs(rows, size, width, at)
            + [partner_spec(rows, p.shape[1], place) for p in partners]
            + other_specs
            + [columns_spec(rows, size, k) for k in sends]
            + [whole] * len(sums)
            + anywhere(after),
            out_specs=[whole] + [pl.BlockSpec(shape, lambda i, table: (0, 0)) for shape in sent],
        ),
        out_shape=[jax.ShapeDtypeStruct(shape, jnp.float32) for shape in [(2, size, width)] + sent],
        compiler_params=params(),
        cost_estimate=piece_cost(flops),
        name="piece",
    )(table, pre_act, g, x, w_out, *partners, *others, *([pre_act] * len(sends)), *sums, *after)


def final_kernel(scale, inner_at, table_ref, own_ref, g_ref, x_ref, w_ref, partner_ref, inner_ref, outer_ref, *refs):
    sum_ref, (in_ref, out_ref) = refs[0], refs[-2:]
    grad_in, grad_out = piece_math(
        scale, own_ref[...], partner_ref[...], g_ref[...], x_ref[...], w_ref[...]
    )
    is_inner = table_ref[inner_at] > 0
    in_ref[...] = jnp.where(is_inner, inner_ref[0], grad_in + outer_ref[0]) + sum_ref[0]
    out_ref[...] = jnp.where(is_inner, inner_ref[1], grad_out + outer_ref[1]) + sum_ref[1]


def final_first(
    scale, count, table, at, inner_at, pre_act, partner, place, g, x, w_out, held, received, added, after
):
    rows, size, width = pre_act.shape[0], partner.shape[1], g.shape[1]
    whole = pl.BlockSpec((2, size, width), lambda i, table: (0, 0, 0))
    shape = jax.ShapeDtypeStruct((count * size, width), jnp.float32)
    return pl.pallas_call(
        functools.partial(final_kernel, scale, inner_at),
        grid_spec=pltpu.PrefetchScalarGridSpec(
            num_scalar_prefetch=1,
            grid=(1,),
            in_specs=piece_specs(rows, size, width, at)
            + [partner_spec(rows, size, place)]
            + [whole] * 3
            + anywhere(after),
            out_specs=[pl.BlockSpec((size, width), lambda i, table: (0, 0))] * 2,
        ),
        out_shape=(shape, shape),
        compiler_params=params(),
        cost_estimate=piece_cost(),
        name="final_first",
    )(table, pre_act, g, x, w_out, partner, held, received, added, *after)


def add_kernel(a_ref, b_ref, *refs):
    in_ref, out_ref = refs[-2:]
    in_ref[...] = a_ref[0] + b_ref[0]
    out_ref[...] = a_ref[1] + b_ref[1]


def final_add(place, a, b, held, after):
    _, size, width = a.shape
    steps = 3
    block = pl.BlockSpec((2, size // steps, width), lambda i: (0, i, 0))
    return pl.pallas_call(
        add_kernel,
        grid=(steps,),
        in_specs=[block, block] + anywhere(held) + anywhere(after),
        out_specs=[pl.BlockSpec((size // steps, width), lambda i: (place * steps + i, 0))] * 2,
        out_shape=[jax.ShapeDtypeStruct(h.shape, h.dtype) for h in held],
        input_output_aliases={2: 0, 3: 1},
        compiler_params=params(),
        name="final_add",
    )(a, b, *held, *after)


def line_body(inputs, out_grads, pre_act, w_in, w_out):
    count = PIECES
    rows, hidden = pre_act.shape
    size = hidden // (8 * count)
    scale = 1.0 / (rows * lax.axis_size("dp")) ** 0.5
    me, blk = lax.axis_index("dp"), lax.axis_index("blk")
    plane, half = me // 2, me % 2
    side = plane // 2
    inner = jnp.where((plane == 1) | (plane == 2), 1, 0).astype(jnp.int32)

    def by_role(on_inner, on_outer):
        return jnp.where(inner > 0, jnp.int32(on_inner), jnp.int32(on_outer))

    def links(pairs):
        return [(2 * a + h, 2 * b + h) for a, b in pairs for h in range(2)]

    def swap(array, planes):
        return lax.ppermute(array, "dp", [(2 * a + h, 2 * a + 1 - h) for a in planes for h in range(2)])

    def flip(array, bit):
        return lax.ppermute(array, "blk", [(i, i ^ bit) for i in range(4)])

    outer_to_inner = links([(0, 1), (3, 2)])
    inner_to_inner = links([(1, 2), (2, 1)])
    inner_to_outer = links([(1, 0), (2, 3)])
    every, inner_planes = (0, 1, 2, 3), (1, 2)

    def block(q, which):
        place = q // count
        chunk = jnp.where(side == 0, 3 - place, place)
        return (chunk * 2 + which) * count + q % count

    def mine(q):
        return block(q, half)

    def theirs(q):
        return block(q, 1 - half)

    near_inner = [2 * count + j for j in range(count)]
    near_outer = [3 * count + j for j in range(count)]
    steps = 3 * count - 1
    ahead = [s if s < 2 * count else s + 1 for s in range(steps)]
    main = [by_role(min(max(s - 2, 0), 2 * count - 1), ahead[s]) for s in range(steps)]
    own_chunk = [by_role(near_inner[j], near_outer[j]) for j in range(count)]
    double = steps - count
    first = jnp.int32(near_inner[0])

    inner_main, outer_main = [max(s - 2, 0) for s in range(steps)], ahead
    exchanges = [
        [(near_outer[0], outer_main[0])],
        [(near_outer[1], outer_main[1])],
        [(inner_main[2], outer_main[2]), (inner_main[3], outer_main[3])],
        [(inner_main[4], outer_main[4]), (inner_main[5], outer_main[5])],
        [
            (inner_main[6], outer_main[6]),
            (inner_main[7], outer_main[7]),
            (near_outer[2], near_outer[0]),
        ],
        [(near_inner[1], near_outer[1]), (near_inner[2], near_outer[2])],
    ]

    third, column = size // 3, theirs(first) * 3
    values, places = [inner], {}

    def put(name, value):
        places[name] = len(values)
        values.append(value)

    for s in range(steps):
        put(("main", s), mine(main[s]))
    for j in range(count):
        put(("out", j), mine(by_role(near_outer[j], ahead[double + j])))
        put(("own", j), mine(own_chunk[j]))
    for e, pairs in enumerate(exchanges):
        for k, pair in enumerate(pairs):
            put(("send", e, k), theirs(by_role(*pair)))
    put("first mine", mine(first))
    put("first theirs", theirs(first))
    put("first part", column + 1)
    put("second part", column + 2)
    table = jnp.stack(values)

    def columns_of(e):
        return [places["send", e, k] for k in range(len(exchanges[e]))]

    quarter, raw_0 = first_sends(jnp.stack([blk, column]), out_grads, inputs, pre_act, third)
    raw_1, send_0, raw_2, send_1 = cast_blocks(
        table,
        [
            (third, [places["first part"], places["second part"]]),
            (size, columns_of(0)),
            (size, [places["first mine"]]),
            (size, columns_of(1)),
        ],
        pre_act,
        [raw_0],
    )

    def send_in(array):
        return lax.ppermute(array, "dp", outer_to_inner)

    tied = lax.optimization_barrier
    pair_0 = swap(quarter, every)
    raw_0, raw_1, raw_2 = send_in(raw_0), send_in(raw_1), send_in(raw_2)
    quarter_in = send_in(quarter)
    got = [swap(send_0, every), swap(send_1, every)]
    pair_0, raw_0 = tied((pair_0, raw_0))
    pair_1, pair_2 = flip(pair_0, 1), flip(pair_0, 2)
    pair_2, pair_1, got[0], raw_1 = tied((pair_2, pair_1, got[0], raw_1))
    pair_3 = flip(pair_2, 1)
    g, x = join(blk, out_grads, inputs, [pair_0, pair_1, pair_2, pair_3], [got[0], raw_1])
    last = g

    def run(name, partner, **more):
        return piece(scale, table, places[name], pre_act, [partner[0]], partner[1], g, x, w_out, **more)

    toward, across = [], {}
    for s in range(steps):
        partner = (got[s], 0) if s < 2 else (got[1 + s // 2], s % 2)
        sends = columns_of(2 + s // 2) if s % 2 == 0 else []
        sums = [toward[s - 2]] if s >= 2 else []
        held_back = ([across[s - 4]] if s >= 4 else []) + ([first_in] if s == 3 else [])
        j = s - double
        if j < 0:
            after = [last] + held_back + ([raw_2] if s == 0 else [])
        else:
            (last,) = run(
                ("out", j),
                partner,
                sums=[across[j]],
                other=(got[j], 0) if j < 2 else (got[4], 2),
                after=[last] + sums + held_back,
            )
            toward.append(lax.ppermute(last, "dp", outer_to_inner + inner_to_outer))
            after = [last] + ([grad_inputs] if j == 0 else [])
        out, *blocks = run(
            ("main", s), partner, sums=sums, sends=sends, after=after, flops=FLOPS if s == 3 else 1
        )
        last = out
        if j < 0:
            toward.append(send_in(out))
        if blocks:
            got.append(swap(blocks[0], every))
        if s >= 2:
            across[s - 2] = lax.ppermute(out, "dp", inner_to_inner)
        if s == 0:
            out, quarter_in = tied((out, quarter_in))
            line_rows = lax.all_gather(quarter_in, "blk", tiled=True)
        if s == 1:
            last = input_partial(out_grads, pre_act, w_in, w_out, 4 * size, [last])
            grad_inputs = lax.psum_scatter(last, "blk", scatter_dimension=0, tiled=True)
            grad_inputs = grad_inputs.astype(jnp.bfloat16)
            line_g, line_x = join(blk, out_grads, inputs, [line_rows], [last])
            (last,) = piece(
                scale,
                table,
                places["first theirs"],
                pre_act,
                [raw_0, raw_1],
                0,
                line_g,
                line_x,
                w_out,
                after=[last],
            )
            first_in = swap(last, inner_planes)
        if s == 4:
            (held_in,) = piece(
                scale,
                table,
                places["first mine"],
                pre_act,
                [raw_2],
                0,
                line_g,
                line_x,
                w_out,
                sums=[first_in],
                after=[last],
            )
            last = held_in

    held = final_first(
        scale,
        count,
        table,
        places["own", 0],
        0,
        pre_act,
        got[4],
        2,
        g,
        x,
        w_out,
        held_in,
        toward[double],
        across[count],
        [last],
    )
    for i in range(1, count):
        (out,) = run(("own", i), (got[5], i - 1), sums=[across[count + i]], after=[held[0]])
        held = final_add(i, out, toward[double + i], held, [])
    return (grad_inputs, held[0], held[1])


def solution(mesh):
    def body(inputs, out_grads, pre_act, w_in, w_out):
        fits = pre_act.shape[1] % (8 * PIECES * 128) == 0 and inputs.shape[0] % 64 == 0
        run = line_body if (mesh.shape["dp"], mesh.shape["blk"]) == (8, 4) and fits else plain_body
        return run(inputs, out_grads, pre_act, w_in, w_out)

    return jax.shard_map(
        body,
        mesh=mesh,
        in_specs=(P("dp", None), P("dp", None), P("dp", "blk"), P("blk", None), P("blk", None)),
        out_specs=(P(("dp", "blk"), None), P(("blk", "dp"), None), P(("blk", "dp"), None)),
        check_vma=False,
    )
```

```python
import functools

import jax
import jax.numpy as jnp
from jax import lax
from jax.experimental import pallas as pl
from jax.experimental.pallas import tpu as pltpu
from jax.sharding import PartitionSpec as P

PIECES = 3
FLOPS = 100_000_000_000
VMEM_LIMIT = 63 * 1024 * 1024


def contract_rows(left, right):
    return lax.dot_general(
        left, right, (((0,), (0,)), ((), ())), preferred_element_type=jnp.float32
    )


def hidden_grads(out_grads, pre_act, w_out):
    back = lax.dot_general(
        out_grads, w_out, (((1,), (1,)), ((), ())), preferred_element_type=jnp.float32
    )
    return jnp.where(pre_act > 0, back, jnp.zeros_like(back)).astype(jnp.bfloat16)


def input_grads(grad_hidden, w_in):
    return lax.psum_scatter(
        jnp.dot(grad_hidden, w_in, preferred_element_type=jnp.float32),
        "blk",
        scatter_dimension=0,
        tiled=True,
    ).astype(jnp.bfloat16)


def plain_body(inputs, out_grads, pre_act, w_in, w_out):
    token_total = inputs.shape[0] * lax.axis_size("dp")
    factor = lax.rsqrt(jnp.asarray(token_total, jnp.float32))
    act = jnp.maximum(pre_act, jnp.zeros_like(pre_act))
    grad_hidden = hidden_grads(out_grads, pre_act, w_out)
    grad_out = contract_rows(act, out_grads) * factor
    grad_in = contract_rows(grad_hidden, inputs) * factor
    return (
        input_grads(grad_hidden, w_in),
        lax.psum_scatter(grad_in, "dp", scatter_dimension=0, tiled=True),
        lax.psum_scatter(grad_out, "dp", scatter_dimension=0, tiled=True),
    )


def params():
    return pltpu.CompilerParams(vmem_limit_bytes=VMEM_LIMIT)


def anywhere(arrays):
    return [pl.BlockSpec(memory_space=pl.ANY)] * len(arrays)


def cast_kernel(shapes, idx_ref, *refs):
    outs = refs[-len(shapes) :]
    for (_, count), out_ref in zip(shapes, outs):
        width = out_ref.shape[1] // count
        for k in range(count):
            out_ref[:, k * width : (k + 1) * width] = refs[k][...].astype(jnp.float32)
        refs = refs[count:]


def cast_blocks(table, groups, pre_act, after):
    rows = pre_act.shape[0]
    in_specs = [columns_spec(rows, width, at) for width, places in groups for at in places]
    shapes = [(width * len(places), len(places)) for width, places in groups]
    return pl.pallas_call(
        functools.partial(cast_kernel, shapes),
        grid_spec=pltpu.PrefetchScalarGridSpec(
            num_scalar_prefetch=1,
            grid=(1,),
            in_specs=in_specs + anywhere(after),
            out_specs=[pl.BlockSpec((rows, width), lambda i, idx: (0, 0)) for width, _ in shapes],
        ),
        out_shape=[jax.ShapeDtypeStruct((rows, width), jnp.float32) for width, _ in shapes],
        compiler_params=params(),
        cost_estimate=piece_cost(),
        name="cast_blocks",
    )(table, *([pre_act] * len(in_specs)), *after)


def first_kernel(blk_ref, column_ref, grads_ref, inputs_ref, pre_ref, quarter_ref, raw_ref):
    quarter = grads_ref.shape[0]
    quarter_ref[:quarter, :] = grads_ref[...].astype(jnp.float32)
    quarter_ref[quarter:, :] = inputs_ref[...].astype(jnp.float32)
    raw_ref[...] = pre_ref[...].astype(jnp.float32)


def first_sends(blk, column, out_grads, inputs, pre_act, size):
    rows, width = out_grads.shape
    quarter = rows // 4
    tokens = pl.BlockSpec((quarter, width), lambda i, blk, column: (blk[0], 0))
    return pl.pallas_call(
        first_kernel,
        grid_spec=pltpu.PrefetchScalarGridSpec(
            num_scalar_prefetch=2,
            grid=(1,),
            in_specs=[tokens, tokens, pl.BlockSpec((rows, size), lambda i, blk, column: (0, column[0]))],
            out_specs=[
                pl.BlockSpec((2 * quarter, width), lambda i, blk, column: (0, 0)),
                pl.BlockSpec((rows, size), lambda i, blk, column: (0, 0)),
            ],
        ),
        out_shape=[
            jax.ShapeDtypeStruct((2 * quarter, width), jnp.float32),
            jax.ShapeDtypeStruct((rows, size), jnp.float32),
        ],
        compiler_params=params(),
        cost_estimate=piece_cost(),
        name="first_sends",
    )(blk.reshape(1), column.reshape(1), out_grads, inputs, pre_act)


def join_kernel(grads_ref, inputs_ref, line_ref, *refs):
    g_ref, x_ref = refs[-2:]
    rows = grads_ref.shape[0]
    quarter = rows // 4
    g_ref[:rows, :] = grads_ref[...]
    x_ref[:rows, :] = inputs_ref[...]
    for k in range(4):
        place, start = pl.ds(rows + k * quarter, quarter), 2 * k * quarter
        g_ref[place, :] = line_ref[start : start + quarter, :].astype(jnp.bfloat16)
        x_ref[place, :] = line_ref[start + quarter : start + 2 * quarter, :].astype(jnp.bfloat16)


def join(out_grads, inputs, line_rows, after):
    rows, width = out_grads.shape
    shape = jax.ShapeDtypeStruct((2 * rows, width), jnp.bfloat16)
    vmem = pl.BlockSpec(memory_space=pltpu.VMEM)
    return pl.pallas_call(
        join_kernel,
        out_shape=(shape, shape),
        in_specs=[vmem] * 3 + anywhere(after),
        out_specs=(vmem, vmem),
        compiler_params=params(),
        cost_estimate=piece_cost(),
        name="join_tokens",
    )(out_grads, inputs, line_rows, *after)


def input_kernel(grads_ref, pre_ref, out_rows_ref, in_rows_ref, *refs):
    total_ref = refs[-1]

    @pl.when(pl.program_id(0) == 0)
    def _():
        total_ref[...] = jnp.zeros_like(total_ref)

    hidden = hidden_grads(grads_ref[...], pre_ref[...], out_rows_ref[...])
    total_ref[...] += jnp.dot(hidden, in_rows_ref[...], preferred_element_type=jnp.float32)


def input_partial(out_grads, pre_act, w_in, w_out, size, after):
    rows, hidden = pre_act.shape
    width = out_grads.shape[1]
    tokens = pl.BlockSpec((rows, width), lambda i: (0, 0))
    weights = pl.BlockSpec((size, width), lambda i: (i, 0))
    return pl.pallas_call(
        input_kernel,
        grid=(hidden // size,),
        in_specs=[tokens, pl.BlockSpec((rows, size), lambda i: (0, i)), weights, weights] + anywhere(after),
        out_specs=tokens,
        out_shape=jax.ShapeDtypeStruct((rows, width), jnp.float32),
        compiler_params=params(),
        cost_estimate=piece_cost(FLOPS),
        name="input_partial",
    )(out_grads, pre_act, w_out, w_in, *after)


def piece_math(scale, own, partner, g, x, w):
    pre = jnp.concatenate([own, partner.astype(jnp.bfloat16)], axis=0)
    hidden = hidden_grads(g, pre, w)
    act = jnp.maximum(pre, jnp.zeros_like(pre))
    return contract_rows(hidden, x) * scale, contract_rows(act, g) * scale


def piece_kernel(scale, counts, inner_at, table_ref, own_ref, g_ref, x_ref, w_ref, *refs):
    groups = []
    for n in counts:
        groups.append(refs[:n])
        refs = refs[n:]
    partners, others, columns, sums, _, (out_ref, *sends) = groups + [refs]
    partner = jnp.concatenate([ref[...] for ref in partners], axis=1)
    for ref in others:
        partner = jnp.where(table_ref[inner_at] > 0, ref[...], partner)
    grad_in, grad_out = piece_math(scale, own_ref[...], partner, g_ref[...], x_ref[...], w_ref[...])
    for ref in sums:
        grad_in = grad_in + ref[0]
        grad_out = grad_out + ref[1]
    out_ref[0], out_ref[1] = grad_in, grad_out
    rows = own_ref.shape[0]
    for ref in sends:
        for k, column_ref in enumerate(columns):
            ref[k * rows : (k + 1) * rows, :] = column_ref[...].astype(jnp.float32)


def columns_spec(rows, size, at):
    return pl.BlockSpec((rows, size), lambda i, table: (0, table[at]))


def piece_specs(rows, size, width, at):
    tokens = pl.BlockSpec((2 * rows, width), lambda i, table: (0, 0))
    return [
        columns_spec(rows, size, at),
        tokens,
        tokens,
        pl.BlockSpec((size, width), lambda i, table: (table[at], 0)),
    ]


def partner_spec(rows, size, place):
    return pl.BlockSpec((rows, size), lambda i, table: (place, 0))


def piece_cost(flops=1):
    return pl.CostEstimate(flops=flops, bytes_accessed=1, transcendentals=0)


def piece(
    scale, table, at, pre_act, partners, place, g, x, w_out, sums=(), other=None, inner_at=0, sends=(), after=(), flops=1
):
    rows, width = pre_act.shape[0], g.shape[1]
    size = sum(p.shape[1] for p in partners)
    whole = pl.BlockSpec((2, size, width), lambda i, table: (0, 0, 0))
    others, other_specs = [], []
    if other is not None:
        others = [other[0]]
        other_specs = [partner_spec(rows, size, other[1])]
    counts = (len(partners), len(others), len(sends), len(sums), len(after))
    sent = [(len(sends) * rows, size)] if sends else []
    return pl.pallas_call(
        functools.partial(piece_kernel, scale, counts, inner_at),
        grid_spec=pltpu.PrefetchScalarGridSpec(
            num_scalar_prefetch=1,
            grid=(1,),
            in_specs=piece_specs(rows, size, width, at)
            + [partner_spec(rows, p.shape[1], place) for p in partners]
            + other_specs
            + [columns_spec(rows, size, k) for k in sends]
            + [whole] * len(sums)
            + anywhere(after),
            out_specs=[whole] + [pl.BlockSpec(shape, lambda i, table: (0, 0)) for shape in sent],
        ),
        out_shape=[jax.ShapeDtypeStruct(shape, jnp.float32) for shape in [(2, size, width)] + sent],
        compiler_params=params(),
        cost_estimate=piece_cost(flops),
        name="piece",
    )(table, pre_act, g, x, w_out, *partners, *others, *([pre_act] * len(sends)), *sums, *after)


def first_piece_kernel(
    scale, blk_at, table_ref, own_ref, w_ref, partner_ref, grads_ref, inputs_ref, q0_ref, q1_ref, q2_ref, q3_ref, a_ref, b_ref, *refs
):
    out_ref, g_ref, x_ref, send_ref = refs[-4:]
    rows = grads_ref.shape[0]
    quarter = rows // 4
    g_ref[:rows, :] = grads_ref[...]
    x_ref[:rows, :] = inputs_ref[...]
    for k, ref in enumerate((q0_ref, q1_ref, q2_ref, q3_ref)):
        where = jnp.bitwise_xor(table_ref[blk_at], k)
        place = pl.ds(pl.multiple_of(rows + where * quarter, quarter), quarter)
        g_ref[place, :] = ref[:quarter, :].astype(jnp.bfloat16)
        x_ref[place, :] = ref[quarter:, :].astype(jnp.bfloat16)
    out_ref[0], out_ref[1] = piece_math(
        scale, own_ref[...], partner_ref[...], g_ref[...], x_ref[...], w_ref[...]
    )
    send_ref[:rows, :] = a_ref[...].astype(jnp.float32)
    send_ref[rows:, :] = b_ref[...].astype(jnp.float32)


def first_piece(scale, table, at, blk_at, pre_act, partner, out_grads, inputs, quarters, w_out, sends, after):
    rows, width = out_grads.shape
    size = partner.shape[1]
    whole = lambda *shape: pl.BlockSpec(shape, lambda i, table: (0,) * len(shape))
    tokens = jax.ShapeDtypeStruct((2 * rows, width), jnp.bfloat16)
    return pl.pallas_call(
        functools.partial(first_piece_kernel, scale, blk_at),
        grid_spec=pltpu.PrefetchScalarGridSpec(
            num_scalar_prefetch=1,
            grid=(1,),
            in_specs=[
                columns_spec(rows, size, at),
                pl.BlockSpec((size, width), lambda i, table: (table[at], 0)),
                whole(rows, size),
                whole(rows, width),
                whole(rows, width),
            ]
            + [whole(rows // 2, width)] * 4
            + [columns_spec(rows, size, k) for k in sends]
            + anywhere(after),
            out_specs=[
                whole(2, size, width),
                whole(2 * rows, width),
                whole(2 * rows, width),
                whole(2 * rows, size),
            ],
        ),
        out_shape=[
            jax.ShapeDtypeStruct((2, size, width), jnp.float32),
            tokens,
            tokens,
            jax.ShapeDtypeStruct((2 * rows, size), jnp.float32),
        ],
        compiler_params=params(),
        cost_estimate=piece_cost(),
        name="first_piece",
    )(table, pre_act, w_out, partner, out_grads, inputs, *quarters, pre_act, pre_act, *after)


def final_kernel(scale, inner_at, table_ref, own_ref, g_ref, x_ref, w_ref, partner_ref, inner_ref, outer_ref, *refs):
    sum_ref, (in_ref, out_ref) = refs[0], refs[-2:]
    grad_in, grad_out = piece_math(
        scale, own_ref[...], partner_ref[...], g_ref[...], x_ref[...], w_ref[...]
    )
    is_inner = table_ref[inner_at] > 0
    in_ref[...] = jnp.where(is_inner, inner_ref[0], grad_in + outer_ref[0]) + sum_ref[0]
    out_ref[...] = jnp.where(is_inner, inner_ref[1], grad_out + outer_ref[1]) + sum_ref[1]


def final_first(
    scale, count, table, at, inner_at, pre_act, partner, place, g, x, w_out, held, received, added, after
):
    rows, size, width = pre_act.shape[0], partner.shape[1], g.shape[1]
    whole = pl.BlockSpec((2, size, width), lambda i, table: (0, 0, 0))
    shape = jax.ShapeDtypeStruct((count * size, width), jnp.float32)
    return pl.pallas_call(
        functools.partial(final_kernel, scale, inner_at),
        grid_spec=pltpu.PrefetchScalarGridSpec(
            num_scalar_prefetch=1,
            grid=(1,),
            in_specs=piece_specs(rows, size, width, at)
            + [partner_spec(rows, size, place)]
            + [whole] * 3
            + anywhere(after),
            out_specs=[pl.BlockSpec((size, width), lambda i, table: (0, 0))] * 2,
        ),
        out_shape=(shape, shape),
        compiler_params=params(),
        cost_estimate=piece_cost(),
        name="final_first",
    )(table, pre_act, g, x, w_out, partner, held, received, added, *after)


def add_kernel(a_ref, b_ref, *refs):
    in_ref, out_ref = refs[-2:]
    in_ref[...] = a_ref[0] + b_ref[0]
    out_ref[...] = a_ref[1] + b_ref[1]


def final_add(place, a, b, held, after):
    _, size, width = a.shape
    steps = 2
    block = pl.BlockSpec((2, size // steps, width), lambda i: (0, i, 0))
    return pl.pallas_call(
        add_kernel,
        grid=(steps,),
        in_specs=[block, block] + anywhere(held) + anywhere(after),
        out_specs=[pl.BlockSpec((size // steps, width), lambda i: (place * steps + i, 0))] * 2,
        out_shape=[jax.ShapeDtypeStruct(h.shape, h.dtype) for h in held],
        input_output_aliases={2: 0, 3: 1},
        compiler_params=params(),
        name="final_add",
    )(a, b, *held, *after)


def line_body(inputs, out_grads, pre_act, w_in, w_out):
    count = PIECES
    rows, hidden = pre_act.shape
    size = hidden // (8 * count)
    scale = 1.0 / (rows * lax.axis_size("dp")) ** 0.5
    me, blk = lax.axis_index("dp"), lax.axis_index("blk")
    plane, half = me // 2, me % 2
    side = plane // 2
    inner = jnp.where((plane == 1) | (plane == 2), 1, 0).astype(jnp.int32)

    def by_role(on_inner, on_outer):
        return jnp.where(inner > 0, jnp.int32(on_inner), jnp.int32(on_outer))

    def links(pairs):
        return [(2 * a + h, 2 * b + h) for a, b in pairs for h in range(2)]

    def swap(array, planes):
        return lax.ppermute(array, "dp", [(2 * a + h, 2 * a + 1 - h) for a in planes for h in range(2)])

    def flip(array, bit):
        return lax.ppermute(array, "blk", [(i, i ^ bit) for i in range(4)])

    outer_to_inner = links([(0, 1), (3, 2)])
    inner_to_inner = links([(1, 2), (2, 1)])
    inner_to_outer = links([(1, 0), (2, 3)])
    every, inner_planes = (0, 1, 2, 3), (1, 2)

    def block(q, which):
        place = q // count
        chunk = jnp.where(side == 0, 3 - place, place)
        return (chunk * 2 + which) * count + q % count

    def mine(q):
        return block(q, half)

    def theirs(q):
        return block(q, 1 - half)

    near_inner = [2 * count + j for j in range(count)]
    near_outer = [3 * count + j for j in range(count)]
    steps = 3 * count - 1
    ahead = [s if s < 2 * count else s + 1 for s in range(steps)]
    main = [by_role(min(max(s - 2, 0), 2 * count - 1), ahead[s]) for s in range(steps)]
    own_chunk = [by_role(near_inner[j], near_outer[j]) for j in range(count)]
    double = steps - count
    first = jnp.int32(near_inner[0])

    inner_main, outer_main = [max(s - 2, 0) for s in range(steps)], ahead
    exchanges = [
        [(near_outer[0], outer_main[0])],
        [(near_outer[1], outer_main[1])],
        [(inner_main[2], outer_main[2]), (inner_main[3], outer_main[3])],
        [(inner_main[4], outer_main[4]), (inner_main[5], outer_main[5])],
        [
            (inner_main[6], outer_main[6]),
            (inner_main[7], outer_main[7]),
            (near_outer[2], near_outer[0]),
        ],
        [(near_inner[1], near_outer[1]), (near_inner[2], near_outer[2])],
    ]

    third, column = size // 3, theirs(first) * 3
    values, places = [inner], {}

    def put(name, value):
        places[name] = len(values)
        values.append(value)

    for s in range(steps):
        put(("main", s), mine(main[s]))
    for j in range(count):
        put(("out", j), mine(by_role(near_outer[j], ahead[double + j])))
        put(("own", j), mine(own_chunk[j]))
    for e, pairs in enumerate(exchanges):
        for k, pair in enumerate(pairs):
            put(("send", e, k), theirs(by_role(*pair)))
    put("blk", blk.astype(jnp.int32))
    put("first mine", mine(first))
    put("first theirs", theirs(first))
    put("first part", column + 1)
    put("second part", column + 2)
    table = jnp.stack(values)

    def columns_of(e):
        return [places["send", e, k] for k in range(len(exchanges[e]))]

    quarter, raw_0 = first_sends(blk, column, out_grads, inputs, pre_act, third)
    raw_1, send_0, raw_2, send_1 = cast_blocks(
        table,
        [
            (third, [places["first part"], places["second part"]]),
            (size, columns_of(0)),
            (size, [places["first mine"]]),
            (size, columns_of(1)),
        ],
        pre_act,
        [raw_0],
    )

    def send_in(array):
        return lax.ppermute(array, "dp", outer_to_inner)

    tied = lax.optimization_barrier
    pair_0 = swap(quarter, every)
    raw_0, raw_1, raw_2 = send_in(raw_0), send_in(raw_1), send_in(raw_2)
    quarter_in = send_in(quarter)
    got = [swap(send_0, every), swap(send_1, every)]
    pair_0, raw_0 = tied((pair_0, raw_0))
    pair_1, pair_2 = flip(pair_0, 1), flip(pair_0, 2)
    pair_2, pair_1, got[0], raw_1 = tied((pair_2, pair_1, got[0], raw_1))
    pair_3 = flip(pair_2, 1)
    def run(name, partner, **more):
        return piece(scale, table, places[name], pre_act, [partner[0]], partner[1], g, x, w_out, **more)

    toward, across = [], {}
    for s in range(steps):
        partner = (got[s], 0) if s < 2 else (got[1 + s // 2], s % 2)
        sends = columns_of(2 + s // 2) if s % 2 == 0 else []
        sums = [toward[s - 2]] if s >= 2 else []
        held_back = ([across[s - 4]] if s >= 4 else []) + ([first_in] if s == 3 else [])
        j = s - double
        if s == 0:
            out, g, x, *blocks = first_piece(
                scale,
                table,
                places["main", 0],
                places["blk"],
                pre_act,
                got[0],
                out_grads,
                inputs,
                [pair_0, pair_1, pair_2, pair_3],
                w_out,
                sends,
                [raw_2],
            )
        else:
            after = [last] + held_back
            if j >= 0:
                (last,) = run(
                    ("out", j),
                    partner,
                    sums=[across[j]],
                    other=(got[j], 0) if j < 2 else (got[4], 2),
                    after=after + sums,
                )
                toward.append(lax.ppermute(last, "dp", outer_to_inner + inner_to_outer))
                after = [last] + ([grad_inputs] if j == 0 else [])
            out, *blocks = run(
                ("main", s), partner, sums=sums, sends=sends, after=after, flops=FLOPS if s == 3 else 1
            )
        last = out
        if j < 0:
            toward.append(send_in(out))
        if blocks:
            got.append(swap(blocks[0], every))
        if s >= 2:
            across[s - 2] = lax.ppermute(out, "dp", inner_to_inner)
        if s == 0:
            out, quarter_in = tied((out, quarter_in))
            line_rows = lax.all_gather(quarter_in, "blk", tiled=True)
        if s == 1:
            last = input_partial(out_grads, pre_act, w_in, w_out, 4 * size, [last])
            grad_inputs = lax.psum_scatter(last, "blk", scatter_dimension=0, tiled=True)
            grad_inputs = grad_inputs.astype(jnp.bfloat16)
            line_g, line_x = join(out_grads, inputs, line_rows, [last])
            (last,) = piece(
                scale,
                table,
                places["first theirs"],
                pre_act,
                [raw_0, raw_1],
                0,
                line_g,
                line_x,
                w_out,
                after=[last],
            )
            first_in = swap(last, inner_planes)
        if s == 4:
            (held_in,) = piece(
                scale,
                table,
                places["first mine"],
                pre_act,
                [raw_2],
                0,
                line_g,
                line_x,
                w_out,
                sums=[first_in],
                after=[last],
            )
            last = held_in

    held = final_first(
        scale,
        count,
        table,
        places["own", 0],
        0,
        pre_act,
        got[4],
        2,
        g,
        x,
        w_out,
        held_in,
        toward[double],
        across[count],
        [last],
    )
    for i in range(1, count):
        (out,) = run(("own", i), (got[5], i - 1), sums=[across[count + i]], after=[held[0]])
        held = final_add(i, out, toward[double + i], held, [])
    return (grad_inputs, held[0], held[1])


def solution(mesh):
    def body(inputs, out_grads, pre_act, w_in, w_out):
        fits = pre_act.shape[1] % (8 * PIECES * 128) == 0 and inputs.shape[0] % 64 == 0
        run = line_body if (mesh.shape["dp"], mesh.shape["blk"]) == (8, 4) and fits else plain_body
        return run(inputs, out_grads, pre_act, w_in, w_out)

    return jax.shard_map(
        body,
        mesh=mesh,
        in_specs=(P("dp", None), P("dp", None), P("dp", "blk"), P("blk", None), P("blk", None)),
        out_specs=(P(("dp", "blk"), None), P(("blk", "dp"), None), P(("blk", "dp"), None)),
        check_vma=False,
    )
```

```python
import functools

import jax
import jax.numpy as jnp
from jax import lax
from jax.experimental import pallas as pl
from jax.experimental.pallas import tpu as pltpu
from jax.sharding import PartitionSpec as P

PIECES = 3
FLOPS = 100_000_000_000
VMEM_LIMIT = 63 * 1024 * 1024


def contract_rows(left, right):
    return lax.dot_general(
        left, right, (((0,), (0,)), ((), ())), preferred_element_type=jnp.float32
    )


def hidden_grads(out_grads, pre_act, w_out):
    back = lax.dot_general(
        out_grads, w_out, (((1,), (1,)), ((), ())), preferred_element_type=jnp.float32
    )
    return jnp.where(pre_act > 0, back, jnp.zeros_like(back)).astype(jnp.bfloat16)


def input_grads(grad_hidden, w_in):
    return lax.psum_scatter(
        jnp.dot(grad_hidden, w_in, preferred_element_type=jnp.float32),
        "blk",
        scatter_dimension=0,
        tiled=True,
    ).astype(jnp.bfloat16)


def plain_body(inputs, out_grads, pre_act, w_in, w_out):
    token_total = inputs.shape[0] * lax.axis_size("dp")
    factor = lax.rsqrt(jnp.asarray(token_total, jnp.float32))
    act = jnp.maximum(pre_act, jnp.zeros_like(pre_act))
    grad_hidden = hidden_grads(out_grads, pre_act, w_out)
    grad_out = contract_rows(act, out_grads) * factor
    grad_in = contract_rows(grad_hidden, inputs) * factor
    return (
        input_grads(grad_hidden, w_in),
        lax.psum_scatter(grad_in, "dp", scatter_dimension=0, tiled=True),
        lax.psum_scatter(grad_out, "dp", scatter_dimension=0, tiled=True),
    )


def params():
    return pltpu.CompilerParams(vmem_limit_bytes=VMEM_LIMIT)


def anywhere(arrays):
    return [pl.BlockSpec(memory_space=pl.ANY)] * len(arrays)


def cast_kernel(shapes, idx_ref, *refs):
    outs = refs[-len(shapes) :]
    for (_, count), out_ref in zip(shapes, outs):
        width = out_ref.shape[1] // count
        for k in range(count):
            out_ref[:, k * width : (k + 1) * width] = refs[k][...].astype(jnp.float32)
        refs = refs[count:]


def cast_blocks(table, groups, pre_act, after):
    rows = pre_act.shape[0]
    in_specs = [columns_spec(rows, width, at) for width, places in groups for at in places]
    shapes = [(width * len(places), len(places)) for width, places in groups]
    return pl.pallas_call(
        functools.partial(cast_kernel, shapes),
        grid_spec=pltpu.PrefetchScalarGridSpec(
            num_scalar_prefetch=1,
            grid=(1,),
            in_specs=in_specs + anywhere(after),
            out_specs=[pl.BlockSpec((rows, width), lambda i, idx: (0, 0)) for width, _ in shapes],
        ),
        out_shape=[jax.ShapeDtypeStruct((rows, width), jnp.float32) for width, _ in shapes],
        compiler_params=params(),
        cost_estimate=piece_cost(),
        name="cast_blocks",
    )(table, *([pre_act] * len(in_specs)), *after)


def first_kernel(blk_ref, column_ref, grads_ref, inputs_ref, pre_ref, quarter_ref, raw_ref):
    quarter = grads_ref.shape[0]
    quarter_ref[:quarter, :] = grads_ref[...].astype(jnp.float32)
    quarter_ref[quarter:, :] = inputs_ref[...].astype(jnp.float32)
    raw_ref[...] = pre_ref[...].astype(jnp.float32)


def first_sends(blk, column, out_grads, inputs, pre_act, size):
    rows, width = out_grads.shape
    quarter = rows // 4
    tokens = pl.BlockSpec((quarter, width), lambda i, blk, column: (blk[0], 0))
    return pl.pallas_call(
        first_kernel,
        grid_spec=pltpu.PrefetchScalarGridSpec(
            num_scalar_prefetch=2,
            grid=(1,),
            in_specs=[tokens, tokens, pl.BlockSpec((rows, size), lambda i, blk, column: (0, column[0]))],
            out_specs=[
                pl.BlockSpec((2 * quarter, width), lambda i, blk, column: (0, 0)),
                pl.BlockSpec((rows, size), lambda i, blk, column: (0, 0)),
            ],
        ),
        out_shape=[
            jax.ShapeDtypeStruct((2 * quarter, width), jnp.float32),
            jax.ShapeDtypeStruct((rows, size), jnp.float32),
        ],
        compiler_params=params(),
        cost_estimate=piece_cost(),
        name="first_sends",
    )(blk.reshape(1), column.reshape(1), out_grads, inputs, pre_act)


def fill_tokens(blk, grads_ref, inputs_ref, quarters, g_ref, x_ref):
    rows = grads_ref.shape[0]
    quarter = rows // 4
    g_ref[:rows, :] = grads_ref[...]
    x_ref[:rows, :] = inputs_ref[...]
    for k, ref in enumerate(quarters):
        where = jnp.bitwise_xor(blk, k)
        place = pl.ds(pl.multiple_of(rows + where * quarter, quarter), quarter)
        g_ref[place, :] = ref[:quarter, :].astype(jnp.bfloat16)
        x_ref[place, :] = ref[quarter:, :].astype(jnp.bfloat16)


def join_kernel(blk_ref, grads_ref, inputs_ref, *refs):
    fill_tokens(blk_ref[0], grads_ref, inputs_ref, refs[:4], *refs[-2:])


def join(blk, out_grads, inputs, quarters, after):
    rows, width = out_grads.shape
    shape = jax.ShapeDtypeStruct((2 * rows, width), jnp.bfloat16)
    vmem = pl.BlockSpec(memory_space=pltpu.VMEM)
    return pl.pallas_call(
        join_kernel,
        out_shape=(shape, shape),
        in_specs=[pl.BlockSpec(memory_space=pltpu.SMEM)] + [vmem] * 6 + anywhere(after),
        out_specs=(vmem, vmem),
        compiler_params=params(),
        cost_estimate=piece_cost(),
        name="join_tokens",
    )(blk.reshape(1), out_grads, inputs, *quarters, *after)


def input_kernel(blk_ref, grads_ref, pre_ref, out_rows_ref, in_rows_ref, *refs):
    keep_ref, give_ref, total_ref = refs[-3:]

    @pl.when(pl.program_id(0) == 0)
    def _():
        total_ref[...] = jnp.zeros_like(total_ref)

    hidden = hidden_grads(grads_ref[...], pre_ref[...], out_rows_ref[...])
    total_ref[...] += jnp.dot(hidden, in_rows_ref[...], preferred_element_type=jnp.float32)

    @pl.when(pl.program_id(0) == pl.num_programs(0) - 1)
    def _():
        half = keep_ref.shape[0]
        x = blk_ref[0] // 2
        keep_ref[...] = total_ref[pl.ds(pl.multiple_of(x * half, half), half), :]
        give_ref[...] = total_ref[pl.ds(pl.multiple_of((1 - x) * half, half), half), :]


def input_partial(blk, out_grads, pre_act, w_in, w_out, size, after):
    rows, hidden = pre_act.shape
    width = out_grads.shape[1]
    tokens = pl.BlockSpec((rows, width), lambda i, blk: (0, 0))
    weights = pl.BlockSpec((size, width), lambda i, blk: (i, 0))
    half = jax.ShapeDtypeStruct((rows // 2, width), jnp.float32)
    return pl.pallas_call(
        input_kernel,
        grid_spec=pltpu.PrefetchScalarGridSpec(
            num_scalar_prefetch=1,
            grid=(hidden // size,),
            in_specs=[tokens, pl.BlockSpec((rows, size), lambda i, blk: (0, i)), weights, weights]
            + anywhere(after),
            out_specs=[pl.BlockSpec(half.shape, lambda i, blk: (0, 0))] * 2,
            scratch_shapes=[pltpu.VMEM((rows, width), jnp.float32)],
        ),
        out_shape=[half, half],
        compiler_params=params(),
        cost_estimate=piece_cost(FLOPS),
        name="input_partial",
    )(blk.reshape(1), out_grads, pre_act, w_out, w_in, *after)


def fold_kernel(blk_ref, kept_ref, got_ref, *refs):
    keep_ref, give_ref = refs[-2:]
    rows = keep_ref.shape[0]
    core = blk_ref[0] % 2
    for ref, place in ((keep_ref, core), (give_ref, 1 - core)):
        part = pl.ds(pl.multiple_of(place * rows, rows), rows)
        ref[...] = kept_ref[part, :] + got_ref[part, :]


def fold(blk, kept, got, after):
    rows, width = kept.shape
    half = jax.ShapeDtypeStruct((rows // 2, width), jnp.float32)
    vmem = pl.BlockSpec(memory_space=pltpu.VMEM)
    return pl.pallas_call(
        fold_kernel,
        out_shape=(half, half),
        in_specs=[pl.BlockSpec(memory_space=pltpu.SMEM), vmem, vmem] + anywhere(after),
        out_specs=(vmem, vmem),
        compiler_params=params(),
        cost_estimate=piece_cost(),
        name="fold_rows",
    )(blk.reshape(1), kept, got, *after)


def round_kernel(kept_ref, got_ref, *refs):
    refs[-1][...] = (kept_ref[...] + got_ref[...]).astype(jnp.bfloat16)


def round_sum(kept, got, after):
    vmem = pl.BlockSpec(memory_space=pltpu.VMEM)
    return pl.pallas_call(
        round_kernel,
        out_shape=jax.ShapeDtypeStruct(kept.shape, jnp.bfloat16),
        in_specs=[vmem, vmem] + anywhere(after),
        out_specs=vmem,
        compiler_params=params(),
        cost_estimate=piece_cost(),
        name="round_sum",
    )(kept, got, *after)


def piece_math(scale, own, partner, g, x, w):
    pre = jnp.concatenate([own, partner.astype(jnp.bfloat16)], axis=0)
    hidden = hidden_grads(g, pre, w)
    act = jnp.maximum(pre, jnp.zeros_like(pre))
    return contract_rows(hidden, x) * scale, contract_rows(act, g) * scale


def piece_kernel(scale, counts, inner_at, table_ref, own_ref, g_ref, x_ref, w_ref, *refs):
    groups = []
    for n in counts:
        groups.append(refs[:n])
        refs = refs[n:]
    partners, others, columns, sums, _, (out_ref, *sends) = groups + [refs]
    partner = jnp.concatenate([ref[...] for ref in partners], axis=1)
    for ref in others:
        partner = jnp.where(table_ref[inner_at] > 0, ref[...], partner)
    grad_in, grad_out = piece_math(scale, own_ref[...], partner, g_ref[...], x_ref[...], w_ref[...])
    for ref in sums:
        grad_in = grad_in + ref[0]
        grad_out = grad_out + ref[1]
    out_ref[0], out_ref[1] = grad_in, grad_out
    rows = own_ref.shape[0]
    for ref in sends:
        for k, column_ref in enumerate(columns):
            ref[k * rows : (k + 1) * rows, :] = column_ref[...].astype(jnp.float32)


def columns_spec(rows, size, at):
    return pl.BlockSpec((rows, size), lambda i, table: (0, table[at]))


def piece_specs(rows, size, width, at):
    tokens = pl.BlockSpec((2 * rows, width), lambda i, table: (0, 0))
    return [
        columns_spec(rows, size, at),
        tokens,
        tokens,
        pl.BlockSpec((size, width), lambda i, table: (table[at], 0)),
    ]


def partner_spec(rows, size, place):
    return pl.BlockSpec((rows, size), lambda i, table: (place, 0))


def piece_cost(flops=1):
    return pl.CostEstimate(flops=flops, bytes_accessed=1, transcendentals=0)


def piece(
    scale, table, at, pre_act, partners, place, g, x, w_out, sums=(), other=None, inner_at=0, sends=(), after=(), flops=1
):
    rows, width = pre_act.shape[0], g.shape[1]
    size = sum(p.shape[1] for p in partners)
    whole = pl.BlockSpec((2, size, width), lambda i, table: (0, 0, 0))
    others, other_specs = [], []
    if other is not None:
        others = [other[0]]
        other_specs = [partner_spec(rows, size, other[1])]
    counts = (len(partners), len(others), len(sends), len(sums), len(after))
    sent = [(len(sends) * rows, size)] if sends else []
    return pl.pallas_call(
        functools.partial(piece_kernel, scale, counts, inner_at),
        grid_spec=pltpu.PrefetchScalarGridSpec(
            num_scalar_prefetch=1,
            grid=(1,),
            in_specs=piece_specs(rows, size, width, at)
            + [partner_spec(rows, p.shape[1], place) for p in partners]
            + other_specs
            + [columns_spec(rows, size, k) for k in sends]
            + [whole] * len(sums)
            + anywhere(after),
            out_specs=[whole] + [pl.BlockSpec(shape, lambda i, table: (0, 0)) for shape in sent],
        ),
        out_shape=[jax.ShapeDtypeStruct(shape, jnp.float32) for shape in [(2, size, width)] + sent],
        compiler_params=params(),
        cost_estimate=piece_cost(flops),
        name="piece",
    )(table, pre_act, g, x, w_out, *partners, *others, *([pre_act] * len(sends)), *sums, *after)


def first_piece_kernel(
    scale, blk_at, table_ref, own_ref, w_ref, partner_ref, grads_ref, inputs_ref, q0_ref, q1_ref, q2_ref, q3_ref, a_ref, b_ref, *refs
):
    out_ref, g_ref, x_ref, send_ref = refs[-4:]
    rows = grads_ref.shape[0]
    quarters = (q0_ref, q1_ref, q2_ref, q3_ref)
    fill_tokens(table_ref[blk_at], grads_ref, inputs_ref, quarters, g_ref, x_ref)
    out_ref[0], out_ref[1] = piece_math(
        scale, own_ref[...], partner_ref[...], g_ref[...], x_ref[...], w_ref[...]
    )
    send_ref[:rows, :] = a_ref[...].astype(jnp.float32)
    send_ref[rows:, :] = b_ref[...].astype(jnp.float32)


def first_piece(scale, table, at, blk_at, pre_act, partner, out_grads, inputs, quarters, w_out, sends, after):
    rows, width = out_grads.shape
    size = partner.shape[1]
    whole = lambda *shape: pl.BlockSpec(shape, lambda i, table: (0,) * len(shape))
    tokens = jax.ShapeDtypeStruct((2 * rows, width), jnp.bfloat16)
    return pl.pallas_call(
        functools.partial(first_piece_kernel, scale, blk_at),
        grid_spec=pltpu.PrefetchScalarGridSpec(
            num_scalar_prefetch=1,
            grid=(1,),
            in_specs=[
                columns_spec(rows, size, at),
                pl.BlockSpec((size, width), lambda i, table: (table[at], 0)),
                whole(rows, size),
                whole(rows, width),
                whole(rows, width),
            ]
            + [whole(rows // 2, width)] * 4
            + [columns_spec(rows, size, k) for k in sends]
            + anywhere(after),
            out_specs=[
                whole(2, size, width),
                whole(2 * rows, width),
                whole(2 * rows, width),
                whole(2 * rows, size),
            ],
        ),
        out_shape=[
            jax.ShapeDtypeStruct((2, size, width), jnp.float32),
            tokens,
            tokens,
            jax.ShapeDtypeStruct((2 * rows, size), jnp.float32),
        ],
        compiler_params=params(),
        cost_estimate=piece_cost(),
        name="first_piece",
    )(table, pre_act, w_out, partner, out_grads, inputs, *quarters, pre_act, pre_act, *after)


def final_kernel(scale, inner_at, table_ref, own_ref, g_ref, x_ref, w_ref, partner_ref, inner_ref, outer_ref, *refs):
    sum_ref, (in_ref, out_ref) = refs[0], refs[-2:]
    grad_in, grad_out = piece_math(
        scale, own_ref[...], partner_ref[...], g_ref[...], x_ref[...], w_ref[...]
    )
    is_inner = table_ref[inner_at] > 0
    in_ref[...] = jnp.where(is_inner, inner_ref[0], grad_in + outer_ref[0]) + sum_ref[0]
    out_ref[...] = jnp.where(is_inner, inner_ref[1], grad_out + outer_ref[1]) + sum_ref[1]


def final_first(
    scale, count, table, at, inner_at, pre_act, partner, place, g, x, w_out, held, received, added, after
):
    rows, size, width = pre_act.shape[0], partner.shape[1], g.shape[1]
    whole = pl.BlockSpec((2, size, width), lambda i, table: (0, 0, 0))
    shape = jax.ShapeDtypeStruct((count * size, width), jnp.float32)
    return pl.pallas_call(
        functools.partial(final_kernel, scale, inner_at),
        grid_spec=pltpu.PrefetchScalarGridSpec(
            num_scalar_prefetch=1,
            grid=(1,),
            in_specs=piece_specs(rows, size, width, at)
            + [partner_spec(rows, size, place)]
            + [whole] * 3
            + anywhere(after),
            out_specs=[pl.BlockSpec((size, width), lambda i, table: (0, 0))] * 2,
        ),
        out_shape=(shape, shape),
        compiler_params=params(),
        cost_estimate=piece_cost(),
        name="final_first",
    )(table, pre_act, g, x, w_out, partner, held, received, added, *after)


def add_kernel(a_ref, b_ref, *refs):
    in_ref, out_ref = refs[-2:]
    in_ref[...] = a_ref[0] + b_ref[0]
    out_ref[...] = a_ref[1] + b_ref[1]


def final_add(place, a, b, held, after):
    _, size, width = a.shape
    steps = 2
    block = pl.BlockSpec((2, size // steps, width), lambda i: (0, i, 0))
    return pl.pallas_call(
        add_kernel,
        grid=(steps,),
        in_specs=[block, block] + anywhere(held) + anywhere(after),
        out_specs=[pl.BlockSpec((size // steps, width), lambda i: (place * steps + i, 0))] * 2,
        out_shape=[jax.ShapeDtypeStruct(h.shape, h.dtype) for h in held],
        input_output_aliases={2: 0, 3: 1},
        compiler_params=params(),
        name="final_add",
    )(a, b, *held, *after)


def line_body(inputs, out_grads, pre_act, w_in, w_out):
    count = PIECES
    rows, hidden = pre_act.shape
    size = hidden // (8 * count)
    scale = 1.0 / (rows * lax.axis_size("dp")) ** 0.5
    me, blk = lax.axis_index("dp"), lax.axis_index("blk")
    plane, half = me // 2, me % 2
    side = plane // 2
    inner = jnp.where((plane == 1) | (plane == 2), 1, 0).astype(jnp.int32)

    def by_role(on_inner, on_outer):
        return jnp.where(inner > 0, jnp.int32(on_inner), jnp.int32(on_outer))

    def links(pairs):
        return [(2 * a + h, 2 * b + h) for a, b in pairs for h in range(2)]

    def swap(array, planes):
        return lax.ppermute(array, "dp", [(2 * a + h, 2 * a + 1 - h) for a in planes for h in range(2)])

    def flip(array, bit):
        return lax.ppermute(array, "blk", [(i, i ^ bit) for i in range(4)])

    outer_to_inner = links([(0, 1), (3, 2)])
    inner_to_inner = links([(1, 2), (2, 1)])
    inner_to_outer = links([(1, 0), (2, 3)])
    every, inner_planes = (0, 1, 2, 3), (1, 2)

    def block(q, which):
        place = q // count
        chunk = jnp.where(side == 0, 3 - place, place)
        return (chunk * 2 + which) * count + q % count

    def mine(q):
        return block(q, half)

    def theirs(q):
        return block(q, 1 - half)

    near_inner = [2 * count + j for j in range(count)]
    near_outer = [3 * count + j for j in range(count)]
    steps = 3 * count - 1
    ahead = [s if s < 2 * count else s + 1 for s in range(steps)]
    main = [by_role(min(max(s - 2, 0), 2 * count - 1), ahead[s]) for s in range(steps)]
    own_chunk = [by_role(near_inner[j], near_outer[j]) for j in range(count)]
    double = steps - count
    first = jnp.int32(near_inner[0])

    inner_main, outer_main = [max(s - 2, 0) for s in range(steps)], ahead
    exchanges = [
        [(near_outer[0], outer_main[0])],
        [(near_outer[1], outer_main[1])],
        [(inner_main[2], outer_main[2]), (inner_main[3], outer_main[3])],
        [(inner_main[4], outer_main[4]), (inner_main[5], outer_main[5])],
        [
            (inner_main[6], outer_main[6]),
            (inner_main[7], outer_main[7]),
            (near_outer[2], near_outer[0]),
        ],
        [(near_inner[1], near_outer[1]), (near_inner[2], near_outer[2])],
    ]

    third, column = size // 3, theirs(first) * 3
    values, places = [inner], {}

    def put(name, value):
        places[name] = len(values)
        values.append(value)

    for s in range(steps):
        put(("main", s), mine(main[s]))
    for j in range(count):
        put(("out", j), mine(by_role(near_outer[j], ahead[double + j])))
        put(("own", j), mine(own_chunk[j]))
    for e, pairs in enumerate(exchanges):
        for k, pair in enumerate(pairs):
            put(("send", e, k), theirs(by_role(*pair)))
    put("blk", blk.astype(jnp.int32))
    put("first mine", mine(first))
    put("first theirs", theirs(first))
    put("first part", column + 1)
    put("second part", column + 2)
    table = jnp.stack(values)

    def columns_of(e):
        return [places["send", e, k] for k in range(len(exchanges[e]))]

    quarter, raw_0 = first_sends(blk, column, out_grads, inputs, pre_act, third)
    raw_1, send_0, raw_2, send_1 = cast_blocks(
        table,
        [
            (third, [places["first part"], places["second part"]]),
            (size, columns_of(0)),
            (size, [places["first mine"]]),
            (size, columns_of(1)),
        ],
        pre_act,
        [raw_0],
    )

    def send_in(array):
        return lax.ppermute(array, "dp", outer_to_inner)

    tied = lax.optimization_barrier
    pair_0 = swap(quarter, every)
    raw_0, raw_1, raw_2 = send_in(raw_0), send_in(raw_1), send_in(raw_2)
    quarter_in = send_in(quarter)
    got = [swap(send_0, every), swap(send_1, every)]
    pair_0, raw_0 = tied((pair_0, raw_0))
    pair_1, pair_2 = flip(pair_0, 1), flip(pair_0, 2)
    pair_2, pair_1, got[0], raw_1 = tied((pair_2, pair_1, got[0], raw_1))
    pair_3 = flip(pair_2, 1)
    def run(name, partner, **more):
        return piece(scale, table, places[name], pre_act, [partner[0]], partner[1], g, x, w_out, **more)

    toward, across = [], {}
    for s in range(steps):
        partner = (got[s], 0) if s < 2 else (got[1 + s // 2], s % 2)
        sends = columns_of(2 + s // 2) if s % 2 == 0 else []
        sums = [toward[s - 2]] if s >= 2 else []
        held_back = ([across[s - 4]] if s >= 4 else []) + ([first_in] if s == 3 else [])
        j = s - double
        if s == 0:
            out, g, x, *blocks = first_piece(
                scale,
                table,
                places["main", 0],
                places["blk"],
                pre_act,
                got[0],
                out_grads,
                inputs,
                [pair_0, pair_1, pair_2, pair_3],
                w_out,
                sends,
                [raw_2],
            )
        else:
            after = [last] + held_back + ([quarter_in] if s == 1 else [])
            if j >= 0:
                (last,) = run(
                    ("out", j),
                    partner,
                    sums=[across[j]],
                    other=(got[j], 0) if j < 2 else (got[4], 2),
                    after=after + sums,
                )
                toward.append(lax.ppermute(last, "dp", outer_to_inner + inner_to_outer))
                after = [last]
            out, *blocks = run(
                ("main", s), partner, sums=sums, sends=sends, after=after, flops=FLOPS
            )
        last = out
        if j < 0:
            toward.append(send_in(out))
        if blocks:
            got.append(swap(blocks[0], every))
        if s >= 2:
            across[s - 2] = lax.ppermute(out, "dp", inner_to_inner)
        if s == 0:
            line_quarter = tied((quarter_in, out))[0]
        if s == 1:
            in_1, in_2 = flip(line_quarter, 1), flip(line_quarter, 2)
            in_3 = flip(in_2, 1)
            line_g, line_x = join(blk, out_grads, inputs, [line_quarter, in_1, in_2, in_3], [last])
            (last,) = piece(
                scale,
                table,
                places["first theirs"],
                pre_act,
                [raw_0, raw_1],
                0,
                line_g,
                line_x,
                w_out,
                after=[last],
            )
            first_in = swap(last, inner_planes)
            rows_kept, last = input_partial(blk, out_grads, pre_act, w_in, w_out, 4 * size, [last, got[2]])
            rows_given = last
        if s == 4:
            (held_in,) = piece(
                scale,
                table,
                places["first mine"],
                pre_act,
                [raw_2],
                0,
                line_g,
                line_x,
                w_out,
                sums=[first_in],
                after=[last],
            )
            last = held_in

    rows_got = flip(tied((rows_given, last))[0], 2)
    held = final_first(
        scale,
        count,
        table,
        places["own", 0],
        0,
        pre_act,
        got[4],
        2,
        g,
        x,
        w_out,
        held_in,
        toward[double],
        across[count],
        [last],
    )
    last = held[0]
    for i in range(1, count):
        (out,) = run(("own", i), (got[5], i - 1), sums=[across[count + i]], after=[last])
        if i == 1:
            rows_kept, rows_given = fold(blk, rows_kept, rows_got, [out])
            rows_got = flip(rows_given, 1)
            held = final_add(i, out, toward[double + i], held, [rows_given])
            grad_inputs = round_sum(rows_kept, rows_got, [held[0]])
            last = grad_inputs
        else:
            held = final_add(i, out, toward[double + i], held, [])
    return (grad_inputs, held[0], held[1])


def solution(mesh):
    def body(inputs, out_grads, pre_act, w_in, w_out):
        fits = pre_act.shape[1] % (8 * PIECES * 128) == 0 and inputs.shape[0] % 64 == 0
        run = line_body if (mesh.shape["dp"], mesh.shape["blk"]) == (8, 4) and fits else plain_body
        return run(inputs, out_grads, pre_act, w_in, w_out)

    return jax.shard_map(
        body,
        mesh=mesh,
        in_specs=(P("dp", None), P("dp", None), P("dp", "blk"), P("blk", None), P("blk", None)),
        out_specs=(P(("dp", "blk"), None), P(("blk", "dp"), None), P(("blk", "dp"), None)),
        check_vma=False,
    )
```

```python
import functools

import jax
import jax.numpy as jnp
from jax import lax
from jax.experimental import pallas as pl
from jax.experimental.pallas import tpu as pltpu
from jax.sharding import PartitionSpec as P

PIECES = 3
FLOPS = 100_000_000_000
VMEM_LIMIT = 63 * 1024 * 1024


def contract_rows(left, right):
    return lax.dot_general(
        left, right, (((0,), (0,)), ((), ())), preferred_element_type=jnp.float32
    )


def hidden_grads(out_grads, pre_act, w_out):
    back = lax.dot_general(
        out_grads, w_out, (((1,), (1,)), ((), ())), preferred_element_type=jnp.float32
    )
    return jnp.where(pre_act > 0, back, jnp.zeros_like(back)).astype(jnp.bfloat16)


def input_grads(grad_hidden, w_in):
    return lax.psum_scatter(
        jnp.dot(grad_hidden, w_in, preferred_element_type=jnp.float32),
        "blk",
        scatter_dimension=0,
        tiled=True,
    ).astype(jnp.bfloat16)


def plain_body(inputs, out_grads, pre_act, w_in, w_out):
    token_total = inputs.shape[0] * lax.axis_size("dp")
    factor = lax.rsqrt(jnp.asarray(token_total, jnp.float32))
    act = jnp.maximum(pre_act, jnp.zeros_like(pre_act))
    grad_hidden = hidden_grads(out_grads, pre_act, w_out)
    grad_out = contract_rows(act, out_grads) * factor
    grad_in = contract_rows(grad_hidden, inputs) * factor
    return (
        input_grads(grad_hidden, w_in),
        lax.psum_scatter(grad_in, "dp", scatter_dimension=0, tiled=True),
        lax.psum_scatter(grad_out, "dp", scatter_dimension=0, tiled=True),
    )


def params():
    return pltpu.CompilerParams(vmem_limit_bytes=VMEM_LIMIT)


def anywhere(arrays):
    return [pl.BlockSpec(memory_space=pl.ANY)] * len(arrays)


def cast_kernel(shapes, idx_ref, *refs):
    outs = refs[-len(shapes) :]
    for (_, count), out_ref in zip(shapes, outs):
        width = out_ref.shape[1] // count
        for k in range(count):
            out_ref[:, k * width : (k + 1) * width] = refs[k][...].astype(jnp.float32)
        refs = refs[count:]


def cast_blocks(table, groups, pre_act, after):
    rows = pre_act.shape[0]
    in_specs = [columns_spec(rows, width, at) for width, places in groups for at in places]
    shapes = [(width * len(places), len(places)) for width, places in groups]
    return pl.pallas_call(
        functools.partial(cast_kernel, shapes),
        grid_spec=pltpu.PrefetchScalarGridSpec(
            num_scalar_prefetch=1,
            grid=(1,),
            in_specs=in_specs + anywhere(after),
            out_specs=[pl.BlockSpec((rows, width), lambda i, idx: (0, 0)) for width, _ in shapes],
        ),
        out_shape=[jax.ShapeDtypeStruct((rows, width), jnp.float32) for width, _ in shapes],
        compiler_params=params(),
        cost_estimate=piece_cost(),
        name="cast_blocks",
    )(table, *([pre_act] * len(in_specs)), *after)


def first_kernel(blk_ref, column_ref, grads_ref, inputs_ref, pre_ref, quarter_ref, raw_ref):
    quarter = grads_ref.shape[0]
    quarter_ref[:quarter, :] = grads_ref[...].astype(jnp.float32)
    quarter_ref[quarter:, :] = inputs_ref[...].astype(jnp.float32)
    raw_ref[...] = pre_ref[...].astype(jnp.float32)


def first_sends(blk, column, out_grads, inputs, pre_act, size):
    rows, width = out_grads.shape
    quarter = rows // 4
    tokens = pl.BlockSpec((quarter, width), lambda i, blk, column: (blk[0], 0))
    return pl.pallas_call(
        first_kernel,
        grid_spec=pltpu.PrefetchScalarGridSpec(
            num_scalar_prefetch=2,
            grid=(1,),
            in_specs=[tokens, tokens, pl.BlockSpec((rows, size), lambda i, blk, column: (0, column[0]))],
            out_specs=[
                pl.BlockSpec((2 * quarter, width), lambda i, blk, column: (0, 0)),
                pl.BlockSpec((rows, size), lambda i, blk, column: (0, 0)),
            ],
        ),
        out_shape=[
            jax.ShapeDtypeStruct((2 * quarter, width), jnp.float32),
            jax.ShapeDtypeStruct((rows, size), jnp.float32),
        ],
        compiler_params=params(),
        cost_estimate=piece_cost(),
        name="first_sends",
    )(blk.reshape(1), column.reshape(1), out_grads, inputs, pre_act)


def fill_tokens(blk, grads_ref, inputs_ref, quarters, g_ref, x_ref):
    rows = grads_ref.shape[0]
    quarter = rows // 4
    g_ref[:rows, :] = grads_ref[...]
    x_ref[:rows, :] = inputs_ref[...]
    for k, ref in enumerate(quarters):
        where = jnp.bitwise_xor(blk, k)
        place = pl.ds(pl.multiple_of(rows + where * quarter, quarter), quarter)
        g_ref[place, :] = ref[:quarter, :].astype(jnp.bfloat16)
        x_ref[place, :] = ref[quarter:, :].astype(jnp.bfloat16)


def join_kernel(blk_ref, grads_ref, inputs_ref, *refs):
    fill_tokens(blk_ref[0], grads_ref, inputs_ref, refs[:4], *refs[-2:])


def join(blk, out_grads, inputs, quarters, after):
    rows, width = out_grads.shape
    shape = jax.ShapeDtypeStruct((2 * rows, width), jnp.bfloat16)
    vmem = pl.BlockSpec(memory_space=pltpu.VMEM)
    return pl.pallas_call(
        join_kernel,
        out_shape=(shape, shape),
        in_specs=[pl.BlockSpec(memory_space=pltpu.SMEM)] + [vmem] * 6 + anywhere(after),
        out_specs=(vmem, vmem),
        compiler_params=params(),
        cost_estimate=piece_cost(),
        name="join_tokens",
    )(blk.reshape(1), out_grads, inputs, *quarters, *after)


def input_kernel(blk_ref, grads_ref, pre_ref, out_rows_ref, in_rows_ref, *refs):
    keep_ref, give_ref, total_ref = refs[-3:]

    @pl.when(pl.program_id(0) == 0)
    def _():
        total_ref[...] = jnp.zeros_like(total_ref)

    hidden = hidden_grads(grads_ref[...], pre_ref[...], out_rows_ref[...])
    total_ref[...] += jnp.dot(hidden, in_rows_ref[...], preferred_element_type=jnp.float32)

    @pl.when(pl.program_id(0) == pl.num_programs(0) - 1)
    def _():
        half = keep_ref.shape[0]
        x = blk_ref[0] // 2
        keep_ref[...] = total_ref[pl.ds(pl.multiple_of(x * half, half), half), :]
        give_ref[...] = total_ref[pl.ds(pl.multiple_of((1 - x) * half, half), half), :]


def input_partial(blk, out_grads, pre_act, w_in, w_out, size, after):
    rows, hidden = pre_act.shape
    width = out_grads.shape[1]
    tokens = pl.BlockSpec((rows, width), lambda i, blk: (0, 0))
    weights = pl.BlockSpec((size, width), lambda i, blk: (i, 0))
    half = jax.ShapeDtypeStruct((rows // 2, width), jnp.float32)
    return pl.pallas_call(
        input_kernel,
        grid_spec=pltpu.PrefetchScalarGridSpec(
            num_scalar_prefetch=1,
            grid=(hidden // size,),
            in_specs=[tokens, pl.BlockSpec((rows, size), lambda i, blk: (0, i)), weights, weights]
            + anywhere(after),
            out_specs=[pl.BlockSpec(half.shape, lambda i, blk: (0, 0))] * 2,
            scratch_shapes=[pltpu.VMEM((rows, width), jnp.float32)],
        ),
        out_shape=[half, half],
        compiler_params=params(),
        cost_estimate=piece_cost(),
        name="input_partial",
    )(blk.reshape(1), out_grads, pre_act, w_out, w_in, *after)


def fold_kernel(blk_ref, kept_ref, got_ref, *refs):
    keep_ref, give_ref = refs[-2:]
    rows = keep_ref.shape[0]
    core = blk_ref[0] % 2
    for ref, place in ((keep_ref, core), (give_ref, 1 - core)):
        part = pl.ds(pl.multiple_of(place * rows, rows), rows)
        ref[...] = kept_ref[part, :] + got_ref[part, :]


def fold(blk, kept, got, after):
    rows, width = kept.shape
    half = jax.ShapeDtypeStruct((rows // 2, width), jnp.float32)
    vmem = pl.BlockSpec(memory_space=pltpu.VMEM)
    return pl.pallas_call(
        fold_kernel,
        out_shape=(half, half),
        in_specs=[pl.BlockSpec(memory_space=pltpu.SMEM), vmem, vmem] + anywhere(after),
        out_specs=(vmem, vmem),
        compiler_params=params(),
        cost_estimate=piece_cost(),
        name="fold_rows",
    )(blk.reshape(1), kept, got, *after)


def round_kernel(kept_ref, got_ref, *refs):
    refs[-1][...] = (kept_ref[...] + got_ref[...]).astype(jnp.bfloat16)


def round_sum(kept, got, after):
    vmem = pl.BlockSpec(memory_space=pltpu.VMEM)
    return pl.pallas_call(
        round_kernel,
        out_shape=jax.ShapeDtypeStruct(kept.shape, jnp.bfloat16),
        in_specs=[vmem, vmem] + anywhere(after),
        out_specs=vmem,
        compiler_params=params(),
        cost_estimate=piece_cost(),
        name="round_sum",
    )(kept, got, *after)


def piece_math(scale, own, partner, g, x, w):
    pre = jnp.concatenate([own, partner.astype(jnp.bfloat16)], axis=0)
    hidden = hidden_grads(g, pre, w)
    act = jnp.maximum(pre, jnp.zeros_like(pre))
    return contract_rows(hidden, x) * scale, contract_rows(act, g) * scale


def piece_kernel(scale, counts, inner_at, table_ref, own_ref, g_ref, x_ref, w_ref, *refs):
    groups = []
    for n in counts:
        groups.append(refs[:n])
        refs = refs[n:]
    partners, others, columns, sums, _, (out_ref, *sends) = groups + [refs]
    partner = jnp.concatenate([ref[...] for ref in partners], axis=1)
    for ref in others:
        partner = jnp.where(table_ref[inner_at] > 0, ref[...], partner)
    grad_in, grad_out = piece_math(scale, own_ref[...], partner, g_ref[...], x_ref[...], w_ref[...])
    for ref in sums:
        grad_in = grad_in + ref[0]
        grad_out = grad_out + ref[1]
    out_ref[0], out_ref[1] = grad_in, grad_out
    rows = own_ref.shape[0]
    for ref in sends:
        for k, column_ref in enumerate(columns):
            ref[k * rows : (k + 1) * rows, :] = column_ref[...].astype(jnp.float32)


def columns_spec(rows, size, at):
    return pl.BlockSpec((rows, size), lambda i, table: (0, table[at]))


def piece_specs(rows, size, width, at):
    tokens = pl.BlockSpec((2 * rows, width), lambda i, table: (0, 0))
    return [
        columns_spec(rows, size, at),
        tokens,
        tokens,
        pl.BlockSpec((size, width), lambda i, table: (table[at], 0)),
    ]


def partner_spec(rows, size, place):
    return pl.BlockSpec((rows, size), lambda i, table: (place, 0))


def piece_cost(flops=1):
    return pl.CostEstimate(flops=flops, bytes_accessed=1, transcendentals=0)


def piece(
    scale, table, at, pre_act, partners, place, g, x, w_out, sums=(), other=None, inner_at=0, sends=(), after=(), flops=1
):
    rows, width = pre_act.shape[0], g.shape[1]
    size = sum(p.shape[1] for p in partners)
    whole = pl.BlockSpec((2, size, width), lambda i, table: (0, 0, 0))
    others, other_specs = [], []
    if other is not None:
        others = [other[0]]
        other_specs = [partner_spec(rows, size, other[1])]
    counts = (len(partners), len(others), len(sends), len(sums), len(after))
    sent = [(len(sends) * rows, size)] if sends else []
    return pl.pallas_call(
        functools.partial(piece_kernel, scale, counts, inner_at),
        grid_spec=pltpu.PrefetchScalarGridSpec(
            num_scalar_prefetch=1,
            grid=(1,),
            in_specs=piece_specs(rows, size, width, at)
            + [partner_spec(rows, p.shape[1], place) for p in partners]
            + other_specs
            + [columns_spec(rows, size, k) for k in sends]
            + [whole] * len(sums)
            + anywhere(after),
            out_specs=[whole] + [pl.BlockSpec(shape, lambda i, table: (0, 0)) for shape in sent],
        ),
        out_shape=[jax.ShapeDtypeStruct(shape, jnp.float32) for shape in [(2, size, width)] + sent],
        compiler_params=params(),
        cost_estimate=piece_cost(flops),
        name="piece",
    )(table, pre_act, g, x, w_out, *partners, *others, *([pre_act] * len(sends)), *sums, *after)


def first_piece_kernel(
    scale, blk_at, table_ref, own_ref, w_ref, partner_ref, grads_ref, inputs_ref, q0_ref, q1_ref, q2_ref, q3_ref, a_ref, b_ref, *refs
):
    out_ref, g_ref, x_ref, send_ref = refs[-4:]
    rows = grads_ref.shape[0]
    quarters = (q0_ref, q1_ref, q2_ref, q3_ref)
    fill_tokens(table_ref[blk_at], grads_ref, inputs_ref, quarters, g_ref, x_ref)
    out_ref[0], out_ref[1] = piece_math(
        scale, own_ref[...], partner_ref[...], g_ref[...], x_ref[...], w_ref[...]
    )
    send_ref[:rows, :] = a_ref[...].astype(jnp.float32)
    send_ref[rows:, :] = b_ref[...].astype(jnp.float32)


def first_piece(scale, table, at, blk_at, pre_act, partner, out_grads, inputs, quarters, w_out, sends, after):
    rows, width = out_grads.shape
    size = partner.shape[1]
    whole = lambda *shape: pl.BlockSpec(shape, lambda i, table: (0,) * len(shape))
    tokens = jax.ShapeDtypeStruct((2 * rows, width), jnp.bfloat16)
    return pl.pallas_call(
        functools.partial(first_piece_kernel, scale, blk_at),
        grid_spec=pltpu.PrefetchScalarGridSpec(
            num_scalar_prefetch=1,
            grid=(1,),
            in_specs=[
                columns_spec(rows, size, at),
                pl.BlockSpec((size, width), lambda i, table: (table[at], 0)),
                whole(rows, size),
                whole(rows, width),
                whole(rows, width),
            ]
            + [whole(rows // 2, width)] * 4
            + [columns_spec(rows, size, k) for k in sends]
            + anywhere(after),
            out_specs=[
                whole(2, size, width),
                whole(2 * rows, width),
                whole(2 * rows, width),
                whole(2 * rows, size),
            ],
        ),
        out_shape=[
            jax.ShapeDtypeStruct((2, size, width), jnp.float32),
            tokens,
            tokens,
            jax.ShapeDtypeStruct((2 * rows, size), jnp.float32),
        ],
        compiler_params=params(),
        cost_estimate=piece_cost(),
        name="first_piece",
    )(table, pre_act, w_out, partner, out_grads, inputs, *quarters, pre_act, pre_act, *after)


def final_kernel(scale, inner_at, table_ref, own_ref, g_ref, x_ref, w_ref, partner_ref, inner_ref, outer_ref, *refs):
    sum_ref, (in_ref, out_ref) = refs[0], refs[-2:]
    grad_in, grad_out = piece_math(
        scale, own_ref[...], partner_ref[...], g_ref[...], x_ref[...], w_ref[...]
    )
    is_inner = table_ref[inner_at] > 0
    in_ref[...] = jnp.where(is_inner, inner_ref[0], grad_in + outer_ref[0]) + sum_ref[0]
    out_ref[...] = jnp.where(is_inner, inner_ref[1], grad_out + outer_ref[1]) + sum_ref[1]


def final_first(
    scale, count, table, at, inner_at, pre_act, partner, place, g, x, w_out, held, received, added, after
):
    rows, size, width = pre_act.shape[0], partner.shape[1], g.shape[1]
    whole = pl.BlockSpec((2, size, width), lambda i, table: (0, 0, 0))
    shape = jax.ShapeDtypeStruct((count * size, width), jnp.float32)
    return pl.pallas_call(
        functools.partial(final_kernel, scale, inner_at),
        grid_spec=pltpu.PrefetchScalarGridSpec(
            num_scalar_prefetch=1,
            grid=(1,),
            in_specs=piece_specs(rows, size, width, at)
            + [partner_spec(rows, size, place)]
            + [whole] * 3
            + anywhere(after),
            out_specs=[pl.BlockSpec((size, width), lambda i, table: (0, 0))] * 2,
        ),
        out_shape=(shape, shape),
        compiler_params=params(),
        cost_estimate=piece_cost(),
        name="final_first",
    )(table, pre_act, g, x, w_out, partner, held, received, added, *after)


def add_kernel(a_ref, b_ref, *refs):
    in_ref, out_ref = refs[-2:]
    in_ref[...] = a_ref[0] + b_ref[0]
    out_ref[...] = a_ref[1] + b_ref[1]


def final_add(place, a, b, held, after):
    _, size, width = a.shape
    steps = 2
    block = pl.BlockSpec((2, size // steps, width), lambda i: (0, i, 0))
    return pl.pallas_call(
        add_kernel,
        grid=(steps,),
        in_specs=[block, block] + anywhere(held) + anywhere(after),
        out_specs=[pl.BlockSpec((size // steps, width), lambda i: (place * steps + i, 0))] * 2,
        out_shape=[jax.ShapeDtypeStruct(h.shape, h.dtype) for h in held],
        input_output_aliases={2: 0, 3: 1},
        compiler_params=params(),
        name="final_add",
    )(a, b, *held, *after)


def line_body(inputs, out_grads, pre_act, w_in, w_out):
    count = PIECES
    rows, hidden = pre_act.shape
    size = hidden // (8 * count)
    scale = 1.0 / (rows * lax.axis_size("dp")) ** 0.5
    me, blk = lax.axis_index("dp"), lax.axis_index("blk")
    plane, half = me // 2, me % 2
    side = plane // 2
    inner = jnp.where((plane == 1) | (plane == 2), 1, 0).astype(jnp.int32)

    def by_role(on_inner, on_outer):
        return jnp.where(inner > 0, jnp.int32(on_inner), jnp.int32(on_outer))

    def links(pairs):
        return [(2 * a + h, 2 * b + h) for a, b in pairs for h in range(2)]

    def swap(array, planes):
        return lax.ppermute(array, "dp", [(2 * a + h, 2 * a + 1 - h) for a in planes for h in range(2)])

    def flip(array, bit):
        return lax.ppermute(array, "blk", [(i, i ^ bit) for i in range(4)])

    outer_to_inner = links([(0, 1), (3, 2)])
    inner_to_inner = links([(1, 2), (2, 1)])
    inner_to_outer = links([(1, 0), (2, 3)])
    every, inner_planes = (0, 1, 2, 3), (1, 2)

    def block(q, which):
        place = q // count
        chunk = jnp.where(side == 0, 3 - place, place)
        return (chunk * 2 + which) * count + q % count

    def mine(q):
        return block(q, half)

    def theirs(q):
        return block(q, 1 - half)

    near_inner = [2 * count + j for j in range(count)]
    near_outer = [3 * count + j for j in range(count)]
    steps = 3 * count - 1
    ahead = [s if s < 2 * count else s + 1 for s in range(steps)]
    main = [by_role(min(max(s - 2, 0), 2 * count - 1), ahead[s]) for s in range(steps)]
    own_chunk = [by_role(near_inner[j], near_outer[j]) for j in range(count)]
    double = steps - count
    first = jnp.int32(near_inner[0])

    inner_main, outer_main = [max(s - 2, 0) for s in range(steps)], ahead
    exchanges = [
        [(near_outer[0], outer_main[0])],
        [(near_outer[1], outer_main[1])],
        [(inner_main[2], outer_main[2]), (inner_main[3], outer_main[3])],
        [(inner_main[4], outer_main[4]), (inner_main[5], outer_main[5])],
        [
            (inner_main[6], outer_main[6]),
            (inner_main[7], outer_main[7]),
            (near_outer[2], near_outer[0]),
        ],
        [(near_inner[1], near_outer[1]), (near_inner[2], near_outer[2])],
    ]

    third, column = size // 3, theirs(first) * 3
    values, places = [inner], {}

    def put(name, value):
        places[name] = len(values)
        values.append(value)

    for s in range(steps):
        put(("main", s), mine(main[s]))
    for j in range(count):
        put(("out", j), mine(by_role(near_outer[j], ahead[double + j])))
        put(("own", j), mine(own_chunk[j]))
    for e, pairs in enumerate(exchanges):
        for k, pair in enumerate(pairs):
            put(("send", e, k), theirs(by_role(*pair)))
    put("blk", blk.astype(jnp.int32))
    put("first mine", mine(first))
    put("first theirs", theirs(first))
    put("first part", column + 1)
    put("second part", column + 2)
    table = jnp.stack(values)

    def columns_of(e):
        return [places["send", e, k] for k in range(len(exchanges[e]))]

    quarter, raw_0 = first_sends(blk, column, out_grads, inputs, pre_act, third)
    raw_1, send_0, raw_2, send_1 = cast_blocks(
        table,
        [
            (third, [places["first part"], places["second part"]]),
            (size, columns_of(0)),
            (size, [places["first mine"]]),
            (size, columns_of(1)),
        ],
        pre_act,
        [raw_0],
    )

    def send_in(array):
        return lax.ppermute(array, "dp", outer_to_inner)

    tied = lax.optimization_barrier
    pair_0 = swap(quarter, every)
    raw_0, raw_1, raw_2 = send_in(raw_0), send_in(raw_1), send_in(raw_2)
    quarter_in = send_in(quarter)
    got = [swap(send_0, every), swap(send_1, every)]
    pair_0, raw_0 = tied((pair_0, raw_0))
    pair_1, pair_2 = flip(pair_0, 1), flip(pair_0, 2)
    pair_2, pair_1, got[0], raw_1 = tied((pair_2, pair_1, got[0], raw_1))
    pair_3 = flip(pair_2, 1)
    def run(name, partner, **more):
        return piece(scale, table, places[name], pre_act, [partner[0]], partner[1], g, x, w_out, **more)

    toward, across = [], {}
    for s in range(steps):
        partner = (got[s], 0) if s < 2 else (got[1 + s // 2], s % 2)
        sends = columns_of(2 + s // 2) if s % 2 == 0 else []
        sums = [toward[s - 2]] if s >= 2 else []
        held_back = ([across[s - 4]] if s >= 4 else []) + ([first_in] if s == 3 else [])
        j = s - double
        if s == 0:
            out, g, x, *blocks = first_piece(
                scale,
                table,
                places["main", 0],
                places["blk"],
                pre_act,
                got[0],
                out_grads,
                inputs,
                [pair_0, pair_1, pair_2, pair_3],
                w_out,
                sends,
                [raw_2],
            )
        else:
            after = [last] + held_back + ([quarter_in] if s == 1 else [])
            if j >= 0:
                (last,) = run(
                    ("out", j),
                    partner,
                    sums=[across[j]],
                    other=(got[j], 0) if j < 2 else (got[4], 2),
                    after=after + sums,
                )
                toward.append(lax.ppermute(last, "dp", outer_to_inner + inner_to_outer))
                after = [last]
            out, *blocks = run(
                ("main", s), partner, sums=sums, sends=sends, after=after, flops=FLOPS
            )
        last = out
        if j < 0:
            toward.append(send_in(out))
        if blocks:
            got.append(swap(blocks[0], every))
        if s >= 2:
            across[s - 2] = lax.ppermute(out, "dp", inner_to_inner)
        if s == 1:
            line_quarter = tied((quarter_in, out))[0]
            in_1, in_2 = flip(line_quarter, 1), flip(line_quarter, 2)
            in_3 = flip(in_2, 1)
            line_g, line_x = join(blk, out_grads, inputs, [line_quarter, in_1, in_2, in_3], [last, got[2]])
            (last,) = piece(
                scale,
                table,
                places["first theirs"],
                pre_act,
                [raw_0, raw_1],
                0,
                line_g,
                line_x,
                w_out,
                after=[last],
            )
            first_in = swap(last, inner_planes)
        if s == 3:
            rows_kept, rows_given = input_partial(blk, out_grads, pre_act, w_in, w_out, 4 * size, [last])
            last = rows_given
        if s == 4:
            (held_in,) = piece(
                scale,
                table,
                places["first mine"],
                pre_act,
                [raw_2],
                0,
                line_g,
                line_x,
                w_out,
                sums=[first_in],
                after=[last],
            )
            last = held_in

    rows_got = flip(tied((rows_given, last))[0], 2)
    held = final_first(
        scale,
        count,
        table,
        places["own", 0],
        0,
        pre_act,
        got[4],
        2,
        g,
        x,
        w_out,
        held_in,
        toward[double],
        across[count],
        [last],
    )
    last = held[0]
    for i in range(1, count):
        (out,) = run(("own", i), (got[5], i - 1), sums=[across[count + i]], after=[last])
        if i == 1:
            rows_kept, rows_given = fold(blk, rows_kept, rows_got, [out])
            rows_got = flip(rows_given, 1)
            held = final_add(i, out, toward[double + i], held, [rows_given])
            grad_inputs = round_sum(rows_kept, rows_got, [held[0]])
            last = grad_inputs
        else:
            held = final_add(i, out, toward[double + i], held, [])
    return (grad_inputs, held[0], held[1])


def solution(mesh):
    def body(inputs, out_grads, pre_act, w_in, w_out):
        fits = pre_act.shape[1] % (8 * PIECES * 128) == 0 and inputs.shape[0] % 64 == 0
        run = line_body if (mesh.shape["dp"], mesh.shape["blk"]) == (8, 4) and fits else plain_body
        return run(inputs, out_grads, pre_act, w_in, w_out)

    return jax.shard_map(
        body,
        mesh=mesh,
        in_specs=(P("dp", None), P("dp", None), P("dp", "blk"), P("blk", None), P("blk", None)),
        out_specs=(P(("dp", "blk"), None), P(("blk", "dp"), None), P(("blk", "dp"), None)),
        check_vma=False,
    )
```

```python
import functools

import jax
import jax.numpy as jnp
from jax import lax
from jax.experimental import pallas as pl
from jax.experimental.pallas import tpu as pltpu
from jax.sharding import PartitionSpec as P

PIECES = 3
FLOPS = 100_000_000_000
VMEM_LIMIT = 63 * 1024 * 1024


def contract_rows(left, right):
    return lax.dot_general(
        left, right, (((0,), (0,)), ((), ())), preferred_element_type=jnp.float32
    )


def hidden_grads(out_grads, pre_act, w_out):
    back = lax.dot_general(
        out_grads, w_out, (((1,), (1,)), ((), ())), preferred_element_type=jnp.float32
    )
    return jnp.where(pre_act > 0, back, jnp.zeros_like(back)).astype(jnp.bfloat16)


def input_grads(grad_hidden, w_in):
    return lax.psum_scatter(
        jnp.dot(grad_hidden, w_in, preferred_element_type=jnp.float32),
        "blk",
        scatter_dimension=0,
        tiled=True,
    ).astype(jnp.bfloat16)


def plain_body(inputs, out_grads, pre_act, w_in, w_out):
    token_total = inputs.shape[0] * lax.axis_size("dp")
    factor = lax.rsqrt(jnp.asarray(token_total, jnp.float32))
    act = jnp.maximum(pre_act, jnp.zeros_like(pre_act))
    grad_hidden = hidden_grads(out_grads, pre_act, w_out)
    grad_out = contract_rows(act, out_grads) * factor
    grad_in = contract_rows(grad_hidden, inputs) * factor
    return (
        input_grads(grad_hidden, w_in),
        lax.psum_scatter(grad_in, "dp", scatter_dimension=0, tiled=True),
        lax.psum_scatter(grad_out, "dp", scatter_dimension=0, tiled=True),
    )


def params():
    return pltpu.CompilerParams(vmem_limit_bytes=VMEM_LIMIT)


def anywhere(arrays):
    return [pl.BlockSpec(memory_space=pl.ANY)] * len(arrays)


def cast_kernel(shapes, idx_ref, *refs):
    outs = refs[-len(shapes) :]
    for (_, count), out_ref in zip(shapes, outs):
        width = out_ref.shape[1] // count
        for k in range(count):
            out_ref[:, k * width : (k + 1) * width] = refs[k][...].astype(jnp.float32)
        refs = refs[count:]


def cast_blocks(table, groups, pre_act, after):
    rows = pre_act.shape[0]
    in_specs = [columns_spec(rows, width, at) for width, places in groups for at in places]
    shapes = [(width * len(places), len(places)) for width, places in groups]
    return pl.pallas_call(
        functools.partial(cast_kernel, shapes),
        grid_spec=pltpu.PrefetchScalarGridSpec(
            num_scalar_prefetch=1,
            grid=(1,),
            in_specs=in_specs + anywhere(after),
            out_specs=[pl.BlockSpec((rows, width), lambda i, idx: (0, 0)) for width, _ in shapes],
        ),
        out_shape=[jax.ShapeDtypeStruct((rows, width), jnp.float32) for width, _ in shapes],
        compiler_params=params(),
        cost_estimate=piece_cost(),
        name="cast_blocks",
    )(table, *([pre_act] * len(in_specs)), *after)


def first_kernel(blk_ref, column_ref, grads_ref, inputs_ref, pre_ref, quarter_ref, raw_ref):
    quarter = grads_ref.shape[0]
    quarter_ref[:quarter, :] = grads_ref[...].astype(jnp.float32)
    quarter_ref[quarter:, :] = inputs_ref[...].astype(jnp.float32)
    raw_ref[...] = pre_ref[...].astype(jnp.float32)


def first_sends(blk, column, out_grads, inputs, pre_act, size):
    rows, width = out_grads.shape
    quarter = rows // 4
    tokens = pl.BlockSpec((quarter, width), lambda i, blk, column: (blk[0], 0))
    return pl.pallas_call(
        first_kernel,
        grid_spec=pltpu.PrefetchScalarGridSpec(
            num_scalar_prefetch=2,
            grid=(1,),
            in_specs=[tokens, tokens, pl.BlockSpec((rows, size), lambda i, blk, column: (0, column[0]))],
            out_specs=[
                pl.BlockSpec((2 * quarter, width), lambda i, blk, column: (0, 0)),
                pl.BlockSpec((rows, size), lambda i, blk, column: (0, 0)),
            ],
        ),
        out_shape=[
            jax.ShapeDtypeStruct((2 * quarter, width), jnp.float32),
            jax.ShapeDtypeStruct((rows, size), jnp.float32),
        ],
        compiler_params=params(),
        cost_estimate=piece_cost(),
        name="first_sends",
    )(blk.reshape(1), column.reshape(1), out_grads, inputs, pre_act)


def fill_tokens(blk, grads_ref, inputs_ref, quarters, g_ref, x_ref):
    rows = grads_ref.shape[0]
    quarter = rows // 4
    g_ref[:rows, :] = grads_ref[...]
    x_ref[:rows, :] = inputs_ref[...]
    for k, ref in enumerate(quarters):
        where = jnp.bitwise_xor(blk, k)
        place = pl.ds(pl.multiple_of(rows + where * quarter, quarter), quarter)
        g_ref[place, :] = ref[:quarter, :].astype(jnp.bfloat16)
        x_ref[place, :] = ref[quarter:, :].astype(jnp.bfloat16)


def join_kernel(blk_ref, grads_ref, inputs_ref, *refs):
    fill_tokens(blk_ref[0], grads_ref, inputs_ref, refs[:4], *refs[-2:])


def join(blk, out_grads, inputs, quarters, after):
    rows, width = out_grads.shape
    shape = jax.ShapeDtypeStruct((2 * rows, width), jnp.bfloat16)
    vmem = pl.BlockSpec(memory_space=pltpu.VMEM)
    return pl.pallas_call(
        join_kernel,
        out_shape=(shape, shape),
        in_specs=[pl.BlockSpec(memory_space=pltpu.SMEM)] + [vmem] * 6 + anywhere(after),
        out_specs=(vmem, vmem),
        compiler_params=params(),
        cost_estimate=piece_cost(),
        name="join_tokens",
    )(blk.reshape(1), out_grads, inputs, *quarters, *after)


def input_kernel(blk_ref, grads_ref, pre_ref, out_rows_ref, in_rows_ref, *refs):
    keep_ref, give_ref, total_ref = refs[-3:]

    @pl.when(pl.program_id(0) == 0)
    def _():
        total_ref[...] = jnp.zeros_like(total_ref)

    hidden = hidden_grads(grads_ref[...], pre_ref[...], out_rows_ref[...])
    total_ref[...] += jnp.dot(hidden, in_rows_ref[...], preferred_element_type=jnp.float32)

    @pl.when(pl.program_id(0) == pl.num_programs(0) - 1)
    def _():
        half = keep_ref.shape[0]
        x = blk_ref[0] // 2
        keep_ref[...] = total_ref[pl.ds(pl.multiple_of(x * half, half), half), :]
        give_ref[...] = total_ref[pl.ds(pl.multiple_of((1 - x) * half, half), half), :]


def input_partial(blk, out_grads, pre_act, w_in, w_out, size, after):
    rows, hidden = pre_act.shape
    width = out_grads.shape[1]
    tokens = pl.BlockSpec((rows, width), lambda i, blk: (0, 0))
    weights = pl.BlockSpec((size, width), lambda i, blk: (i, 0))
    half = jax.ShapeDtypeStruct((rows // 2, width), jnp.float32)
    return pl.pallas_call(
        input_kernel,
        grid_spec=pltpu.PrefetchScalarGridSpec(
            num_scalar_prefetch=1,
            grid=(hidden // size,),
            in_specs=[tokens, pl.BlockSpec((rows, size), lambda i, blk: (0, i)), weights, weights]
            + anywhere(after),
            out_specs=[pl.BlockSpec(half.shape, lambda i, blk: (0, 0))] * 2,
            scratch_shapes=[pltpu.VMEM((rows, width), jnp.float32)],
        ),
        out_shape=[half, half],
        compiler_params=params(),
        cost_estimate=piece_cost(),
        name="input_partial",
    )(blk.reshape(1), out_grads, pre_act, w_out, w_in, *after)


def fold_kernel(blk_ref, kept_ref, got_ref, *refs):
    keep_ref, give_ref = refs[-2:]
    rows = keep_ref.shape[0]
    core = blk_ref[0] % 2
    for ref, place in ((keep_ref, core), (give_ref, 1 - core)):
        part = pl.ds(pl.multiple_of(place * rows, rows), rows)
        ref[...] = kept_ref[part, :] + got_ref[part, :]


def fold(blk, kept, got, after):
    rows, width = kept.shape
    half = jax.ShapeDtypeStruct((rows // 2, width), jnp.float32)
    vmem = pl.BlockSpec(memory_space=pltpu.VMEM)
    return pl.pallas_call(
        fold_kernel,
        out_shape=(half, half),
        in_specs=[pl.BlockSpec(memory_space=pltpu.SMEM), vmem, vmem] + anywhere(after),
        out_specs=(vmem, vmem),
        compiler_params=params(),
        cost_estimate=piece_cost(),
        name="fold_rows",
    )(blk.reshape(1), kept, got, *after)


def round_kernel(kept_ref, got_ref, *refs):
    refs[-1][...] = (kept_ref[...] + got_ref[...]).astype(jnp.bfloat16)


def round_sum(kept, got, after):
    vmem = pl.BlockSpec(memory_space=pltpu.VMEM)
    return pl.pallas_call(
        round_kernel,
        out_shape=jax.ShapeDtypeStruct(kept.shape, jnp.bfloat16),
        in_specs=[vmem, vmem] + anywhere(after),
        out_specs=vmem,
        compiler_params=params(),
        cost_estimate=piece_cost(),
        name="round_sum",
    )(kept, got, *after)


def piece_math(scale, own, partner, g, x, w):
    pre = jnp.concatenate([own, partner.astype(jnp.bfloat16)], axis=0)
    hidden = hidden_grads(g, pre, w)
    act = jnp.maximum(pre, jnp.zeros_like(pre))
    return contract_rows(hidden, x) * scale, contract_rows(act, g) * scale


def piece_kernel(scale, counts, inner_at, table_ref, own_ref, g_ref, x_ref, w_ref, *refs):
    groups = []
    for n in counts:
        groups.append(refs[:n])
        refs = refs[n:]
    partners, others, columns, sums, _, outs = groups + [refs]
    outs, sends = (outs[:-1], outs[-1:]) if columns else (outs, [])
    partner = jnp.concatenate([ref[...] for ref in partners], axis=1)
    for ref in others:
        partner = jnp.where(table_ref[inner_at] > 0, ref[...], partner)
    grad_in, grad_out = piece_math(scale, own_ref[...], partner, g_ref[...], x_ref[...], w_ref[...])
    for ref in sums:
        grad_in = grad_in + ref[0]
        grad_out = grad_out + ref[1]
    start = 0
    for ref in outs:
        end = start + ref.shape[1]
        ref[0], ref[1] = grad_in[start:end], grad_out[start:end]
        start = end
    rows = own_ref.shape[0]
    for ref in sends:
        for k, column_ref in enumerate(columns):
            ref[k * rows : (k + 1) * rows, :] = column_ref[...].astype(jnp.float32)


def columns_spec(rows, size, at):
    return pl.BlockSpec((rows, size), lambda i, table: (0, table[at]))


def piece_specs(rows, size, width, at):
    tokens = pl.BlockSpec((2 * rows, width), lambda i, table: (0, 0))
    return [
        columns_spec(rows, size, at),
        tokens,
        tokens,
        pl.BlockSpec((size, width), lambda i, table: (table[at], 0)),
    ]


def partner_spec(rows, size, place):
    return pl.BlockSpec((rows, size), lambda i, table: (place, 0))


def piece_cost(flops=1):
    return pl.CostEstimate(flops=flops, bytes_accessed=1, transcendentals=0)


def piece(
    scale, table, at, pre_act, partners, place, g, x, w_out, sums=(), other=None, inner_at=0, sends=(), split=(), after=(), flops=1
):
    rows, width = pre_act.shape[0], g.shape[1]
    size = sum(p.shape[1] for p in partners)
    shapes = [(2, n, width) for n in split or (size,)]
    whole = pl.BlockSpec((2, size, width), lambda i, table: (0, 0, 0))
    others, other_specs = [], []
    if other is not None:
        others = [other[0]]
        other_specs = [partner_spec(rows, size, other[1])]
    counts = (len(partners), len(others), len(sends), len(sums), len(after))
    sent = [(len(sends) * rows, size)] if sends else []
    return pl.pallas_call(
        functools.partial(piece_kernel, scale, counts, inner_at),
        grid_spec=pltpu.PrefetchScalarGridSpec(
            num_scalar_prefetch=1,
            grid=(1,),
            in_specs=piece_specs(rows, size, width, at)
            + [partner_spec(rows, p.shape[1], place) for p in partners]
            + other_specs
            + [columns_spec(rows, size, k) for k in sends]
            + [whole] * len(sums)
            + anywhere(after),
            out_specs=[pl.BlockSpec(shape, lambda i, table: (0, 0, 0)) for shape in shapes]
            + [pl.BlockSpec(shape, lambda i, table: (0, 0)) for shape in sent],
        ),
        out_shape=[jax.ShapeDtypeStruct(shape, jnp.float32) for shape in shapes + sent],
        compiler_params=params(),
        cost_estimate=piece_cost(flops),
        name="piece",
    )(table, pre_act, g, x, w_out, *partners, *others, *([pre_act] * len(sends)), *sums, *after)


def first_piece_kernel(
    scale, blk_at, table_ref, own_ref, w_ref, partner_ref, grads_ref, inputs_ref, q0_ref, q1_ref, q2_ref, q3_ref, a_ref, b_ref, *refs
):
    out_ref, g_ref, x_ref, send_ref = refs[-4:]
    rows = grads_ref.shape[0]
    quarters = (q0_ref, q1_ref, q2_ref, q3_ref)
    fill_tokens(table_ref[blk_at], grads_ref, inputs_ref, quarters, g_ref, x_ref)
    out_ref[0], out_ref[1] = piece_math(
        scale, own_ref[...], partner_ref[...], g_ref[...], x_ref[...], w_ref[...]
    )
    send_ref[:rows, :] = a_ref[...].astype(jnp.float32)
    send_ref[rows:, :] = b_ref[...].astype(jnp.float32)


def first_piece(scale, table, at, blk_at, pre_act, partner, out_grads, inputs, quarters, w_out, sends, after):
    rows, width = out_grads.shape
    size = partner.shape[1]
    whole = lambda *shape: pl.BlockSpec(shape, lambda i, table: (0,) * len(shape))
    tokens = jax.ShapeDtypeStruct((2 * rows, width), jnp.bfloat16)
    return pl.pallas_call(
        functools.partial(first_piece_kernel, scale, blk_at),
        grid_spec=pltpu.PrefetchScalarGridSpec(
            num_scalar_prefetch=1,
            grid=(1,),
            in_specs=[
                columns_spec(rows, size, at),
                pl.BlockSpec((size, width), lambda i, table: (table[at], 0)),
                whole(rows, size),
                whole(rows, width),
                whole(rows, width),
            ]
            + [whole(rows // 2, width)] * 4
            + [columns_spec(rows, size, k) for k in sends]
            + anywhere(after),
            out_specs=[
                whole(2, size, width),
                whole(2 * rows, width),
                whole(2 * rows, width),
                whole(2 * rows, size),
            ],
        ),
        out_shape=[
            jax.ShapeDtypeStruct((2, size, width), jnp.float32),
            tokens,
            tokens,
            jax.ShapeDtypeStruct((2 * rows, size), jnp.float32),
        ],
        compiler_params=params(),
        cost_estimate=piece_cost(),
        name="first_piece",
    )(table, pre_act, w_out, partner, out_grads, inputs, *quarters, pre_act, pre_act, *after)


def final_kernel(scale, inner_at, table_ref, own_ref, g_ref, x_ref, w_ref, partner_ref, inner_ref, outer_ref, *refs):
    sum_ref, (in_ref, out_ref) = refs[0], refs[-2:]
    grad_in, grad_out = piece_math(
        scale, own_ref[...], partner_ref[...], g_ref[...], x_ref[...], w_ref[...]
    )
    is_inner = table_ref[inner_at] > 0
    in_ref[...] = jnp.where(is_inner, inner_ref[0], grad_in + outer_ref[0]) + sum_ref[0]
    out_ref[...] = jnp.where(is_inner, inner_ref[1], grad_out + outer_ref[1]) + sum_ref[1]


def final_first(
    scale, count, table, at, inner_at, pre_act, partner, place, g, x, w_out, held, received, added, after
):
    rows, size, width = pre_act.shape[0], partner.shape[1], g.shape[1]
    whole = pl.BlockSpec((2, size, width), lambda i, table: (0, 0, 0))
    shape = jax.ShapeDtypeStruct((count * size, width), jnp.float32)
    return pl.pallas_call(
        functools.partial(final_kernel, scale, inner_at),
        grid_spec=pltpu.PrefetchScalarGridSpec(
            num_scalar_prefetch=1,
            grid=(1,),
            in_specs=piece_specs(rows, size, width, at)
            + [partner_spec(rows, size, place)]
            + [whole] * 3
            + anywhere(after),
            out_specs=[pl.BlockSpec((size, width), lambda i, table: (0, 0))] * 2,
        ),
        out_shape=(shape, shape),
        compiler_params=params(),
        cost_estimate=piece_cost(),
        name="final_first",
    )(table, pre_act, g, x, w_out, partner, held, received, added, *after)


def add_kernel(a_ref, b_ref, *refs):
    in_ref, out_ref = refs[-2:]
    in_ref[...] = a_ref[0] + b_ref[0]
    out_ref[...] = a_ref[1] + b_ref[1]


def final_add(first_row, offset, a, b, held, steps, after):
    _, size, width = b.shape
    step = size // steps
    return pl.pallas_call(
        add_kernel,
        grid=(steps,),
        in_specs=[
            pl.BlockSpec((2, step, width), lambda i: (0, offset // step + i, 0)),
            pl.BlockSpec((2, step, width), lambda i: (0, i, 0)),
        ]
        + anywhere(held)
        + anywhere(after),
        out_specs=[pl.BlockSpec((step, width), lambda i: (first_row // step + i, 0))] * 2,
        out_shape=[jax.ShapeDtypeStruct(h.shape, h.dtype) for h in held],
        input_output_aliases={2: 0, 3: 1},
        compiler_params=params(),
        cost_estimate=piece_cost(),
        name="final_add",
    )(a, b, *held, *after)


def line_body(inputs, out_grads, pre_act, w_in, w_out):
    count = PIECES
    rows, hidden = pre_act.shape
    size = hidden // (8 * count)
    scale = 1.0 / (rows * lax.axis_size("dp")) ** 0.5
    me, blk = lax.axis_index("dp"), lax.axis_index("blk")
    plane, half = me // 2, me % 2
    side = plane // 2
    inner = jnp.where((plane == 1) | (plane == 2), 1, 0).astype(jnp.int32)

    def by_role(on_inner, on_outer):
        return jnp.where(inner > 0, jnp.int32(on_inner), jnp.int32(on_outer))

    def links(pairs):
        return [(2 * a + h, 2 * b + h) for a, b in pairs for h in range(2)]

    def swap(array, planes):
        return lax.ppermute(array, "dp", [(2 * a + h, 2 * a + 1 - h) for a in planes for h in range(2)])

    def flip(array, bit):
        return lax.ppermute(array, "blk", [(i, i ^ bit) for i in range(4)])

    outer_to_inner = links([(0, 1), (3, 2)])
    inner_to_inner = links([(1, 2), (2, 1)])
    inner_to_outer = links([(1, 0), (2, 3)])
    every, inner_planes = (0, 1, 2, 3), (1, 2)

    def block(q, which):
        place = q // count
        chunk = jnp.where(side == 0, 3 - place, place)
        return (chunk * 2 + which) * count + q % count

    def mine(q):
        return block(q, half)

    def theirs(q):
        return block(q, 1 - half)

    near_inner = [2 * count + j for j in range(count)]
    near_outer = [3 * count + j for j in range(count)]
    steps = 3 * count - 1
    ahead = [s if s < 2 * count else s + 1 for s in range(steps)]
    main = [by_role(min(max(s - 2, 0), 2 * count - 1), ahead[s]) for s in range(steps)]
    own_chunk = [by_role(near_inner[j], near_outer[j]) for j in range(count)]
    double = steps - count
    first = jnp.int32(near_inner[0])

    inner_main, outer_main = [max(s - 2, 0) for s in range(steps)], ahead
    exchanges = [
        [(near_outer[0], outer_main[0])],
        [(near_outer[1], outer_main[1])],
        [(inner_main[2], outer_main[2]), (inner_main[3], outer_main[3])],
        [(inner_main[4], outer_main[4]), (inner_main[5], outer_main[5])],
        [
            (inner_main[6], outer_main[6]),
            (inner_main[7], outer_main[7]),
            (near_outer[2], near_outer[0]),
        ],
        [(near_inner[1], near_outer[1]), (near_inner[2], near_outer[2])],
    ]

    third, column = size // 3, theirs(first) * 3
    values, places = [inner], {}

    def put(name, value):
        places[name] = len(values)
        values.append(value)

    for s in range(steps):
        put(("main", s), mine(main[s]))
    for j in range(count):
        put(("out", j), mine(by_role(near_outer[j], ahead[double + j])))
        put(("own", j), mine(own_chunk[j]))
    for e, pairs in enumerate(exchanges):
        for k, pair in enumerate(pairs):
            put(("send", e, k), theirs(by_role(*pair)))
    put("blk", blk.astype(jnp.int32))
    put("first mine", mine(first))
    put("first theirs", theirs(first))
    put("first part", column + 1)
    put("second part", column + 2)
    table = jnp.stack(values)

    def columns_of(e):
        return [places["send", e, k] for k in range(len(exchanges[e]))]

    quarter, raw_0 = first_sends(blk, column, out_grads, inputs, pre_act, third)
    raw_1, send_0, raw_2, send_1 = cast_blocks(
        table,
        [
            (third, [places["first part"], places["second part"]]),
            (size, columns_of(0)),
            (size, [places["first mine"]]),
            (size, columns_of(1)),
        ],
        pre_act,
        [raw_0],
    )

    def send_in(array):
        return lax.ppermute(array, "dp", outer_to_inner)

    tied = lax.optimization_barrier
    pair_0 = swap(quarter, every)
    raw_0, raw_1, raw_2 = send_in(raw_0), send_in(raw_1), send_in(raw_2)
    quarter_in = send_in(quarter)
    got = [swap(send_0, every), swap(send_1, every)]
    pair_0, raw_0 = tied((pair_0, raw_0))
    pair_1, pair_2 = flip(pair_0, 1), flip(pair_0, 2)
    pair_2, pair_1, got[0], raw_1 = tied((pair_2, pair_1, got[0], raw_1))
    pair_3 = flip(pair_2, 1)
    def run(name, partner, **more):
        return piece(scale, table, places[name], pre_act, [partner[0]], partner[1], g, x, w_out, **more)

    toward, across = [], {}
    for s in range(steps):
        partner = (got[s], 0) if s < 2 else (got[1 + s // 2], s % 2)
        sends = columns_of(2 + s // 2) if s % 2 == 0 else []
        sums = [toward[s - 2]] if s >= 2 else []
        held_back = ([across[s - 4]] if s >= 4 else []) + ([first_in] if s == 3 else [])
        j = s - double
        if s == 0:
            out, g, x, *blocks = first_piece(
                scale,
                table,
                places["main", 0],
                places["blk"],
                pre_act,
                got[0],
                out_grads,
                inputs,
                [pair_0, pair_1, pair_2, pair_3],
                w_out,
                sends,
                [raw_2],
            )
        else:
            after = [last] + held_back + ([quarter_in] if s == 1 else [])
            if j >= 0:
                split = (2 * third, third) if j == count - 1 else (size,)
                last, *rest = run(
                    ("out", j),
                    partner,
                    sums=[across[j]],
                    other=(got[j], 0) if j < 2 else (got[4], 2),
                    split=split,
                    after=after + sums,
                )
                parts = [lax.ppermute(array, "dp", outer_to_inner + inner_to_outer) for array in (last, *rest)]
                toward.append(parts[0] if j < count - 1 else parts)
                after = [last]
            out, *blocks = run(
                ("main", s), partner, sums=sums, sends=sends, after=after, flops=FLOPS
            )
        last = out
        if j < 0:
            toward.append(send_in(out))
        if blocks:
            got.append(swap(blocks[0], every))
        if s >= 2:
            across[s - 2] = lax.ppermute(out, "dp", inner_to_inner)
        if s == 1:
            line_quarter = tied((quarter_in, out))[0]
            in_1, in_2 = flip(line_quarter, 1), flip(line_quarter, 2)
            in_3 = flip(in_2, 1)
            line_g, line_x = join(blk, out_grads, inputs, [line_quarter, in_1, in_2, in_3], [last, got[2]])
            (last,) = piece(
                scale,
                table,
                places["first theirs"],
                pre_act,
                [raw_0, raw_1],
                0,
                line_g,
                line_x,
                w_out,
                after=[last],
            )
            first_in = swap(last, inner_planes)
        if s == 3:
            rows_kept, rows_given = input_partial(blk, out_grads, pre_act, w_in, w_out, 4 * size, [last])
            last = rows_given
        if s == 4:
            (held_in,) = piece(
                scale,
                table,
                places["first mine"],
                pre_act,
                [raw_2],
                0,
                line_g,
                line_x,
                w_out,
                sums=[first_in],
                after=[last],
            )
            last = held_in

    rows_got = flip(tied((rows_given, last))[0], 2)
    held = final_first(
        scale,
        count,
        table,
        places["own", 0],
        0,
        pre_act,
        got[4],
        2,
        g,
        x,
        w_out,
        held_in,
        toward[double],
        across[count],
        [last],
    )
    last = held[0]
    for i in range(1, count):
        (out,) = run(("own", i), (got[5], i - 1), sums=[across[count + i]], after=[last])
        if i == 1:
            rows_kept, rows_given = fold(blk, rows_kept, rows_got, [out])
            rows_got = flip(rows_given, 1)
            held = final_add(i * size, 0, out, toward[double + i], held, 2, [rows_given])
            grad_inputs = round_sum(rows_kept, rows_got, [held[0]])
            last = grad_inputs
        else:
            held = final_add(i * size, 0, out, parts[0], held, 1, [])
            held = final_add(i * size + 2 * third, 2 * third, out, parts[1], held, 1, [])
    return (grad_inputs, held[0], held[1])


def solution(mesh):
    def body(inputs, out_grads, pre_act, w_in, w_out):
        fits = pre_act.shape[1] % (8 * PIECES * 128) == 0 and inputs.shape[0] % 64 == 0
        run = line_body if (mesh.shape["dp"], mesh.shape["blk"]) == (8, 4) and fits else plain_body
        return run(inputs, out_grads, pre_act, w_in, w_out)

    return jax.shard_map(
        body,
        mesh=mesh,
        in_specs=(P("dp", None), P("dp", None), P("dp", "blk"), P("blk", None), P("blk", None)),
        out_specs=(P(("dp", "blk"), None), P(("blk", "dp"), None), P(("blk", "dp"), None)),
        check_vma=False,
    )
```

```python
import functools

import jax
import jax.numpy as jnp
from jax import lax
from jax.experimental import pallas as pl
from jax.experimental.pallas import tpu as pltpu
from jax.sharding import PartitionSpec as P

PIECES = 3
FLOPS = 100_000_000_000
VMEM_LIMIT = 64 * 1024 * 1024


def contract_rows(left, right):
    return lax.dot_general(
        left, right, (((0,), (0,)), ((), ())), preferred_element_type=jnp.float32
    )


def hidden_grads(out_grads, pre_act, w_out):
    back = lax.dot_general(
        out_grads, w_out, (((1,), (1,)), ((), ())), preferred_element_type=jnp.float32
    )
    return jnp.where(pre_act > 0, back, jnp.zeros_like(back)).astype(jnp.bfloat16)


def input_grads(grad_hidden, w_in):
    return lax.psum_scatter(
        jnp.dot(grad_hidden, w_in, preferred_element_type=jnp.float32),
        "blk",
        scatter_dimension=0,
        tiled=True,
    ).astype(jnp.bfloat16)


def plain_body(inputs, out_grads, pre_act, w_in, w_out):
    token_total = inputs.shape[0] * lax.axis_size("dp")
    factor = lax.rsqrt(jnp.asarray(token_total, jnp.float32))
    act = jnp.maximum(pre_act, jnp.zeros_like(pre_act))
    grad_hidden = hidden_grads(out_grads, pre_act, w_out)
    grad_out = contract_rows(act, out_grads) * factor
    grad_in = contract_rows(grad_hidden, inputs) * factor
    return (
        input_grads(grad_hidden, w_in),
        lax.psum_scatter(grad_in, "dp", scatter_dimension=0, tiled=True),
        lax.psum_scatter(grad_out, "dp", scatter_dimension=0, tiled=True),
    )


def params():
    return pltpu.CompilerParams(vmem_limit_bytes=VMEM_LIMIT)


def anywhere(arrays):
    return [pl.BlockSpec(memory_space=pl.ANY)] * len(arrays)


def cast_kernel(shapes, idx_ref, *refs):
    outs = refs[-len(shapes) :]
    for (_, count), out_ref in zip(shapes, outs):
        width = out_ref.shape[1] // count
        for k in range(count):
            out_ref[:, k * width : (k + 1) * width] = refs[k][...].astype(jnp.float32)
        refs = refs[count:]


def cast_blocks(table, groups, pre_act, after):
    rows = pre_act.shape[0]
    in_specs = [columns_spec(rows, width, at) for width, places in groups for at in places]
    shapes = [(width * len(places), len(places)) for width, places in groups]
    return pl.pallas_call(
        functools.partial(cast_kernel, shapes),
        grid_spec=pltpu.PrefetchScalarGridSpec(
            num_scalar_prefetch=1,
            grid=(1,),
            in_specs=in_specs + anywhere(after),
            out_specs=[pl.BlockSpec((rows, width), lambda i, idx: (0, 0)) for width, _ in shapes],
        ),
        out_shape=[jax.ShapeDtypeStruct((rows, width), jnp.float32) for width, _ in shapes],
        compiler_params=params(),
        cost_estimate=piece_cost(),
        name="cast_blocks",
    )(table, *([pre_act] * len(in_specs)), *after)


def first_kernel(blk_ref, column_ref, grads_ref, inputs_ref, pre_ref, quarter_ref, raw_ref):
    quarter = grads_ref.shape[0]
    quarter_ref[:quarter, :] = grads_ref[...].astype(jnp.float32)
    quarter_ref[quarter:, :] = inputs_ref[...].astype(jnp.float32)
    raw_ref[...] = pre_ref[...].astype(jnp.float32)


def first_sends(blk, column, out_grads, inputs, pre_act, size):
    rows, width = out_grads.shape
    quarter = rows // 4
    tokens = pl.BlockSpec((quarter, width), lambda i, blk, column: (blk[0], 0))
    return pl.pallas_call(
        first_kernel,
        grid_spec=pltpu.PrefetchScalarGridSpec(
            num_scalar_prefetch=2,
            grid=(1,),
            in_specs=[tokens, tokens, pl.BlockSpec((rows, size), lambda i, blk, column: (0, column[0]))],
            out_specs=[
                pl.BlockSpec((2 * quarter, width), lambda i, blk, column: (0, 0)),
                pl.BlockSpec((rows, size), lambda i, blk, column: (0, 0)),
            ],
        ),
        out_shape=[
            jax.ShapeDtypeStruct((2 * quarter, width), jnp.float32),
            jax.ShapeDtypeStruct((rows, size), jnp.float32),
        ],
        compiler_params=params(),
        cost_estimate=piece_cost(),
        name="first_sends",
    )(blk.reshape(1), column.reshape(1), out_grads, inputs, pre_act)


def fill_tokens(blk, grads_ref, inputs_ref, quarters, g_ref, x_ref):
    rows = grads_ref.shape[0]
    quarter = rows // 4
    g_ref[:rows, :] = grads_ref[...]
    x_ref[:rows, :] = inputs_ref[...]
    for k, ref in enumerate(quarters):
        where = jnp.bitwise_xor(blk, k)
        place = pl.ds(pl.multiple_of(rows + where * quarter, quarter), quarter)
        g_ref[place, :] = ref[:quarter, :].astype(jnp.bfloat16)
        x_ref[place, :] = ref[quarter:, :].astype(jnp.bfloat16)


def join_kernel(blk_ref, grads_ref, inputs_ref, *refs):
    fill_tokens(blk_ref[0], grads_ref, inputs_ref, refs[:4], *refs[-2:])


def join(blk, out_grads, inputs, quarters, after):
    rows, width = out_grads.shape
    shape = jax.ShapeDtypeStruct((2 * rows, width), jnp.bfloat16)
    vmem = pl.BlockSpec(memory_space=pltpu.VMEM)
    return pl.pallas_call(
        join_kernel,
        out_shape=(shape, shape),
        in_specs=[pl.BlockSpec(memory_space=pltpu.SMEM)] + [vmem] * 6 + anywhere(after),
        out_specs=(vmem, vmem),
        compiler_params=params(),
        cost_estimate=piece_cost(),
        name="join_tokens",
    )(blk.reshape(1), out_grads, inputs, *quarters, *after)


def input_kernel(blk_ref, grads_ref, pre_ref, out_rows_ref, in_rows_ref, *refs):
    keep_ref, give_ref, total_ref = refs[-3:]

    @pl.when(pl.program_id(0) == 0)
    def _():
        total_ref[...] = jnp.zeros_like(total_ref)

    hidden = hidden_grads(grads_ref[...], pre_ref[...], out_rows_ref[...])
    total_ref[...] += jnp.dot(hidden, in_rows_ref[...], preferred_element_type=jnp.float32)

    @pl.when(pl.program_id(0) == pl.num_programs(0) - 1)
    def _():
        half = keep_ref.shape[0]
        x = blk_ref[0] // 2
        keep_ref[...] = total_ref[pl.ds(pl.multiple_of(x * half, half), half), :]
        give_ref[...] = total_ref[pl.ds(pl.multiple_of((1 - x) * half, half), half), :]


def input_partial(blk, out_grads, pre_act, w_in, w_out, size, after):
    rows, hidden = pre_act.shape
    width = out_grads.shape[1]
    tokens = pl.BlockSpec((rows, width), lambda i, blk: (0, 0))
    weights = pl.BlockSpec((size, width), lambda i, blk: (i, 0))
    half = jax.ShapeDtypeStruct((rows // 2, width), jnp.float32)
    return pl.pallas_call(
        input_kernel,
        grid_spec=pltpu.PrefetchScalarGridSpec(
            num_scalar_prefetch=1,
            grid=(hidden // size,),
            in_specs=[tokens, pl.BlockSpec((rows, size), lambda i, blk: (0, i)), weights, weights]
            + anywhere(after),
            out_specs=[pl.BlockSpec(half.shape, lambda i, blk: (0, 0))] * 2,
            scratch_shapes=[pltpu.VMEM((rows, width), jnp.float32)],
        ),
        out_shape=[half, half],
        compiler_params=params(),
        cost_estimate=piece_cost(),
        name="input_partial",
    )(blk.reshape(1), out_grads, pre_act, w_out, w_in, *after)


def fold_kernel(blk_ref, kept_ref, got_ref, *refs):
    keep_ref, give_ref = refs[-2:]
    rows = keep_ref.shape[0]
    core = blk_ref[0] % 2
    for ref, place in ((keep_ref, core), (give_ref, 1 - core)):
        part = pl.ds(pl.multiple_of(place * rows, rows), rows)
        ref[...] = kept_ref[part, :] + got_ref[part, :]


def fold(blk, kept, got, after):
    rows, width = kept.shape
    half = jax.ShapeDtypeStruct((rows // 2, width), jnp.float32)
    vmem = pl.BlockSpec(memory_space=pltpu.VMEM)
    return pl.pallas_call(
        fold_kernel,
        out_shape=(half, half),
        in_specs=[pl.BlockSpec(memory_space=pltpu.SMEM), vmem, vmem] + anywhere(after),
        out_specs=(vmem, vmem),
        compiler_params=params(),
        cost_estimate=piece_cost(),
        name="fold_rows",
    )(blk.reshape(1), kept, got, *after)


def round_kernel(kept_ref, got_ref, *refs):
    refs[-1][...] = (kept_ref[...] + got_ref[...]).astype(jnp.bfloat16)


def round_sum(kept, got, after):
    vmem = pl.BlockSpec(memory_space=pltpu.VMEM)
    return pl.pallas_call(
        round_kernel,
        out_shape=jax.ShapeDtypeStruct(kept.shape, jnp.bfloat16),
        in_specs=[vmem, vmem] + anywhere(after),
        out_specs=vmem,
        compiler_params=params(),
        cost_estimate=piece_cost(),
        name="round_sum",
    )(kept, got, *after)


def piece_math(scale, own, partner, g, x, w):
    pre = jnp.concatenate([own, partner.astype(jnp.bfloat16)], axis=0)
    hidden = hidden_grads(g, pre, w)
    act = jnp.maximum(pre, jnp.zeros_like(pre))
    return contract_rows(hidden, x) * scale, contract_rows(act, g) * scale


def piece_kernel(scale, counts, inner_at, table_ref, own_ref, g_ref, x_ref, w_ref, *refs):
    groups = []
    for n in counts:
        groups.append(refs[:n])
        refs = refs[n:]
    partners, others, columns, sums, _, outs = groups + [refs]
    outs, sends = (outs[:-1], outs[-1:]) if columns else (outs, [])
    partner = jnp.concatenate([ref[...] for ref in partners], axis=1)
    for ref in others:
        partner = jnp.where(table_ref[inner_at] > 0, ref[...], partner)
    grad_in, grad_out = piece_math(scale, own_ref[...], partner, g_ref[...], x_ref[...], w_ref[...])
    for ref in sums:
        grad_in = grad_in + ref[0]
        grad_out = grad_out + ref[1]
    start = 0
    for ref in outs:
        end = start + ref.shape[1]
        ref[0], ref[1] = grad_in[start:end], grad_out[start:end]
        start = end
    rows = own_ref.shape[0]
    for ref in sends:
        for k, column_ref in enumerate(columns):
            ref[k * rows : (k + 1) * rows, :] = column_ref[...].astype(jnp.float32)


def columns_spec(rows, size, at):
    return pl.BlockSpec((rows, size), lambda i, table: (0, table[at]))


def piece_specs(rows, size, width, at):
    tokens = pl.BlockSpec((2 * rows, width), lambda i, table: (0, 0))
    return [
        columns_spec(rows, size, at),
        tokens,
        tokens,
        pl.BlockSpec((size, width), lambda i, table: (table[at], 0)),
    ]


def partner_spec(rows, size, place):
    return pl.BlockSpec((rows, size), lambda i, table: (place, 0))


def piece_cost(flops=1):
    return pl.CostEstimate(flops=flops, bytes_accessed=1, transcendentals=0)


def piece(
    scale, table, at, pre_act, partners, place, g, x, w_out, sums=(), other=None, inner_at=0, sends=(), split=(), after=(), flops=1
):
    rows, width = pre_act.shape[0], g.shape[1]
    size = sum(p.shape[1] for p in partners)
    shapes = [(2, n, width) for n in split or (size,)]
    whole = pl.BlockSpec((2, size, width), lambda i, table: (0, 0, 0))
    others, other_specs = [], []
    if other is not None:
        others = [other[0]]
        other_specs = [partner_spec(rows, size, other[1])]
    counts = (len(partners), len(others), len(sends), len(sums), len(after))
    sent = [(len(sends) * rows, size)] if sends else []
    return pl.pallas_call(
        functools.partial(piece_kernel, scale, counts, inner_at),
        grid_spec=pltpu.PrefetchScalarGridSpec(
            num_scalar_prefetch=1,
            grid=(1,),
            in_specs=piece_specs(rows, size, width, at)
            + [partner_spec(rows, p.shape[1], place) for p in partners]
            + other_specs
            + [columns_spec(rows, size, k) for k in sends]
            + [whole] * len(sums)
            + anywhere(after),
            out_specs=[pl.BlockSpec(shape, lambda i, table: (0, 0, 0)) for shape in shapes]
            + [pl.BlockSpec(shape, lambda i, table: (0, 0)) for shape in sent],
        ),
        out_shape=[jax.ShapeDtypeStruct(shape, jnp.float32) for shape in shapes + sent],
        compiler_params=params(),
        cost_estimate=piece_cost(flops),
        name="piece",
    )(table, pre_act, g, x, w_out, *partners, *others, *([pre_act] * len(sends)), *sums, *after)


def first_piece_kernel(
    scale, blk_at, table_ref, own_ref, w_ref, partner_ref, grads_ref, inputs_ref, q0_ref, q1_ref, q2_ref, q3_ref, a_ref, b_ref, *refs
):
    out_ref, g_ref, x_ref, send_ref = refs[-4:]
    rows = grads_ref.shape[0]
    quarters = (q0_ref, q1_ref, q2_ref, q3_ref)
    fill_tokens(table_ref[blk_at], grads_ref, inputs_ref, quarters, g_ref, x_ref)
    out_ref[0], out_ref[1] = piece_math(
        scale, own_ref[...], partner_ref[...], g_ref[...], x_ref[...], w_ref[...]
    )
    send_ref[:rows, :] = a_ref[...].astype(jnp.float32)
    send_ref[rows:, :] = b_ref[...].astype(jnp.float32)


def first_piece(scale, table, at, blk_at, pre_act, partner, out_grads, inputs, quarters, w_out, sends, after):
    rows, width = out_grads.shape
    size = partner.shape[1]
    whole = lambda *shape: pl.BlockSpec(shape, lambda i, table: (0,) * len(shape))
    tokens = jax.ShapeDtypeStruct((2 * rows, width), jnp.bfloat16)
    return pl.pallas_call(
        functools.partial(first_piece_kernel, scale, blk_at),
        grid_spec=pltpu.PrefetchScalarGridSpec(
            num_scalar_prefetch=1,
            grid=(1,),
            in_specs=[
                columns_spec(rows, size, at),
                pl.BlockSpec((size, width), lambda i, table: (table[at], 0)),
                whole(rows, size),
                whole(rows, width),
                whole(rows, width),
            ]
            + [whole(rows // 2, width)] * 4
            + [columns_spec(rows, size, k) for k in sends]
            + anywhere(after),
            out_specs=[
                whole(2, size, width),
                whole(2 * rows, width),
                whole(2 * rows, width),
                whole(2 * rows, size),
            ],
        ),
        out_shape=[
            jax.ShapeDtypeStruct((2, size, width), jnp.float32),
            tokens,
            tokens,
            jax.ShapeDtypeStruct((2 * rows, size), jnp.float32),
        ],
        compiler_params=params(),
        cost_estimate=piece_cost(),
        name="first_piece",
    )(table, pre_act, w_out, partner, out_grads, inputs, *quarters, pre_act, pre_act, *after)


def final_kernel(scale, inner_at, table_ref, own_ref, g_ref, x_ref, w_ref, partner_ref, inner_ref, outer_ref, *refs):
    sum_ref, (in_ref, out_ref) = refs[0], refs[-2:]
    grad_in, grad_out = piece_math(
        scale, own_ref[...], partner_ref[...], g_ref[...], x_ref[...], w_ref[...]
    )
    is_inner = table_ref[inner_at] > 0
    in_ref[...] = jnp.where(is_inner, inner_ref[0], grad_in + outer_ref[0]) + sum_ref[0]
    out_ref[...] = jnp.where(is_inner, inner_ref[1], grad_out + outer_ref[1]) + sum_ref[1]


def final_first(
    scale, count, table, at, inner_at, pre_act, partner, place, g, x, w_out, held, received, added, after
):
    rows, size, width = pre_act.shape[0], partner.shape[1], g.shape[1]
    whole = pl.BlockSpec((2, size, width), lambda i, table: (0, 0, 0))
    shape = jax.ShapeDtypeStruct((count * size, width), jnp.float32)
    return pl.pallas_call(
        functools.partial(final_kernel, scale, inner_at),
        grid_spec=pltpu.PrefetchScalarGridSpec(
            num_scalar_prefetch=1,
            grid=(1,),
            in_specs=piece_specs(rows, size, width, at)
            + [partner_spec(rows, size, place)]
            + [whole] * 3
            + anywhere(after),
            out_specs=[pl.BlockSpec((size, width), lambda i, table: (0, 0))] * 2,
        ),
        out_shape=(shape, shape),
        compiler_params=params(),
        cost_estimate=piece_cost(),
        name="final_first",
    )(table, pre_act, g, x, w_out, partner, held, received, added, *after)


def add_kernel(a_ref, b_ref, *refs):
    in_ref, out_ref = refs[-2:]
    in_ref[...] = a_ref[0] + b_ref[0]
    out_ref[...] = a_ref[1] + b_ref[1]


def final_add(first_row, offset, a, b, held, steps, after):
    _, size, width = b.shape
    step = size // steps
    return pl.pallas_call(
        add_kernel,
        grid=(steps,),
        in_specs=[
            pl.BlockSpec((2, step, width), lambda i: (0, offset // step + i, 0)),
            pl.BlockSpec((2, step, width), lambda i: (0, i, 0)),
        ]
        + anywhere(held)
        + anywhere(after),
        out_specs=[pl.BlockSpec((step, width), lambda i: (first_row // step + i, 0))] * 2,
        out_shape=[jax.ShapeDtypeStruct(h.shape, h.dtype) for h in held],
        input_output_aliases={2: 0, 3: 1},
        compiler_params=params(),
        cost_estimate=piece_cost(),
        name="final_add",
    )(a, b, *held, *after)


def line_body(inputs, out_grads, pre_act, w_in, w_out):
    count = PIECES
    rows, hidden = pre_act.shape
    size = hidden // (8 * count)
    scale = 1.0 / (rows * lax.axis_size("dp")) ** 0.5
    me, blk = lax.axis_index("dp"), lax.axis_index("blk")
    plane, half = me // 2, me % 2
    side = plane // 2
    inner = jnp.where((plane == 1) | (plane == 2), 1, 0).astype(jnp.int32)

    def by_role(on_inner, on_outer):
        return jnp.where(inner > 0, jnp.int32(on_inner), jnp.int32(on_outer))

    def links(pairs):
        return [(2 * a + h, 2 * b + h) for a, b in pairs for h in range(2)]

    def swap(array, planes):
        return lax.ppermute(array, "dp", [(2 * a + h, 2 * a + 1 - h) for a in planes for h in range(2)])

    def flip(array, bit):
        return lax.ppermute(array, "blk", [(i, i ^ bit) for i in range(4)])

    outer_to_inner = links([(0, 1), (3, 2)])
    inner_to_inner = links([(1, 2), (2, 1)])
    inner_to_outer = links([(1, 0), (2, 3)])
    every, inner_planes = (0, 1, 2, 3), (1, 2)

    def block(q, which):
        place = q // count
        chunk = jnp.where(side == 0, 3 - place, place)
        return (chunk * 2 + which) * count + q % count

    def mine(q):
        return block(q, half)

    def theirs(q):
        return block(q, 1 - half)

    near_inner = [2 * count + j for j in range(count)]
    near_outer = [3 * count + j for j in range(count)]
    steps = 3 * count - 1
    ahead = [s if s < 2 * count else s + 1 for s in range(steps)]
    main = [by_role(min(max(s - 2, 0), 2 * count - 1), ahead[s]) for s in range(steps)]
    own_chunk = [by_role(near_inner[j], near_outer[j]) for j in range(count)]
    double = steps - count
    first = jnp.int32(near_inner[0])

    inner_main, outer_main = [max(s - 2, 0) for s in range(steps)], ahead
    exchanges = [
        [(near_outer[0], outer_main[0])],
        [(near_outer[1], outer_main[1])],
        [(inner_main[2], outer_main[2]), (inner_main[3], outer_main[3])],
        [(inner_main[4], outer_main[4]), (inner_main[5], outer_main[5])],
        [
            (inner_main[6], outer_main[6]),
            (inner_main[7], outer_main[7]),
            (near_outer[2], near_outer[0]),
        ],
        [(near_inner[1], near_outer[1]), (near_inner[2], near_outer[2])],
    ]

    third, column = size // 3, theirs(first) * 3
    values, places = [inner], {}

    def put(name, value):
        places[name] = len(values)
        values.append(value)

    for s in range(steps):
        put(("main", s), mine(main[s]))
    for j in range(count):
        put(("out", j), mine(by_role(near_outer[j], ahead[double + j])))
        put(("own", j), mine(own_chunk[j]))
    for e, pairs in enumerate(exchanges):
        for k, pair in enumerate(pairs):
            put(("send", e, k), theirs(by_role(*pair)))
    put("blk", blk.astype(jnp.int32))
    put("first mine", mine(first))
    put("first theirs", theirs(first))
    put("first part", column + 1)
    put("second part", column + 2)
    table = jnp.stack(values)

    def columns_of(e):
        return [places["send", e, k] for k in range(len(exchanges[e]))]

    quarter, raw_0 = first_sends(blk, column, out_grads, inputs, pre_act, third)
    raw_1, send_0, raw_2, send_1 = cast_blocks(
        table,
        [
            (third, [places["first part"], places["second part"]]),
            (size, columns_of(0)),
            (size, [places["first mine"]]),
            (size, columns_of(1)),
        ],
        pre_act,
        [raw_0],
    )

    def send_in(array):
        return lax.ppermute(array, "dp", outer_to_inner)

    tied = lax.optimization_barrier
    pair_0 = swap(quarter, every)
    raw_0, raw_1, raw_2 = send_in(raw_0), send_in(raw_1), send_in(raw_2)
    quarter_in = send_in(quarter)
    got = [swap(send_0, every), swap(send_1, every)]
    pair_0, raw_0 = tied((pair_0, raw_0))
    pair_1, pair_2 = flip(pair_0, 1), flip(pair_0, 2)
    pair_2, pair_1, got[0], raw_1 = tied((pair_2, pair_1, got[0], raw_1))
    pair_3 = flip(pair_2, 1)
    def run(name, partner, **more):
        return piece(scale, table, places[name], pre_act, [partner[0]], partner[1], g, x, w_out, **more)

    toward, across = [], {}
    for s in range(steps):
        partner = (got[s], 0) if s < 2 else (got[1 + s // 2], s % 2)
        sends = columns_of(2 + s // 2) if s % 2 == 0 else []
        sums = [toward[s - 2]] if s >= 2 else []
        held_back = ([across[s - 4]] if s >= 4 else []) + ([first_in] if s == 3 else [])
        j = s - double
        if s == 0:
            out, g, x, *blocks = first_piece(
                scale,
                table,
                places["main", 0],
                places["blk"],
                pre_act,
                got[0],
                out_grads,
                inputs,
                [pair_0, pair_1, pair_2, pair_3],
                w_out,
                sends,
                [raw_2],
            )
        else:
            after = [last] + held_back + ([quarter_in] if s == 1 else [])
            if j >= 0:
                split = (2 * third, third) if j == count - 1 else (size,)
                last, *rest = run(
                    ("out", j),
                    partner,
                    sums=[across[j]],
                    other=(got[j], 0) if j < 2 else (got[4], 2),
                    split=split,
                    after=after + sums,
                )
                parts = [lax.ppermute(array, "dp", outer_to_inner + inner_to_outer) for array in (last, *rest)]
                toward.append(parts[0] if j < count - 1 else parts)
                after = [last]
            out, *blocks = run(
                ("main", s), partner, sums=sums, sends=sends, after=after, flops=FLOPS
            )
        last = out
        if j < 0:
            toward.append(send_in(out))
        if blocks:
            got.append(swap(blocks[0], every))
        if s >= 2:
            across[s - 2] = lax.ppermute(out, "dp", inner_to_inner)
        if s == 1:
            line_quarter = tied((quarter_in, out))[0]
            in_1, in_2 = flip(line_quarter, 1), flip(line_quarter, 2)
            in_3 = flip(in_2, 1)
            line_g, line_x = join(blk, out_grads, inputs, [line_quarter, in_1, in_2, in_3], [last, got[2]])
            (last,) = piece(
                scale,
                table,
                places["first theirs"],
                pre_act,
                [raw_0, raw_1],
                0,
                line_g,
                line_x,
                w_out,
                after=[last],
            )
            first_in = swap(last, inner_planes)
        if s == 3:
            rows_kept, rows_given = input_partial(blk, out_grads, pre_act, w_in, w_out, 4 * size, [last])
            last = rows_given
        if s == 4:
            (held_in,) = piece(
                scale,
                table,
                places["first mine"],
                pre_act,
                [raw_2],
                0,
                line_g,
                line_x,
                w_out,
                sums=[first_in],
                after=[last],
            )
            last = held_in

    rows_got = flip(tied((rows_given, last))[0], 2)
    held = final_first(
        scale,
        count,
        table,
        places["own", 0],
        0,
        pre_act,
        got[4],
        2,
        g,
        x,
        w_out,
        held_in,
        toward[double],
        across[count],
        [last],
    )
    last = held[0]
    for i in range(1, count):
        (out,) = run(("own", i), (got[5], i - 1), sums=[across[count + i]], after=[last])
        if i == 1:
            rows_kept, rows_given = fold(blk, rows_kept, rows_got, [out])
            rows_got = flip(rows_given, 1)
            held = final_add(i * size, 0, out, toward[double + i], held, 2, [rows_given])
            grad_inputs = round_sum(rows_kept, rows_got, [held[0]])
            last = grad_inputs
        else:
            held = final_add(i * size, 0, out, parts[0], held, 1, [])
            held = final_add(i * size + 2 * third, 2 * third, out, parts[1], held, 1, [])
    return (grad_inputs, held[0], held[1])


def solution(mesh):
    def body(inputs, out_grads, pre_act, w_in, w_out):
        fits = pre_act.shape[1] % (8 * PIECES * 128) == 0 and inputs.shape[0] % 64 == 0
        run = line_body if (mesh.shape["dp"], mesh.shape["blk"]) == (8, 4) and fits else plain_body
        return run(inputs, out_grads, pre_act, w_in, w_out)

    return jax.shard_map(
        body,
        mesh=mesh,
        in_specs=(P("dp", None), P("dp", None), P("dp", "blk"), P("blk", None), P("blk", None)),
        out_specs=(P(("dp", "blk"), None), P(("blk", "dp"), None), P(("blk", "dp"), None)),
        check_vma=False,
    )
```
